32 devices in a mesh: expert: 16 (over z, y, x), rep: 2 (over core).
Axes of the slice: x: 2, y: 2, z: 4, core: 2. Of those that a mesh axis runs over, the one named last changes fastest.
Arguments:
- inputs: bfloat16 [4096, 2048], P(('expert', 'rep')), may hold values from -6 to 6
- out_grad: bfloat16 [4096, 2048], P(('expert', 'rep')), may hold values from -3 to 3
- expert_ids: int32 [4096, 2], P(('expert', 'rep')), may hold values from 0 to 15, all different within a row; in each aligned block of 128 rows (0 to 127, 128 to 255, ...) at most 32 rows name the same one
- gates: float32 [4096, 2], P(('expert', 'rep')), may hold values from 0.1 to 1
- gate_w: bfloat16 [16, 2048, 768], P('expert', 'rep'), may hold values from -0.125 to 0.125
- up_w: bfloat16 [16, 2048, 768], P('expert', 'rep'), may hold values from -0.125 to 0.125
- down_w: bfloat16 [16, 768, 2048], P('expert', None, 'rep'), may hold values from -0.21875 to 0.21875
Outputs:
- input_grad: bfloat16 [4096, 2048], P(('expert', 'rep'))
- gate_w_grad: bfloat16 [16, 2048, 768], P('expert', 'rep')
- up_w_grad: bfloat16 [16, 2048, 768], P('expert', 'rep')
- down_w_grad: bfloat16 [16, 768, 2048], P('expert', None, 'rep')
The draws below stay inside these ranges and needn't reach their ends.
Inputs may be any that keep to these rules, and one draw needn't show every extreme that they name: `expert_ids`: each row names 2 different experts; within the 128 rows of one device no expert is named more than 32 times.
All inputs are finite; a program needn't handle non-finite values.
Results may differ from the reference program's by a relative error of at most 0.0065.
Values may be sent and summed in bfloat16 or wider, within the bound.
A program may use at most 128 MiB of HBM per device.

```python
import math
import jax
import jax.numpy as jnp
import numpy as np
from jax import lax

D = 2048
H = 768
TOPK = 2
TOK_DEV = 128
EXPERTS = 16
GROUPS = 16
REPLICAS = 2
CAP = 32
TOKENS = 4096


def level_of(own_key, dims, pieces, least, high):
    def one(dim, blocks):
        heights = jax.random.uniform(jax.random.fold_in(jax.random.fold_in(own_key, 6), dim), (blocks,), jnp.float32, least / len(pieces), high / len(pieces))
        return jnp.repeat(jnp.exp(heights), dims[dim] // blocks).reshape((-1,) + (1,) * (len(dims) - dim - 1))

    loudness = one(*pieces[0])
    for cut in pieces[1:]:
        loudness = loudness * one(*cut)
    return loudness


def routed_block(key, own, number, rows, number_of, top, bound, slope):
    order = jax.random.permutation(key, number_of)
    packed, usual = shares(number_of, rows * top, bound, slope, True), shares(number_of, rows * top, bound, slope, False)
    places = jnp.arange(number_of)

    def named(sizes, turn):
        used = int((sizes > 0).sum())
        fixed = max(1, used // 4)
        passed = fixed + (places - fixed + turn * (used - fixed)) % max(1, number_of - fixed)
        return jnp.zeros((number_of,), jnp.int32).at[order[jnp.where(places < fixed, places, passed)]].set(jnp.asarray(sizes, jnp.int32))

    sizes = jnp.where(number % 4 == 0, named(packed, number // 4), named(usual, number - number // 4 - 1))
    mixed = jax.random.permutation(jax.random.fold_in(own, 3), number_of)
    giver, receiver = mixed[0:number_of // 2 * 2:2], mixed[1:number_of // 2 * 2:2]
    margin = jnp.minimum(sizes[giver] - 1, bound - sizes[receiver]) // 2
    margin = jnp.where((giver == order[0]) | (receiver == order[0]) | (sizes[receiver] == 0), 0, jnp.maximum(margin, 0))
    passed = jax.random.randint(jax.random.fold_in(own, 4), (number_of // 2,), 0, 1 << 20) % (margin + 1)
    sizes = sizes.at[giver].add(-passed).at[receiver].add(passed)
    labels = jnp.searchsorted(jnp.cumsum(sizes), jnp.arange(rows * top), side="right").astype(jnp.int32)
    listing = labels.reshape(top, rows).T
    listing = listing[jax.random.permutation(jax.random.fold_in(own, 1), rows)]
    turn = jax.random.randint(jax.random.fold_in(own, 2), (rows, 1), 0, top)
    return jnp.take_along_axis(listing, (jnp.arange(top)[None, :] + turn) % top, axis=1)


def shares(count, total, limit, slope, full):
    loads = [(1 << 20) // math.isqrt(rank ** slope) + 1 for rank in range(1, count + 1)]
    largest = limit if full else min(limit, max(-(-total // count), total * loads[0] // sum(loads)))
    least = 1 if total - largest >= count - 1 else 0
    holding, spare = [largest] + [least] * (count - 1), total - largest - least * (count - 1)
    while spare > 0:
        candidates = [i for i in range(1, count) if holding[i] < largest] or [i for i in range(1, count) if holding[i] < limit]
        pool, left = sum([loads[i] for i in candidates]), spare
        for i in candidates:
            extra = min(limit - holding[i], max(1, left * loads[i] // pool), spare)
            holding[i] = holding[i] + extra
            spare = spare - extra
    return np.array(holding)


def scatter_about(rng, dims, scale, reach, cuts=(), held_as=jnp.bfloat16):
    result = jax.random.normal(rng, dims, jnp.float32) * scale
    if len(cuts) > 0:
        result = level_of(rng, dims, cuts, -0.22, 0.18) * result
    return jnp.clip(result, min=-reach, max=reach).astype(held_as)


def setup_inputs(seed: int = 0) -> dict:
    key_list = jax.random.split(jax.random.key(seed), 8)
    inputs = scatter_about(key_list[0], (TOKENS, D), 1.0, 6.0, ((0, 32),))
    out_grad = scatter_about(key_list[1], (TOKENS, D), 0.5, 3.0, ((0, 32),))
    expert_ids_keys = jax.random.split(jax.random.fold_in(key_list[2], 1), TOKENS // TOK_DEV)
    expert_ids_turns = jax.random.permutation(jax.random.fold_in(key_list[2], 3), TOKENS // TOK_DEV)
    expert_ids = jax.vmap(lambda own, number: routed_block(jax.random.fold_in(key_list[2], 2), own, number, TOK_DEV, EXPERTS, TOPK, CAP, 2))(expert_ids_keys, expert_ids_turns).reshape((TOKENS, TOPK))
    gates = jnp.clip(0.1 + 0.9 * jax.random.uniform(key_list[3], (TOKENS, TOPK), jnp.float32) ** level_of(key_list[3], (TOKENS, TOPK), ((0, 32),), -0.2, 0.2), 0.1, 1.0)
    gate_w = scatter_about(key_list[4], (EXPERTS, D, H), D ** -0.5, 0.125, ((0, 16), (1, 2)))
    up_w = scatter_about(key_list[5], (EXPERTS, D, H), D ** -0.5, 0.125, ((0, 16), (1, 2)))
    down_w = scatter_about(key_list[6], (EXPERTS, H, D), H ** -0.5, 0.21875, ((0, 16), (2, 2)))
    return {"inputs": inputs, "out_grad": out_grad, "expert_ids": expert_ids, "gates": gates, "gate_w": gate_w, "up_w": up_w, "down_w": down_w}


def reference(inputs, out_grad, expert_ids, gates, gate_w, up_w, down_w):
    block_count = TOKENS // TOK_DEV
    pair_count = TOK_DEV * TOPK
    slot_rows = GROUPS * CAP
    block_ids = expert_ids.reshape(block_count, pair_count).astype(jnp.int32)
    one_hot = (block_ids[:, :, None] == jnp.arange(EXPERTS, dtype=jnp.int32)[None, None, :]).astype(jnp.int32)
    rank_index = jnp.sum(jnp.cumsum(one_hot, axis=1, dtype=jnp.int32) * one_hot, axis=2, dtype=jnp.int32) - 1
    block_index = jnp.arange(block_count, dtype=jnp.int32)[:, None]
    replica = jnp.broadcast_to(block_index % REPLICAS, (block_count, pair_count)).astype(jnp.int32)
    position = ((block_index // REPLICAS) * CAP + rank_index).astype(jnp.int32)
    pair_index = jnp.arange(block_count * pair_count, dtype=jnp.int32).reshape(block_count, pair_count)
    sentinel = block_count * pair_count
    table = jnp.full((REPLICAS, EXPERTS, slot_rows), sentinel, jnp.int32)
    table = table.at[replica, block_ids, position].set(pair_index)
    token_of = jnp.where(table == sentinel, TOKENS, table // TOPK).astype(jnp.int32)
    input_pad = jnp.concatenate([inputs, jnp.zeros((1, D), inputs.dtype)], axis=0)
    grad_pad = jnp.concatenate([out_grad, jnp.zeros((1, D), out_grad.dtype)], axis=0)
    gate_pad = jnp.concatenate([gates.reshape(-1), jnp.zeros((1,), gates.dtype)], axis=0)
    gate_rows = gate_pad[table]
    token_by_expert = jnp.transpose(token_of, (1, 0, 2))
    gate_by_expert = jnp.transpose(gate_rows, (1, 0, 2))

    def per_expert(operands):
        token_rows, gate_col, w_gate, w_up, w_down = operands
        rows_in = input_pad[token_rows]
        scaled = (gate_col[:, :, None].astype(jnp.float32) * grad_pad[token_rows].astype(jnp.float32)).astype(jnp.bfloat16)
        rows_f = rows_in.astype(jnp.float32)
        scaled_f = scaled.astype(jnp.float32)
        gate_f = w_gate.astype(jnp.float32)
        up_f = w_up.astype(jnp.float32)
        down_f = w_down.astype(jnp.float32)
        gate_act = jnp.einsum('rsd,dh->rsh', rows_f, gate_f)
        up_act = jnp.einsum('rsd,dh->rsh', rows_f, up_f)
        sigma = jax.nn.sigmoid(gate_act)
        silu_val = gate_act * sigma
        hidden = (silu_val * up_act).astype(jnp.bfloat16)
        hidden_grad = jnp.einsum('rsd,hd->rsh', scaled_f, down_f)
        gate_grad = (hidden_grad * up_act * sigma * (1.0 + gate_act * (1.0 - sigma))).astype(jnp.bfloat16)
        up_grad = (hidden_grad * silu_val).astype(jnp.bfloat16)
        gate_grad_f = gate_grad.astype(jnp.float32)
        up_grad_f = up_grad.astype(jnp.float32)
        slot_grad = (jnp.einsum('rsh,dh->rsd', gate_grad_f, gate_f) + jnp.einsum('rsh,dh->rsd', up_grad_f, up_f)).astype(jnp.bfloat16)
        gate_part = jnp.einsum('rsd,rsh->rdh', rows_f, gate_grad_f).astype(jnp.bfloat16)
        up_part = jnp.einsum('rsd,rsh->rdh', rows_f, up_grad_f).astype(jnp.bfloat16)
        down_part = jnp.einsum('rsh,rsd->rhd', hidden.astype(jnp.float32), scaled_f).astype(jnp.bfloat16)
        gate_part, up_part, down_part = lax.optimization_barrier((gate_part, up_part, down_part))
        gate_sum = jnp.sum(gate_part.astype(jnp.float32), axis=0).astype(jnp.bfloat16)
        up_sum = jnp.sum(up_part.astype(jnp.float32), axis=0).astype(jnp.bfloat16)
        down_sum = jnp.sum(down_part.astype(jnp.float32), axis=0).astype(jnp.bfloat16)
        return slot_grad, gate_sum, up_sum, down_sum

    slot_grads, gate_w_grad, up_w_grad, down_w_grad = lax.map(
        per_expert, (token_by_expert, gate_by_expert, gate_w, up_w, down_w))
    picked = slot_grads[block_ids, replica, position]
    input_grad = jnp.sum(picked.reshape(TOKENS, TOPK, D).astype(jnp.float32), axis=1).astype(jnp.bfloat16)
    return input_grad, gate_w_grad, up_w_grad, down_w_grad
```

```python
import functools

import jax
import jax.numpy as jnp
from jax import lax
from jax.experimental import pallas as pl
from jax.experimental.pallas import tpu as pltpu
from jax.sharding import PartitionSpec as P

MESH = pl.DeviceIdType.MESH
COLS = 4
F32 = jnp.float32
BF16 = jnp.bfloat16
NT = (((1,), (1,)), ((), ()))
TN = (((0,), (0,)), ((), ()))


def layer_kernel(
    planes, experts, cap,
    ids_ref, gates_ref, x_hbm, g_hbm, gw_hbm, uw_hbm, dw_hbm,
    out_ref, gwo_ref, uwo_ref, dwo_ref,
    xg, gg, meta, st_x, st_g, rows, scaled, sel_t, wg, wu, wd, ga, ua,
    hid, gate_gr, up_gr, rows_h, scaled_h, sg, ret, rcv, snd,
    load_sem, w_send, w_recv, zm_s, zm_r, zx_s, zx_r, zg_s, zg_r,
    px_s, px_r, pg_s, pg_r, pr_s, pr_r, zr_s, zr_r, rep_s, rep_r, loc_sem,
):
    e, r = lax.axis_index("expert"), lax.axis_index("rep")
    z, c = e // COLS, e % COLS
    other = 1 - r
    tok = x_hbm.shape[0]
    last = planes - 1
    slots = COLS * cap
    half = gw_hbm.shape[1]
    feat = x_hbm.shape[1]
    hidden_n = gw_hbm.shape[2]
    total = planes * slots

    def al(v, m):
        return pl.multiple_of(v, m)

    w_at = [
        (gw_hbm.at[0], wg.at[pl.ds(al(r * half, half), half)]),
        (uw_hbm.at[0], wu.at[pl.ds(al(r * half, half), half)]),
        (dw_hbm.at[0], wd.at[:, pl.ds(al(r * half, half), half)]),
    ]
    load_x = pltpu.make_async_copy(x_hbm, xg.at[z], load_sem.at[0])
    load_g = pltpu.make_async_copy(g_hbm, gg.at[z], load_sem.at[1])
    load_x.start()
    load_g.start()
    load_w = [pltpu.make_async_copy(s, d, load_sem.at[2 + i]) for i, (s, d) in enumerate(w_at)]
    for cp in load_w:
        cp.start()

    barrier = pltpu.get_barrier_semaphore()
    for j in range(1, COLS):
        pl.semaphore_signal(barrier, inc=1, device_id=(z * COLS + (c + j) % COLS, r), device_id_type=MESH)
    pl.semaphore_signal(barrier, inc=1, device_id=(e, other), device_id_type=MESH)

    @pl.when(z < last)
    def _():
        pl.semaphore_signal(barrier, inc=1, device_id=(e + COLS, r), device_id_type=MESH)

    @pl.when(z > 0)
    def _():
        pl.semaphore_signal(barrier, inc=1, device_id=(e - COLS, r), device_id_type=MESH)

    id0, id1 = ids_ref[0:1, :], ids_ref[1:2, :]
    exp_iota = lax.broadcasted_iota(jnp.int32, (experts, tok), 0)
    one0 = jnp.where(exp_iota == id0, 1.0, 0.0)
    one1 = jnp.where(exp_iota == id1, 1.0, 0.0)
    before = jnp.where(
        lax.broadcasted_iota(jnp.int32, (tok, tok), 0) < lax.broadcasted_iota(jnp.int32, (tok, tok), 1), 1.0, 0.0
    ).astype(BF16)
    rank = jnp.dot((one0 + one1).astype(BF16), before, preferred_element_type=F32)
    slot0 = jnp.sum(rank * one0, axis=0, keepdims=True) + id0.astype(F32) * cap
    slot1 = jnp.sum(rank * one1, axis=0, keepdims=True) + id1.astype(F32) * cap
    meta[z] = jnp.concatenate(
        [slot0, slot1, gates_ref[0:1, :], gates_ref[1:2, :], jnp.zeros((4, tok), F32)], axis=0
    )
    neighbours = COLS + jnp.where(z < last, 1, 0) + jnp.where(z > 0, 1, 0)
    pl.semaphore_wait(barrier, neighbours)

    def up(buf, ss, rs, k):
        return pltpu.make_async_remote_copy(
            src_ref=buf.at[jnp.maximum(z - k, 0)], dst_ref=buf.at[jnp.maximum(z - k, 0)],
            send_sem=ss.at[0, k], recv_sem=rs.at[0, k], device_id=(e + COLS, r), device_id_type=MESH)

    def down(buf, ss, rs, k):
        return pltpu.make_async_remote_copy(
            src_ref=buf.at[jnp.minimum(z + k, last)], dst_ref=buf.at[jnp.minimum(z + k, last)],
            send_sem=ss.at[1, k], recv_sem=rs.at[1, k], device_id=(e - COLS, r), device_id_type=MESH)

    def can_up(k):
        return (z < last) & (z - k >= 0)

    def can_down(k):
        return (z > 0) & (z + k <= last)

    def chain_start(buf, ss, rs, k):
        @pl.when(can_up(k))
        def _():
            up(buf, ss, rs, k).start()

        @pl.when(can_down(k))
        def _():
            down(buf, ss, rs, k).start()

    def chain_wait(buf, ss, rs, k):
        @pl.when(z - 1 - k >= 0)
        def _():
            b = buf.at[jnp.maximum(z - 1 - k, 0)]
            pltpu.make_async_remote_copy(
                src_ref=b, dst_ref=b, send_sem=ss.at[0, k], recv_sem=rs.at[0, k],
                device_id=(e, other), device_id_type=MESH).wait_recv()

        @pl.when(z + 1 + k <= last)
        def _():
            b = buf.at[jnp.minimum(z + 1 + k, last)]
            pltpu.make_async_remote_copy(
                src_ref=b, dst_ref=b, send_sem=ss.at[1, k], recv_sem=rs.at[1, k],
                device_id=(e, other), device_id_type=MESH).wait_recv()

    def chain_drain(buf, ss, rs):
        for k in range(planes - 1):
            @pl.when(can_up(k))
            def _(k=k):
                up(buf, ss, rs, k).wait_send()

            @pl.when(can_down(k))
            def _(k=k):
                down(buf, ss, rs, k).wait_send()

    def plane_copy(st, dst, ss, rs, p, j):
        d = (c + j) % COLS
        return pltpu.make_async_remote_copy(
            src_ref=st.at[p, pl.ds(al(d * cap, cap), cap)],
            dst_ref=dst.at[p, pl.ds(al(c * cap, cap), cap)],
            send_sem=ss.at[p, j - 1], recv_sem=rs.at[p, j - 1],
            device_id=(z * COLS + d, r), device_id_type=MESH)

    def plane_send(st, dst, ss, rs, p):
        for j in range(1, COLS):
            plane_copy(st, dst, ss, rs, p, j).start()
        dst[p, pl.ds(al(c * cap, cap), cap), :] = st[p, pl.ds(al(c * cap, cap), cap), :]

    def plane_wait(st, dst, ss, rs, p):
        for j in range(1, COLS):
            plane_copy(st, dst, ss, rs, p, j).wait_recv()

    def plane_drain(st, dst, ss, rs):
        for p in range(planes):
            for j in range(1, COLS):
                plane_copy(st, dst, ss, rs, p, j).wait_send()

    def selection(p):
        m = meta[p]
        place = (lax.broadcasted_iota(jnp.int32, (slots, tok), 0) + z * slots).astype(F32)
        return jnp.where(place == m[0:1, :], 1.0, 0.0), jnp.where(place == m[1:2, :], 1.0, 0.0), m

    def dispatch_x(p):
        s0, s1, _ = selection(p)
        pick = s0 + s1
        sel_t[p] = pick.T.astype(BF16)
        st_x[p] = jnp.dot(pick.astype(BF16), xg[p], preferred_element_type=F32).astype(BF16)
        plane_send(st_x, rows, px_s, px_r, p)

    def dispatch_g(p):
        s0, s1, m = selection(p)
        gate = jnp.sum(s0 * m[2:3, :] + s1 * m[3:4, :], axis=1, keepdims=True)
        picked = jnp.dot((s0 + s1).astype(BF16), gg[p], preferred_element_type=F32)
        st_g[p] = (picked * gate).astype(BF16)
        plane_send(st_g, scaled, pg_s, pg_r, p)

    def both(fn, k):
        @pl.when(z - 1 - k >= 0)
        def _():
            fn(jnp.maximum(z - 1 - k, 0))

        @pl.when(z + 1 + k <= last)
        def _():
            fn(jnp.minimum(z + 1 + k, last))

    chain_start(meta, zm_s, zm_r, 0)
    load_x.wait()
    chain_start(xg, zx_s, zx_r, 0)

    def w_copy(i):
        s, d = w_at[i]
        return pltpu.make_async_remote_copy(
            src_ref=s, dst_ref=d, send_sem=w_send.at[i], recv_sem=w_recv.at[i],
            device_id=(e, other), device_id_type=MESH)

    for i in range(3):
        w_copy(i).start()
    load_g.wait()
    dispatch_x(z)
    for k in range(planes - 1):
        chain_wait(meta, zm_s, zm_r, k)
        chain_wait(xg, zx_s, zx_r, k)
        if k < planes - 2:
            chain_start(meta, zm_s, zm_r, k + 1)
            chain_start(xg, zx_s, zx_r, k + 1)
        if k == planes - 3:
            chain_start(gg, zg_s, zg_r, 0)
        both(dispatch_x, k)
    dispatch_g(z)
    chain_wait(gg, zg_s, zg_r, 0)
    chain_start(gg, zg_s, zg_r, 1)
    both(dispatch_g, 0)
    for cp in load_w:
        cp.wait()
    for i in range(3):
        w_copy(i).wait()
    for p in range(planes):
        plane_wait(st_x, rows, px_s, px_r, p)

    def halves(src, dst, i):
        lo = pl.ds(al(r * half, half), half)
        hi = pl.ds(al(other * half, half), half)
        return (
            pltpu.make_async_copy(src.at[:, :, lo], dst.at[r], loc_sem.at[i]),
            pltpu.make_async_remote_copy(
                src_ref=src.at[:, :, hi], dst_ref=dst.at[r], send_sem=rep_s.at[i], recv_sem=rep_r.at[i],
                device_id=(e, other), device_id_type=MESH),
        )

    rows_cp = halves(rows, rows_h, 0)
    for cp in rows_cp:
        cp.start()
    step_h = 256 if hidden_n % 256 == 0 else hidden_n

    @pl.loop(0, hidden_n // step_h)
    def _(i):
        cols = pl.ds(al(i * step_h, step_h), step_h)
        a = rows[...].reshape(total, feat)
        ga[:, cols] = jnp.dot(a, wg[:, cols], preferred_element_type=F32)
        ua[:, cols] = jnp.dot(a, wu[:, cols], preferred_element_type=F32)

    for k in range(1, planes - 1):
        chain_wait(gg, zg_s, zg_r, k)
        if k < planes - 2:
            chain_start(gg, zg_s, zg_r, k + 1)
        both(dispatch_g, k)
    for p in range(planes):
        plane_wait(st_g, scaled, pg_s, pg_r, p)
    scaled_cp = halves(scaled, scaled_h, 1)
    for cp in scaled_cp:
        cp.start()

    @pl.loop(0, hidden_n // step_h)
    def _(i):
        cols = pl.ds(al(i * step_h, step_h), step_h)
        hg = lax.dot_general(scaled[...].reshape(total, feat), wd[cols, :], NT, preferred_element_type=F32)
        gate_act, up_act = ga[:, cols], ua[:, cols]
        sigma = jax.nn.sigmoid(gate_act)
        silu = gate_act * sigma
        hid[r, :, cols] = (silu * up_act).astype(BF16)
        gate_gr[r, :, cols] = (hg * up_act * sigma * (1.0 + gate_act * (1.0 - sigma))).astype(BF16)
        up_gr[r, :, cols] = (hg * silu).astype(BF16)

    def rep_copy(ref, i):
        return pltpu.make_async_remote_copy(
            src_ref=ref.at[r], dst_ref=ref.at[r], send_sem=rep_s.at[i], recv_sem=rep_r.at[i],
            device_id=(e, other), device_id_type=MESH)

    rep_cp = [rep_copy(ref, 2 + i) for i, ref in enumerate((gate_gr, up_gr, hid))]
    for cp in rep_cp:
        cp.start()
    step_d = 256

    @pl.loop(0, feat // step_d)
    def _(i):
        cols = pl.ds(al(i * step_d, step_d), step_d)
        v = lax.dot_general(gate_gr[r], wg[cols, :], NT, preferred_element_type=F32)
        v = v + lax.dot_general(up_gr[r], wu[cols, :], NT, preferred_element_type=F32)
        sg[:, :, cols] = v.astype(BF16).reshape(planes, slots, step_d)

    order = sorted(range(planes), key=lambda p: min(p, last - p))
    for p in order:
        plane_send(sg, ret, pr_s, pr_r, p)

    def part(p):
        return jnp.dot(sel_t[p], ret[p], preferred_element_type=F32)

    def ret_copy(way, p):
        return pltpu.make_async_remote_copy(
            src_ref=snd.at[p], dst_ref=rcv.at[way, p], send_sem=zr_s.at[p], recv_sem=zr_r.at[way, p],
            device_id=(e + COLS if way == 0 else e - COLS, r), device_id_type=MESH)

    def ret_wait(way, p):
        pltpu.make_async_remote_copy(
            src_ref=snd.at[p], dst_ref=rcv.at[way, p], send_sem=zr_s.at[p], recv_sem=zr_r.at[way, p],
            device_id=(e, other), device_id_type=MESH).wait_recv()

    def forward(way, p, first):
        @pl.when(first)
        def _():
            snd[p] = part(p).astype(BF16)

        @pl.when(jnp.logical_not(first))
        def _():
            ret_wait(way, p)
            snd[p] = (part(p) + rcv[way, p].astype(F32)).astype(BF16)

        ret_copy(way, p).start()

    def weight_in(a_half, grads, out):
        step = 256

        @pl.loop(0, half // step)
        def _(i):
            cols = pl.ds(al(i * step, step), step)
            v = lax.dot_general(a_half[0, :, :, cols].reshape(total, step), grads[0], TN, preferred_element_type=F32)
            v = v + lax.dot_general(a_half[1, :, :, cols].reshape(total, step), grads[1], TN, preferred_element_type=F32)
            out[0, cols, :] = v.astype(BF16)

    def weight_down():
        @pl.loop(0, hidden_n // step_h)
        def _(i):
            cols = pl.ds(al(i * step_h, step_h), step_h)
            v = lax.dot_general(hid[0, :, cols], scaled_h[0].reshape(total, half), TN, preferred_element_type=F32)
            v = v + lax.dot_general(hid[1, :, cols], scaled_h[1].reshape(total, half), TN, preferred_element_type=F32)
            dwo_ref[0, cols, :] = v.astype(BF16)

    for p in order:
        plane_wait(sg, ret, pr_s, pr_r, p)
    for k in range(planes):
        @pl.when(k < z)
        def _(k=k):
            forward(1, k, z == last)

        @pl.when(last - k > z)
        def _(k=k):
            forward(0, last - k, z == 0)

        if k == 0:
            for cp in (rows_cp, scaled_cp):
                cp[0].wait()
                cp[1].wait()
            for cp in rep_cp:
                cp.wait()
            weight_in(rows_h, gate_gr, gwo_ref)
        elif k == 1:
            weight_in(rows_h, up_gr, uwo_ref)
        elif k == 2:
            weight_down()

    own = part(z)
    snd[z] = own.astype(BF16)

    @pl.when(z < last)
    def _():
        ret_wait(1, z)

    @pl.when(z > 0)
    def _():
        ret_wait(0, z)

    above = jnp.where(z < last, rcv[1, z].astype(F32), 0.0)
    below = jnp.where(z > 0, rcv[0, z].astype(F32), 0.0)
    out_ref[...] = (own + above + below).astype(BF16)

    chain_drain(meta, zm_s, zm_r)
    chain_drain(xg, zx_s, zx_r)
    chain_drain(gg, zg_s, zg_r)
    plane_drain(st_x, rows, px_s, px_r)
    plane_drain(st_g, scaled, pg_s, pg_r)
    plane_drain(sg, ret, pr_s, pr_r)
    for p in range(planes):
        @pl.when(p < z)
        def _(p=p):
            ret_copy(1, p).wait_send()

        @pl.when(p > z)
        def _(p=p):
            ret_copy(0, p).wait_send()


def chained(inputs, out_grad, expert_ids, gates, gate_w, up_w, down_w):
    tok, feat = inputs.shape
    half, hidden_n = gate_w.shape[1], gate_w.shape[2]
    experts = lax.axis_size("expert")
    planes = experts // COLS
    cap = 2 * tok * expert_ids.shape[1] // experts
    slots = COLS * cap
    total = planes * slots
    dma = pltpu.SemaphoreType.DMA
    vmem = pl.BlockSpec(memory_space=pltpu.VMEM)
    hbm = pl.BlockSpec(memory_space=pl.ANY)
    block = (planes, slots, feat)
    scratch = [
        pltpu.VMEM((planes, tok, feat), BF16), pltpu.VMEM((planes, tok, feat), BF16),
        pltpu.VMEM((planes, 8, tok), F32),
        pltpu.VMEM(block, BF16), pltpu.VMEM(block, BF16), pltpu.VMEM(block, BF16), pltpu.VMEM(block, BF16),
        pltpu.VMEM((planes, tok, slots), BF16),
        pltpu.VMEM((feat, hidden_n), BF16), pltpu.VMEM((feat, hidden_n), BF16), pltpu.VMEM((hidden_n, feat), BF16),
        pltpu.VMEM((total, hidden_n), F32), pltpu.VMEM((total, hidden_n), F32),
        pltpu.VMEM((2, total, hidden_n), BF16), pltpu.VMEM((2, total, hidden_n), BF16),
        pltpu.VMEM((2, total, hidden_n), BF16),
        pltpu.VMEM((2, planes, slots, half), BF16), pltpu.VMEM((2, planes, slots, half), BF16),
        pltpu.VMEM(block, BF16), pltpu.VMEM(block, BF16),
        pltpu.VMEM((2, planes, tok, feat), BF16), pltpu.VMEM((planes, tok, feat), BF16),
        dma((5,)), dma((3,)), dma((3,)),
        dma((2, planes - 1)), dma((2, planes - 1)), dma((2, planes - 1)), dma((2, planes - 1)),
        dma((2, planes - 1)), dma((2, planes - 1)),
        dma((planes, COLS - 1)), dma((planes, COLS - 1)), dma((planes, COLS - 1)), dma((planes, COLS - 1)),
        dma((planes, COLS - 1)), dma((planes, COLS - 1)),
        dma((planes,)), dma((2, planes)), dma((5,)), dma((5,)), dma((2,)),
    ]
    return pl.pallas_call(
        functools.partial(layer_kernel, planes, experts, cap),
        out_shape=(
            jax.ShapeDtypeStruct((tok, feat), BF16),
            jax.ShapeDtypeStruct(gate_w.shape, BF16),
            jax.ShapeDtypeStruct(up_w.shape, BF16),
            jax.ShapeDtypeStruct(down_w.shape, BF16),
        ),
        in_specs=[vmem, vmem] + [hbm] * 5,
        out_specs=(vmem,) * 4,
        scratch_shapes=scratch,
        compiler_params=pltpu.CompilerParams(
            collective_id=0, has_side_effects=True, vmem_limit_bytes=60 * 1024 * 1024
        ),
        cost_estimate=pl.CostEstimate(
            flops=18 * total * feat * hidden_n, bytes_accessed=8 * feat * hidden_n, transcendentals=total * hidden_n
        ),
    )(expert_ids.T, gates.T, inputs, out_grad, gate_w, up_w, down_w)


def arrange(received, owners, local_exp, capacity):
    feature_n = received.shape[1]
    shaped = received.reshape(owners, local_exp, capacity, feature_n)
    return shaped.transpose(1, 0, 2, 3).reshape(local_exp, owners * capacity, feature_n)


def restore(slot_rows, owners, capacity):
    local_exp = slot_rows.shape[0]
    feature_n = slot_rows.shape[2]
    shaped = slot_rows.reshape(local_exp, owners, capacity, feature_n)
    return shaped.transpose(1, 0, 2, 3).reshape(owners * local_exp * capacity, feature_n)


def local(inputs, out_grad, expert_ids, gates, gate_w, up_w, down_w):
    if lax.axis_size("expert") <= 16:
        return chained(inputs, out_grad, expert_ids, gates, gate_w, up_w, down_w)
    tok_dev = inputs.shape[0]
    feature_n = inputs.shape[1]
    topk_n = expert_ids.shape[1]
    local_exp = gate_w.shape[0]
    owners = lax.axis_size("expert")
    expert_total = local_exp * owners
    capacity = 2 * tok_dev * topk_n // expert_total
    pair_count = tok_dev * topk_n
    slot_total = expert_total * capacity
    flat_ids = expert_ids.reshape(pair_count)
    one_hot = (flat_ids[:, None] == jnp.arange(expert_total, dtype=jnp.int32)[None, :]).astype(
        jnp.int32
    )
    rank_index = (
        jnp.sum(jnp.cumsum(one_hot, axis=0, dtype=jnp.int32) * one_hot, axis=1, dtype=jnp.int32) - 1
    )
    slot_index = flat_ids * capacity + rank_index
    input_pairs = jnp.repeat(inputs, topk_n, axis=0)
    scaled_pairs = (
        gates.reshape(pair_count, 1) * jnp.repeat(out_grad, topk_n, axis=0).astype(jnp.float32)
    ).astype(jnp.bfloat16)
    send_inputs = jnp.zeros((slot_total, feature_n), jnp.bfloat16).at[slot_index].set(input_pairs)
    send_grads = jnp.zeros((slot_total, feature_n), jnp.bfloat16).at[slot_index].set(scaled_pairs)
    full_gate, full_up, full_down = (
        lax.all_gather(gate_w, "rep", axis=1, tiled=True),
        lax.all_gather(up_w, "rep", axis=1, tiled=True),
        lax.all_gather(down_w, "rep", axis=2, tiled=True),
    )
    recv_inputs, recv_grads = (
        lax.all_to_all(send_inputs, "expert", split_axis=0, concat_axis=0, tiled=True),
        lax.all_to_all(send_grads, "expert", split_axis=0, concat_axis=0, tiled=True),
    )
    rows_in = arrange(recv_inputs, owners, local_exp, capacity)
    scaled_rows = arrange(recv_grads, owners, local_exp, capacity)
    gate_act = jnp.einsum("erd,edh->erh", rows_in, full_gate, preferred_element_type=jnp.float32)
    up_act = jnp.einsum("erd,edh->erh", rows_in, full_up, preferred_element_type=jnp.float32)
    gate_act, up_act = (gate_act, up_act)
    sigma = jax.nn.sigmoid(gate_act)
    silu_val = gate_act * sigma
    hidden = (silu_val * up_act).astype(jnp.bfloat16)
    hidden_grad = jnp.einsum(
        "erd,ehd->erh", scaled_rows, full_down, preferred_element_type=jnp.float32
    )
    gate_grad = (hidden_grad * up_act * sigma * (1.0 + gate_act * (1.0 - sigma))).astype(
        jnp.bfloat16
    )
    up_grad = (hidden_grad * silu_val).astype(jnp.bfloat16)
    first = jnp.einsum("erh,edh->erd", gate_grad, full_gate, preferred_element_type=jnp.float32)
    slot_grad = (
        first + jnp.einsum("erh,edh->erd", up_grad, full_up, preferred_element_type=jnp.float32)
    ).astype(jnp.bfloat16)
    returned = lax.all_to_all(
        restore(slot_grad, owners, capacity), "expert", split_axis=0, concat_axis=0, tiled=True
    )
    gate_part = jnp.einsum("erd,erh->edh", rows_in, gate_grad, preferred_element_type=jnp.float32)
    up_part = jnp.einsum("erd,erh->edh", rows_in, up_grad, preferred_element_type=jnp.float32)
    down_part = jnp.einsum("erh,erd->ehd", hidden, scaled_rows, preferred_element_type=jnp.float32)
    gate_sum, up_sum, down_sum = (
        lax.psum_scatter(
            gate_part.astype(jnp.bfloat16), "rep", scatter_dimension=1, tiled=True
        ).astype(jnp.float32),
        lax.psum_scatter(
            up_part.astype(jnp.bfloat16), "rep", scatter_dimension=1, tiled=True
        ).astype(jnp.float32),
        lax.psum_scatter(
            down_part.astype(jnp.bfloat16), "rep", scatter_dimension=2, tiled=True
        ).astype(jnp.float32),
    )
    picked = returned[slot_index]
    input_grad = jnp.sum(
        picked.reshape(tok_dev, topk_n, feature_n).astype(jnp.float32), axis=1
    ).astype(jnp.bfloat16)
    return (
        input_grad,
        gate_sum.astype(jnp.bfloat16),
        up_sum.astype(jnp.bfloat16),
        down_sum.astype(jnp.bfloat16),
    )


def solution(mesh):
    return jax.shard_map(
        local,
        mesh=mesh,
        in_specs=(
            P(("expert", "rep"), None),
            P(("expert", "rep"), None),
            P(("expert", "rep"), None),
            P(("expert", "rep"), None),
            P("expert", "rep", None),
            P("expert", "rep", None),
            P("expert", None, "rep"),
        ),
        out_specs=(
            P(("expert", "rep"), None),
            P("expert", "rep", None),
            P("expert", "rep", None),
            P("expert", None, "rep"),
        ),
        check_vma=False,
    )
```

```python
import functools

import jax
import jax.numpy as jnp
from jax import lax
from jax.experimental import pallas as pl
from jax.experimental.pallas import tpu as pltpu
from jax.sharding import PartitionSpec as P

MESH = pl.DeviceIdType.MESH
COLS = 4
PIECES = 4
F32 = jnp.float32
BF16 = jnp.bfloat16
NT = (((1,), (1,)), ((), ()))
TN = (((0,), (0,)), ((), ()))


def layer_kernel(
    planes, experts, cap,
    ids_ref, gates_ref, x_hbm, g_hbm, gw_hbm, uw_hbm, dw_hbm,
    out_ref, gwo_ref, uwo_ref, dwo_ref,
    xg, gg, meta, st_x, st_g, rows, scaled, sel_t, wg, wu, wd, ga, ua,
    hid, gate_gr, up_gr, rows_h, scaled_h, sg, ret, rcv, snd,
    own_part, gwo_v, uwo_v, dwo_v,
    load_sem, w_send, w_recv, zm_s, zm_r, zx_s, zx_r, zg_s, zg_r,
    px_s, px_r, pg_s, pg_r, pr_s, pr_r, zr_s, zr_r, rep_s, rep_r, loc_sem, out_sem,
):
    e, r = lax.axis_index("expert"), lax.axis_index("rep")
    z, c = e // COLS, e % COLS
    other = 1 - r
    tok = x_hbm.shape[0]
    last = planes - 1
    slots = COLS * cap
    half = gw_hbm.shape[1]
    feat = x_hbm.shape[1]
    hidden_n = gw_hbm.shape[2]
    total = planes * slots

    def al(v, m):
        return pl.multiple_of(v, m)

    w_at = [
        (gw_hbm.at[0], wg.at[pl.ds(al(r * half, half), half)]),
        (uw_hbm.at[0], wu.at[pl.ds(al(r * half, half), half)]),
        (dw_hbm.at[0], wd.at[:, pl.ds(al(r * half, half), half)]),
    ]
    load_x = pltpu.make_async_copy(x_hbm, xg.at[z], load_sem.at[0])
    load_g = pltpu.make_async_copy(g_hbm, gg.at[z], load_sem.at[1])
    load_x.start()
    load_g.start()
    load_w = [pltpu.make_async_copy(s, d, load_sem.at[2 + i]) for i, (s, d) in enumerate(w_at)]
    for cp in load_w:
        cp.start()

    barrier = pltpu.get_barrier_semaphore()
    for j in range(1, COLS):
        pl.semaphore_signal(barrier, inc=1, device_id=(z * COLS + (c + j) % COLS, r), device_id_type=MESH)
    pl.semaphore_signal(barrier, inc=1, device_id=(e, other), device_id_type=MESH)

    @pl.when(z < last)
    def _():
        pl.semaphore_signal(barrier, inc=1, device_id=(e + COLS, r), device_id_type=MESH)

    @pl.when(z > 0)
    def _():
        pl.semaphore_signal(barrier, inc=1, device_id=(e - COLS, r), device_id_type=MESH)

    id0, id1 = ids_ref[0:1, :], ids_ref[1:2, :]
    exp_iota = lax.broadcasted_iota(jnp.int32, (experts, tok), 0)
    one0 = jnp.where(exp_iota == id0, 1.0, 0.0)
    one1 = jnp.where(exp_iota == id1, 1.0, 0.0)
    before = jnp.where(
        lax.broadcasted_iota(jnp.int32, (tok, tok), 0) < lax.broadcasted_iota(jnp.int32, (tok, tok), 1), 1.0, 0.0
    ).astype(BF16)
    rank = jnp.dot((one0 + one1).astype(BF16), before, preferred_element_type=F32)
    slot0 = jnp.sum(rank * one0, axis=0, keepdims=True) + id0.astype(F32) * cap
    slot1 = jnp.sum(rank * one1, axis=0, keepdims=True) + id1.astype(F32) * cap
    meta[z] = jnp.concatenate(
        [slot0, slot1, gates_ref[0:1, :], gates_ref[1:2, :], jnp.zeros((4, tok), F32)], axis=0
    )
    neighbours = COLS + jnp.where(z < last, 1, 0) + jnp.where(z > 0, 1, 0)
    pl.semaphore_wait(barrier, neighbours)

    def up(buf, ss, rs, k):
        return pltpu.make_async_remote_copy(
            src_ref=buf.at[jnp.maximum(z - k, 0)], dst_ref=buf.at[jnp.maximum(z - k, 0)],
            send_sem=ss.at[0, k], recv_sem=rs.at[0, k], device_id=(e + COLS, r), device_id_type=MESH)

    def down(buf, ss, rs, k):
        return pltpu.make_async_remote_copy(
            src_ref=buf.at[jnp.minimum(z + k, last)], dst_ref=buf.at[jnp.minimum(z + k, last)],
            send_sem=ss.at[1, k], recv_sem=rs.at[1, k], device_id=(e - COLS, r), device_id_type=MESH)

    def can_up(k):
        return (z < last) & (z - k >= 0)

    def can_down(k):
        return (z > 0) & (z + k <= last)

    def chain_start(buf, ss, rs, k):
        @pl.when(can_up(k))
        def _():
            up(buf, ss, rs, k).start()

        @pl.when(can_down(k))
        def _():
            down(buf, ss, rs, k).start()

    def chain_wait(buf, ss, rs, k):
        @pl.when(z - 1 - k >= 0)
        def _():
            b = buf.at[jnp.maximum(z - 1 - k, 0)]
            pltpu.make_async_remote_copy(
                src_ref=b, dst_ref=b, send_sem=ss.at[0, k], recv_sem=rs.at[0, k],
                device_id=(e, other), device_id_type=MESH).wait_recv()

        @pl.when(z + 1 + k <= last)
        def _():
            b = buf.at[jnp.minimum(z + 1 + k, last)]
            pltpu.make_async_remote_copy(
                src_ref=b, dst_ref=b, send_sem=ss.at[1, k], recv_sem=rs.at[1, k],
                device_id=(e, other), device_id_type=MESH).wait_recv()

    def chain_drain(buf, ss, rs):
        for k in range(planes - 1):
            @pl.when(can_up(k))
            def _(k=k):
                up(buf, ss, rs, k).wait_send()

            @pl.when(can_down(k))
            def _(k=k):
                down(buf, ss, rs, k).wait_send()

    def plane_copy(st, dst, ss, rs, p, j):
        d = (c + j) % COLS
        return pltpu.make_async_remote_copy(
            src_ref=st.at[p, pl.ds(al(d * cap, cap), cap)],
            dst_ref=dst.at[p, pl.ds(al(c * cap, cap), cap)],
            send_sem=ss.at[p, j - 1], recv_sem=rs.at[p, j - 1],
            device_id=(z * COLS + d, r), device_id_type=MESH)

    def plane_send(st, dst, ss, rs, p):
        for j in range(1, COLS):
            plane_copy(st, dst, ss, rs, p, j).start()
        dst[p, pl.ds(al(c * cap, cap), cap), :] = st[p, pl.ds(al(c * cap, cap), cap), :]

    def plane_wait(st, dst, ss, rs, p):
        for j in range(1, COLS):
            plane_copy(st, dst, ss, rs, p, j).wait_recv()

    def plane_drain(st, dst, ss, rs):
        for p in range(planes):
            for j in range(1, COLS):
                plane_copy(st, dst, ss, rs, p, j).wait_send()

    def selection(p):
        m = meta[p]
        place = (lax.broadcasted_iota(jnp.int32, (slots, tok), 0) + z * slots).astype(F32)
        return jnp.where(place == m[0:1, :], 1.0, 0.0), jnp.where(place == m[1:2, :], 1.0, 0.0), m

    def dispatch_x(p):
        s0, s1, _ = selection(p)
        pick = s0 + s1
        sel_t[p] = pick.T.astype(BF16)
        st_x[p] = jnp.dot(pick.astype(BF16), xg[p], preferred_element_type=F32).astype(BF16)
        plane_send(st_x, rows, px_s, px_r, p)

    def dispatch_g(p):
        s0, s1, m = selection(p)
        gate = jnp.sum(s0 * m[2:3, :] + s1 * m[3:4, :], axis=1, keepdims=True)
        picked = jnp.dot((s0 + s1).astype(BF16), gg[p], preferred_element_type=F32)
        st_g[p] = (picked * gate).astype(BF16)
        plane_send(st_g, scaled, pg_s, pg_r, p)

    def both(fn, k):
        @pl.when(z - 1 - k >= 0)
        def _():
            fn(jnp.maximum(z - 1 - k, 0))

        @pl.when(z + 1 + k <= last)
        def _():
            fn(jnp.minimum(z + 1 + k, last))

    def w_copy(i):
        s, d = w_at[i]
        return pltpu.make_async_remote_copy(
            src_ref=s, dst_ref=d, send_sem=w_send.at[i], recv_sem=w_recv.at[i],
            device_id=(e, other), device_id_type=MESH)

    def halves(src, dst, i, p):
        lo = pl.ds(al(r * half, half), half)
        hi = pl.ds(al(other * half, half), half)
        return (
            pltpu.make_async_copy(src.at[p, :, lo], dst.at[r, p], loc_sem.at[i, p]),
            pltpu.make_async_remote_copy(
                src_ref=src.at[p, :, hi], dst_ref=dst.at[r, p], send_sem=rep_s.at[i, p], recv_sem=rep_r.at[i, p],
                device_id=(e, other), device_id_type=MESH),
        )

    def rep_copy(ref, i, p):
        return pltpu.make_async_remote_copy(
            src_ref=ref.at[r, p], dst_ref=ref.at[r, p], send_sem=rep_s.at[i, p], recv_sem=rep_r.at[i, p],
            device_id=(e, other), device_id_type=MESH)

    step_h = 256 if hidden_n % 256 == 0 else hidden_n
    step_d = 512

    def acts(p):
        plane_wait(st_x, rows, px_s, px_r, p)
        for cp in halves(rows, rows_h, 0, p):
            cp.start()

        @pl.loop(0, hidden_n // step_h)
        def _(i):
            cols = pl.ds(al(i * step_h, step_h), step_h)
            ga[p, :, cols] = jnp.dot(rows[p], wg[:, cols], preferred_element_type=F32)
            ua[p, :, cols] = jnp.dot(rows[p], wu[:, cols], preferred_element_type=F32)

    def grads(p):
        plane_wait(st_g, scaled, pg_s, pg_r, p)
        for cp in halves(scaled, scaled_h, 1, p):
            cp.start()

        @pl.loop(0, hidden_n // step_h)
        def _(i):
            cols = pl.ds(al(i * step_h, step_h), step_h)
            hg = lax.dot_general(scaled[p], wd[cols, :], NT, preferred_element_type=F32)
            gate_act, up_act = ga[p, :, cols], ua[p, :, cols]
            sigma = jax.nn.sigmoid(gate_act)
            silu = gate_act * sigma
            hid[r, p, :, cols] = (silu * up_act).astype(BF16)
            gate_gr[r, p, :, cols] = (hg * up_act * sigma * (1.0 + gate_act * (1.0 - sigma))).astype(BF16)
            up_gr[r, p, :, cols] = (hg * silu).astype(BF16)

        @pl.loop(0, feat // step_d)
        def _(i):
            cols = pl.ds(al(i * step_d, step_d), step_d)
            v = lax.dot_general(gate_gr[r, p], wg[cols, :], NT, preferred_element_type=F32)
            v = v + lax.dot_general(up_gr[r, p], wu[cols, :], NT, preferred_element_type=F32)
            sg[p, :, cols] = v.astype(BF16)

        plane_send(sg, ret, pr_s, pr_r, p)
        for i, ref in enumerate((gate_gr, up_gr, hid)):
            rep_copy(ref, 2 + i, p).start()

    piece = tok // PIECES

    def ret_copy(way, p, q):
        at = pl.ds(q * piece, piece)
        return pltpu.make_async_remote_copy(
            src_ref=snd.at[p, at], dst_ref=rcv.at[way, p, at], send_sem=zr_s.at[p, q], recv_sem=zr_r.at[way, p, q],
            device_id=(jnp.where(way == 0, e + COLS, e - COLS), r), device_id_type=MESH)

    def ret_wait(way, p, q):
        at = pl.ds(q * piece, piece)
        pltpu.make_async_remote_copy(
            src_ref=snd.at[p, at], dst_ref=rcv.at[way, p, at], send_sem=zr_s.at[p, q], recv_sem=zr_r.at[way, p, q],
            device_id=(e, other), device_id_type=MESH).wait_recv()

    def forward(way, p, first):
        plane_wait(sg, ret, pr_s, pr_r, p)
        own_part[...] = jnp.dot(sel_t[p], ret[p], preferred_element_type=F32)
        for q in range(PIECES):
            at = pl.ds(q * piece, piece)

            @pl.when(first)
            def _():
                snd[p, at, :] = own_part[at, :].astype(BF16)

            @pl.when(jnp.logical_not(first))
            def _():
                ret_wait(way, p, q)
                snd[p, at, :] = (own_part[at, :] + rcv[way, p, at, :].astype(F32)).astype(BF16)

            ret_copy(way, p, q).start()

    def forward_both(k):
        @pl.loop(0, 2)
        def _(side):
            way = jnp.where(z >= planes // 2, 1 - side, side)
            p = jnp.where(way == 1, last - 1 - k, k + 1)

            @pl.when(((way == 1) & (p < z)) | ((way == 0) & (p > z)))
            def _():
                forward(way, p, ((way == 1) & (z == last)) | ((way == 0) & (z == 0)))

    def weight_in(a_half, grad, out):
        step = 256

        @pl.loop(0, half // step)
        def _(i):
            cols = pl.ds(al(i * step, step), step)
            v = 0.0
            for rep in range(2):
                v = v + lax.dot_general(
                    a_half[rep, :, :, cols].reshape(total, step), grad[rep].reshape(total, hidden_n), TN,
                    preferred_element_type=F32)
            out[0, cols, :] = v.astype(BF16)

    def weight_down():
        @pl.loop(0, hidden_n // step_h)
        def _(i):
            cols = pl.ds(al(i * step_h, step_h), step_h)
            v = 0.0
            for rep in range(2):
                v = v + lax.dot_general(
                    hid[rep, :, :, cols].reshape(total, step_h), scaled_h[rep].reshape(total, half), TN,
                    preferred_element_type=F32)
            dwo_v[0, cols, :] = v.astype(BF16)

    def out_copy(i):
        src, dst = ((gwo_v, gwo_ref), (uwo_v, uwo_ref), (dwo_v, dwo_ref))[i]
        return pltpu.make_async_copy(src, dst, out_sem.at[i])

    chain_start(meta, zm_s, zm_r, 0)
    load_x.wait()
    chain_start(xg, zx_s, zx_r, 0)
    load_g.wait()
    chain_start(gg, zg_s, zg_r, 0)
    for i in range(3):
        w_copy(i).start()
    dispatch_x(z)
    dispatch_g(z)
    for k in range(planes - 1):
        chain_wait(meta, zm_s, zm_r, k)
        chain_wait(xg, zx_s, zx_r, k)
        if k < planes - 2:
            chain_start(meta, zm_s, zm_r, k + 1)
            chain_start(xg, zx_s, zx_r, k + 1)
        both(dispatch_x, k)
        if k == 0:
            for cp in load_w:
                cp.wait()
            for i in range(3):
                w_copy(i).wait()
            acts(z)
        else:
            both(acts, k - 1)
        if k > 1:
            forward_both(k - 2)
        chain_wait(gg, zg_s, zg_r, k)
        if k < planes - 2:
            chain_start(gg, zg_s, zg_r, k + 1)
        both(dispatch_g, k)
        if k == 0:
            grads(z)
        else:
            both(grads, k - 1)
    both(acts, planes - 2)
    forward_both(planes - 3)
    both(grads, planes - 2)

    for p in range(planes):
        for i, (src, dst) in enumerate(((rows, rows_h), (scaled, scaled_h))):
            for cp in halves(src, dst, i, p):
                cp.wait()
        for i, ref in enumerate((gate_gr, up_gr, hid)):
            rep_copy(ref, 2 + i, p).wait()
    weight_in(rows_h, gate_gr, gwo_v)
    out_copy(0).start()
    forward_both(planes - 2)
    weight_in(rows_h, up_gr, uwo_v)
    out_copy(1).start()
    weight_down()
    out_copy(2).start()

    plane_wait(sg, ret, pr_s, pr_r, z)
    own_part[...] = jnp.dot(sel_t[z], ret[z], preferred_element_type=F32)

    @pl.when(z < last)
    def _():
        for q in range(PIECES):
            ret_wait(1, z, q)
        own_part[...] += rcv[1, z].astype(F32)

    @pl.when(z > 0)
    def _():
        for q in range(PIECES):
            ret_wait(0, z, q)
        own_part[...] += rcv[0, z].astype(F32)

    out_ref[...] = own_part[...].astype(BF16)
    for i in range(3):
        out_copy(i).wait()

    chain_drain(meta, zm_s, zm_r)
    chain_drain(xg, zx_s, zx_r)
    chain_drain(gg, zg_s, zg_r)
    plane_drain(st_x, rows, px_s, px_r)
    plane_drain(st_g, scaled, pg_s, pg_r)
    plane_drain(sg, ret, pr_s, pr_r)
    for p in range(planes):
        @pl.when(p < z)
        def _(p=p):
            for q in range(PIECES):
                ret_copy(1, p, q).wait_send()

        @pl.when(p > z)
        def _(p=p):
            for q in range(PIECES):
                ret_copy(0, p, q).wait_send()


def chained(inputs, out_grad, expert_ids, gates, gate_w, up_w, down_w):
    tok, feat = inputs.shape
    half, hidden_n = gate_w.shape[1], gate_w.shape[2]
    experts = lax.axis_size("expert")
    planes = experts // COLS
    cap = 2 * tok * expert_ids.shape[1] // experts
    slots = COLS * cap
    total = planes * slots
    dma = pltpu.SemaphoreType.DMA
    vmem = pl.BlockSpec(memory_space=pltpu.VMEM)
    hbm = pl.BlockSpec(memory_space=pl.ANY)
    block = (planes, slots, feat)
    act = (planes, slots, hidden_n)
    scratch = [
        pltpu.VMEM((planes, tok, feat), BF16), pltpu.VMEM((planes, tok, feat), BF16),
        pltpu.VMEM((planes, 8, tok), F32),
        pltpu.VMEM(block, BF16), pltpu.VMEM(block, BF16), pltpu.VMEM(block, BF16), pltpu.VMEM(block, BF16),
        pltpu.VMEM((planes, tok, slots), BF16),
        pltpu.VMEM((feat, hidden_n), BF16), pltpu.VMEM((feat, hidden_n), BF16), pltpu.VMEM((hidden_n, feat), BF16),
        pltpu.VMEM(act, F32), pltpu.VMEM(act, F32),
        pltpu.VMEM((2,) + act, BF16), pltpu.VMEM((2,) + act, BF16), pltpu.VMEM((2,) + act, BF16),
        pltpu.VMEM((2, planes, slots, half), BF16), pltpu.VMEM((2, planes, slots, half), BF16),
        pltpu.VMEM(block, BF16), pltpu.VMEM(block, BF16),
        pltpu.VMEM((2, planes, tok, feat), BF16), pltpu.VMEM((planes, tok, feat), BF16),
        pltpu.VMEM((tok, feat), F32),
        pltpu.VMEM(gate_w.shape, BF16), pltpu.VMEM(up_w.shape, BF16), pltpu.VMEM(down_w.shape, BF16),
        dma((5,)), dma((3,)), dma((3,)),
        dma((2, planes - 1)), dma((2, planes - 1)), dma((2, planes - 1)), dma((2, planes - 1)),
        dma((2, planes - 1)), dma((2, planes - 1)),
        dma((planes, COLS - 1)), dma((planes, COLS - 1)), dma((planes, COLS - 1)), dma((planes, COLS - 1)),
        dma((planes, COLS - 1)), dma((planes, COLS - 1)),
        dma((planes, PIECES)), dma((2, planes, PIECES)), dma((5, planes)), dma((5, planes)), dma((2, planes)), dma((3,)),
    ]
    return pl.pallas_call(
        functools.partial(layer_kernel, planes, experts, cap),
        out_shape=(
            jax.ShapeDtypeStruct((tok, feat), BF16),
            jax.ShapeDtypeStruct(gate_w.shape, BF16),
            jax.ShapeDtypeStruct(up_w.shape, BF16),
            jax.ShapeDtypeStruct(down_w.shape, BF16),
        ),
        in_specs=[vmem, vmem] + [hbm] * 5,
        out_specs=(vmem, hbm, hbm, hbm),
        scratch_shapes=scratch,
        compiler_params=pltpu.CompilerParams(
            collective_id=0, has_side_effects=True, vmem_limit_bytes=60 * 1024 * 1024
        ),
        cost_estimate=pl.CostEstimate(
            flops=18 * total * feat * hidden_n, bytes_accessed=8 * feat * hidden_n, transcendentals=total * hidden_n
        ),
    )(expert_ids.T, gates.T, inputs, out_grad, gate_w, up_w, down_w)


def arrange(received, owners, local_exp, capacity):
    feature_n = received.shape[1]
    shaped = received.reshape(owners, local_exp, capacity, feature_n)
    return shaped.transpose(1, 0, 2, 3).reshape(local_exp, owners * capacity, feature_n)


def restore(slot_rows, owners, capacity):
    local_exp = slot_rows.shape[0]
    feature_n = slot_rows.shape[2]
    shaped = slot_rows.reshape(local_exp, owners, capacity, feature_n)
    return shaped.transpose(1, 0, 2, 3).reshape(owners * local_exp * capacity, feature_n)


def local(inputs, out_grad, expert_ids, gates, gate_w, up_w, down_w):
    if lax.axis_size("expert") <= 16:
        return chained(inputs, out_grad, expert_ids, gates, gate_w, up_w, down_w)
    tok_dev = inputs.shape[0]
    feature_n = inputs.shape[1]
    topk_n = expert_ids.shape[1]
    local_exp = gate_w.shape[0]
    owners = lax.axis_size("expert")
    expert_total = local_exp * owners
    capacity = 2 * tok_dev * topk_n // expert_total
    pair_count = tok_dev * topk_n
    slot_total = expert_total * capacity
    flat_ids = expert_ids.reshape(pair_count)
    one_hot = (flat_ids[:, None] == jnp.arange(expert_total, dtype=jnp.int32)[None, :]).astype(
        jnp.int32
    )
    rank_index = (
        jnp.sum(jnp.cumsum(one_hot, axis=0, dtype=jnp.int32) * one_hot, axis=1, dtype=jnp.int32) - 1
    )
    slot_index = flat_ids * capacity + rank_index
    input_pairs = jnp.repeat(inputs, topk_n, axis=0)
    scaled_pairs = (
        gates.reshape(pair_count, 1) * jnp.repeat(out_grad, topk_n, axis=0).astype(jnp.float32)
    ).astype(jnp.bfloat16)
    send_inputs = jnp.zeros((slot_total, feature_n), jnp.bfloat16).at[slot_index].set(input_pairs)
    send_grads = jnp.zeros((slot_total, feature_n), jnp.bfloat16).at[slot_index].set(scaled_pairs)
    full_gate, full_up, full_down = (
        lax.all_gather(gate_w, "rep", axis=1, tiled=True),
        lax.all_gather(up_w, "rep", axis=1, tiled=True),
        lax.all_gather(down_w, "rep", axis=2, tiled=True),
    )
    recv_inputs, recv_grads = (
        lax.all_to_all(send_inputs, "expert", split_axis=0, concat_axis=0, tiled=True),
        lax.all_to_all(send_grads, "expert", split_axis=0, concat_axis=0, tiled=True),
    )
    rows_in = arrange(recv_inputs, owners, local_exp, capacity)
    scaled_rows = arrange(recv_grads, owners, local_exp, capacity)
    gate_act = jnp.einsum("erd,edh->erh", rows_in, full_gate, preferred_element_type=jnp.float32)
    up_act = jnp.einsum("erd,edh->erh", rows_in, full_up, preferred_element_type=jnp.float32)
    gate_act, up_act = (gate_act, up_act)
    sigma = jax.nn.sigmoid(gate_act)
    silu_val = gate_act * sigma
    hidden = (silu_val * up_act).astype(jnp.bfloat16)
    hidden_grad = jnp.einsum(
        "erd,ehd->erh", scaled_rows, full_down, preferred_element_type=jnp.float32
    )
    gate_grad = (hidden_grad * up_act * sigma * (1.0 + gate_act * (1.0 - sigma))).astype(
        jnp.bfloat16
    )
    up_grad = (hidden_grad * silu_val).astype(jnp.bfloat16)
    first = jnp.einsum("erh,edh->erd", gate_grad, full_gate, preferred_element_type=jnp.float32)
    slot_grad = (
        first + jnp.einsum("erh,edh->erd", up_grad, full_up, preferred_element_type=jnp.float32)
    ).astype(jnp.bfloat16)
    returned = lax.all_to_all(
        restore(slot_grad, owners, capacity), "expert", split_axis=0, concat_axis=0, tiled=True
    )
    gate_part = jnp.einsum("erd,erh->edh", rows_in, gate_grad, preferred_element_type=jnp.float32)
    up_part = jnp.einsum("erd,erh->edh", rows_in, up_grad, preferred_element_type=jnp.float32)
    down_part = jnp.einsum("erh,erd->ehd", hidden, scaled_rows, preferred_element_type=jnp.float32)
    gate_sum, up_sum, down_sum = (
        lax.psum_scatter(
            gate_part.astype(jnp.bfloat16), "rep", scatter_dimension=1, tiled=True
        ).astype(jnp.float32),
        lax.psum_scatter(
            up_part.astype(jnp.bfloat16), "rep", scatter_dimension=1, tiled=True
        ).astype(jnp.float32),
        lax.psum_scatter(
            down_part.astype(jnp.bfloat16), "rep", scatter_dimension=2, tiled=True
        ).astype(jnp.float32),
    )
    picked = returned[slot_index]
    input_grad = jnp.sum(
        picked.reshape(tok_dev, topk_n, feature_n).astype(jnp.float32), axis=1
    ).astype(jnp.bfloat16)
    return (
        input_grad,
        gate_sum.astype(jnp.bfloat16),
        up_sum.astype(jnp.bfloat16),
        down_sum.astype(jnp.bfloat16),
    )


def solution(mesh):
    return jax.shard_map(
        local,
        mesh=mesh,
        in_specs=(
            P(("expert", "rep"), None),
            P(("expert", "rep"), None),
            P(("expert", "rep"), None),
            P(("expert", "rep"), None),
            P("expert", "rep", None),
            P("expert", "rep", None),
            P("expert", None, "rep"),
        ),
        out_specs=(
            P(("expert", "rep"), None),
            P("expert", "rep", None),
            P("expert", "rep", None),
            P("expert", None, "rep"),
        ),
        check_vma=False,
    )
```

```python
import functools

import jax
import jax.numpy as jnp
from jax import lax
from jax.experimental import pallas as pl
from jax.experimental.pallas import tpu as pltpu
from jax.sharding import PartitionSpec as P

MESH = pl.DeviceIdType.MESH
COLS = 4
PIECES = 4
F32 = jnp.float32
BF16 = jnp.bfloat16
NT = (((1,), (1,)), ((), ()))
TN = (((0,), (0,)), ((), ()))


def layer_kernel(
    planes, experts, cap,
    ids_ref, gates_ref, x_hbm, g_hbm, gw_hbm, uw_hbm, dw_hbm,
    out_ref, gwo_ref, uwo_ref, dwo_ref,
    xg, gg, meta, st_x, st_g, rows, scaled, sel_t, wg, wu, wd, ga, ua,
    hid, gate_gr, up_gr, rows_h, scaled_h, sg, ret, rcv, snd,
    own_part, gwo_v, uwo_v, dwo_v,
    load_sem, w_send, w_recv, zm_s, zm_r, zx_s, zx_r, zg_s, zg_r,
    px_s, px_r, pg_s, pg_r, pr_s, pr_r, zr_s, zr_r, rep_s, rep_r, loc_sem, out_sem,
):
    e, r = lax.axis_index("expert"), lax.axis_index("rep")
    z, c = e // COLS, e % COLS
    other = 1 - r
    tok = x_hbm.shape[0]
    last = planes - 1
    slots = COLS * cap
    half = gw_hbm.shape[1]
    feat = x_hbm.shape[1]
    hidden_n = gw_hbm.shape[2]
    total = planes * slots

    def al(v, m):
        return pl.multiple_of(v, m)

    w_at = [
        (gw_hbm.at[0], wg.at[pl.ds(al(r * half, half), half)]),
        (uw_hbm.at[0], wu.at[pl.ds(al(r * half, half), half)]),
        (dw_hbm.at[0], wd.at[:, pl.ds(al(r * half, half), half)]),
    ]
    load_x = pltpu.make_async_copy(x_hbm, xg.at[z], load_sem.at[0])
    load_g = pltpu.make_async_copy(g_hbm, gg.at[z], load_sem.at[1])
    load_x.start()
    load_g.start()
    load_w = [pltpu.make_async_copy(s, d, load_sem.at[2 + i]) for i, (s, d) in enumerate(w_at)]
    for cp in load_w:
        cp.start()

    barrier = pltpu.get_barrier_semaphore()
    for j in range(1, COLS):
        pl.semaphore_signal(barrier, inc=1, device_id=(z * COLS + (c + j) % COLS, r), device_id_type=MESH)
    pl.semaphore_signal(barrier, inc=1, device_id=(e, other), device_id_type=MESH)

    @pl.when(z < last)
    def _():
        pl.semaphore_signal(barrier, inc=1, device_id=(e + COLS, r), device_id_type=MESH)

    @pl.when(z > 0)
    def _():
        pl.semaphore_signal(barrier, inc=1, device_id=(e - COLS, r), device_id_type=MESH)

    id0, id1 = ids_ref[0:1, :], ids_ref[1:2, :]
    exp_iota = lax.broadcasted_iota(jnp.int32, (experts, tok), 0)
    one0 = jnp.where(exp_iota == id0, 1.0, 0.0)
    one1 = jnp.where(exp_iota == id1, 1.0, 0.0)
    before = jnp.where(
        lax.broadcasted_iota(jnp.int32, (tok, tok), 0) < lax.broadcasted_iota(jnp.int32, (tok, tok), 1), 1.0, 0.0
    ).astype(BF16)
    rank = jnp.dot((one0 + one1).astype(BF16), before, preferred_element_type=F32)
    slot0 = jnp.sum(rank * one0, axis=0, keepdims=True) + id0.astype(F32) * cap
    slot1 = jnp.sum(rank * one1, axis=0, keepdims=True) + id1.astype(F32) * cap
    meta[z] = jnp.concatenate(
        [slot0, slot1, gates_ref[0:1, :], gates_ref[1:2, :], jnp.zeros((4, tok), F32)], axis=0
    )
    neighbours = COLS + jnp.where(z < last, 1, 0) + jnp.where(z > 0, 1, 0)
    pl.semaphore_wait(barrier, neighbours)

    def up(buf, ss, rs, k):
        return pltpu.make_async_remote_copy(
            src_ref=buf.at[jnp.maximum(z - k, 0)], dst_ref=buf.at[jnp.maximum(z - k, 0)],
            send_sem=ss.at[0, k], recv_sem=rs.at[0, k], device_id=(e + COLS, r), device_id_type=MESH)

    def down(buf, ss, rs, k):
        return pltpu.make_async_remote_copy(
            src_ref=buf.at[jnp.minimum(z + k, last)], dst_ref=buf.at[jnp.minimum(z + k, last)],
            send_sem=ss.at[1, k], recv_sem=rs.at[1, k], device_id=(e - COLS, r), device_id_type=MESH)

    def can_up(k):
        return (z < last) & (z - k >= 0)

    def can_down(k):
        return (z > 0) & (z + k <= last)

    def chain_start(buf, ss, rs, k):
        @pl.when(can_up(k))
        def _():
            up(buf, ss, rs, k).start()

        @pl.when(can_down(k))
        def _():
            down(buf, ss, rs, k).start()

    def chain_wait(buf, ss, rs, k):
        @pl.when(z - 1 - k >= 0)
        def _():
            b = buf.at[jnp.maximum(z - 1 - k, 0)]
            pltpu.make_async_remote_copy(
                src_ref=b, dst_ref=b, send_sem=ss.at[0, k], recv_sem=rs.at[0, k],
                device_id=(e, other), device_id_type=MESH).wait_recv()

        @pl.when(z + 1 + k <= last)
        def _():
            b = buf.at[jnp.minimum(z + 1 + k, last)]
            pltpu.make_async_remote_copy(
                src_ref=b, dst_ref=b, send_sem=ss.at[1, k], recv_sem=rs.at[1, k],
                device_id=(e, other), device_id_type=MESH).wait_recv()

    def chain_drain(buf, ss, rs):
        for k in range(planes - 1):
            @pl.when(can_up(k))
            def _(k=k):
                up(buf, ss, rs, k).wait_send()

            @pl.when(can_down(k))
            def _(k=k):
                down(buf, ss, rs, k).wait_send()

    def plane_copy(st, dst, ss, rs, p, j):
        d = (c + j) % COLS
        return pltpu.make_async_remote_copy(
            src_ref=st.at[p, pl.ds(al(d * cap, cap), cap)],
            dst_ref=dst.at[p, pl.ds(al(c * cap, cap), cap)],
            send_sem=ss.at[p, j - 1], recv_sem=rs.at[p, j - 1],
            device_id=(z * COLS + d, r), device_id_type=MESH)

    def plane_send(st, dst, ss, rs, p):
        for j in range(1, COLS):
            plane_copy(st, dst, ss, rs, p, j).start()
        dst[p, pl.ds(al(c * cap, cap), cap), :] = st[p, pl.ds(al(c * cap, cap), cap), :]

    def plane_wait(st, dst, ss, rs, p):
        for j in range(1, COLS):
            plane_copy(st, dst, ss, rs, p, j).wait_recv()

    def plane_drain(st, dst, ss, rs):
        for p in range(planes):
            for j in range(1, COLS):
                plane_copy(st, dst, ss, rs, p, j).wait_send()

    def selection(p):
        m = meta[p]
        place = (lax.broadcasted_iota(jnp.int32, (slots, tok), 0) + z * slots).astype(F32)
        return jnp.where(place == m[0:1, :], 1.0, 0.0), jnp.where(place == m[1:2, :], 1.0, 0.0), m

    def dispatch_x(p):
        s0, s1, _ = selection(p)
        pick = s0 + s1
        sel_t[p] = pick.T.astype(BF16)
        st_x[p] = jnp.dot(pick.astype(BF16), xg[p], preferred_element_type=F32).astype(BF16)
        plane_send(st_x, rows, px_s, px_r, p)

    def dispatch_g(p):
        s0, s1, m = selection(p)
        gate = jnp.sum(s0 * m[2:3, :] + s1 * m[3:4, :], axis=1, keepdims=True)
        picked = jnp.dot((s0 + s1).astype(BF16), gg[p], preferred_element_type=F32)
        st_g[p] = (picked * gate).astype(BF16)
        plane_send(st_g, scaled, pg_s, pg_r, p)

    def both(fn, k):
        @pl.when(z - 1 - k >= 0)
        def _():
            fn(jnp.maximum(z - 1 - k, 0))

        @pl.when(z + 1 + k <= last)
        def _():
            fn(jnp.minimum(z + 1 + k, last))

    def w_copy(i):
        s, d = w_at[i]
        return pltpu.make_async_remote_copy(
            src_ref=s, dst_ref=d, send_sem=w_send.at[i], recv_sem=w_recv.at[i],
            device_id=(e, other), device_id_type=MESH)

    def halves(src, dst, i, p):
        lo = pl.ds(al(r * half, half), half)
        hi = pl.ds(al(other * half, half), half)
        return (
            pltpu.make_async_copy(src.at[p, :, lo], dst.at[r, p], loc_sem.at[i, p]),
            pltpu.make_async_remote_copy(
                src_ref=src.at[p, :, hi], dst_ref=dst.at[r, p], send_sem=rep_s.at[i, p], recv_sem=rep_r.at[i, p],
                device_id=(e, other), device_id_type=MESH),
        )

    def rep_copy(ref, i, p):
        return pltpu.make_async_remote_copy(
            src_ref=ref.at[r, p], dst_ref=ref.at[r, p], send_sem=rep_s.at[i, p], recv_sem=rep_r.at[i, p],
            device_id=(e, other), device_id_type=MESH)

    step_h = 256 if hidden_n % 256 == 0 else hidden_n
    step_d = 512

    def acts(p):
        plane_wait(st_x, rows, px_s, px_r, p)
        for cp in halves(rows, rows_h, 0, p):
            cp.start()

        @pl.loop(0, hidden_n // step_h)
        def _(i):
            cols = pl.ds(al(i * step_h, step_h), step_h)
            ga[p, :, cols] = jnp.dot(rows[p], wg[:, cols], preferred_element_type=F32)
            ua[p, :, cols] = jnp.dot(rows[p], wu[:, cols], preferred_element_type=F32)

    def grads(p):
        plane_wait(st_g, scaled, pg_s, pg_r, p)
        for cp in halves(scaled, scaled_h, 1, p):
            cp.start()

        @pl.loop(0, hidden_n // step_h)
        def _(i):
            cols = pl.ds(al(i * step_h, step_h), step_h)
            hg = lax.dot_general(scaled[p], wd[cols, :], NT, preferred_element_type=F32)
            gate_act, up_act = ga[p, :, cols], ua[p, :, cols]
            sigma = jax.nn.sigmoid(gate_act)
            silu = gate_act * sigma
            hid[r, p, :, cols] = (silu * up_act).astype(BF16)
            gate_gr[r, p, :, cols] = (hg * up_act * sigma * (1.0 + gate_act * (1.0 - sigma))).astype(BF16)
            up_gr[r, p, :, cols] = (hg * silu).astype(BF16)

        @pl.loop(0, feat // step_d)
        def _(i):
            cols = pl.ds(al(i * step_d, step_d), step_d)
            v = lax.dot_general(gate_gr[r, p], wg[cols, :], NT, preferred_element_type=F32)
            v = v + lax.dot_general(up_gr[r, p], wu[cols, :], NT, preferred_element_type=F32)
            sg[p, :, cols] = v.astype(BF16)

        plane_send(sg, ret, pr_s, pr_r, p)
        for i, ref in enumerate((gate_gr, up_gr, hid)):
            rep_copy(ref, 2 + i, p).start()

    piece = tok // PIECES

    def ret_copy(way, p, q):
        at = pl.ds(q * piece, piece)
        return pltpu.make_async_remote_copy(
            src_ref=snd.at[p, at], dst_ref=rcv.at[way, p, at], send_sem=zr_s.at[p, q], recv_sem=zr_r.at[way, p, q],
            device_id=(jnp.where(way == 0, e + COLS, e - COLS), r), device_id_type=MESH)

    def ret_wait(way, p, q):
        at = pl.ds(q * piece, piece)
        pltpu.make_async_remote_copy(
            src_ref=snd.at[p, at], dst_ref=rcv.at[way, p, at], send_sem=zr_s.at[p, q], recv_sem=zr_r.at[way, p, q],
            device_id=(e, other), device_id_type=MESH).wait_recv()

    def forward(way, p, first):
        plane_wait(sg, ret, pr_s, pr_r, p)
        own_part[...] = jnp.dot(sel_t[p], ret[p], preferred_element_type=F32)
        for q in range(PIECES):
            at = pl.ds(q * piece, piece)

            @pl.when(first)
            def _():
                snd[p, at, :] = own_part[at, :].astype(BF16)

            @pl.when(jnp.logical_not(first))
            def _():
                ret_wait(way, p, q)
                snd[p, at, :] = (own_part[at, :] + rcv[way, p, at, :].astype(F32)).astype(BF16)

            ret_copy(way, p, q).start()

    def forward_both(k):
        @pl.loop(0, 2)
        def _(side):
            way = jnp.where(z >= planes // 2, 1 - side, side)
            p = jnp.where(way == 1, last - 1 - k, k + 1)

            @pl.when(((way == 1) & (p < z)) | ((way == 0) & (p > z)))
            def _():
                forward(way, p, ((way == 1) & (z == last)) | ((way == 0) & (z == 0)))

    def weight_in(a_half, grad, out):
        step = 256

        @pl.loop(0, half // step)
        def _(i):
            cols = pl.ds(al(i * step, step), step)
            v = 0.0
            for rep in range(2):
                v = v + lax.dot_general(
                    a_half[rep, :, :, cols].reshape(total, step), grad[rep].reshape(total, hidden_n), TN,
                    preferred_element_type=F32)
            out[0, cols, :] = v.astype(BF16)

    def weight_down():
        @pl.loop(0, hidden_n // step_h)
        def _(i):
            cols = pl.ds(al(i * step_h, step_h), step_h)
            v = 0.0
            for rep in range(2):
                v = v + lax.dot_general(
                    hid[rep, :, :, cols].reshape(total, step_h), scaled_h[rep].reshape(total, half), TN,
                    preferred_element_type=F32)
            dwo_v[0, cols, :] = v.astype(BF16)

    def out_copy(i):
        src, dst = ((gwo_v, gwo_ref), (uwo_v, uwo_ref), (dwo_v, dwo_ref))[i]
        return pltpu.make_async_copy(src, dst, out_sem.at[i])

    chain_start(meta, zm_s, zm_r, 0)
    load_x.wait()
    chain_start(xg, zx_s, zx_r, 0)
    load_g.wait()
    chain_start(gg, zg_s, zg_r, 0)
    for i in range(3):
        w_copy(i).start()
    dispatch_x(z)
    dispatch_g(z)
    for cp in load_w:
        cp.wait()
    for i in range(3):
        w_copy(i).wait()
    acts(z)
    for k in range(planes - 1):
        chain_wait(meta, zm_s, zm_r, k)
        chain_wait(xg, zx_s, zx_r, k)
        if k < planes - 2:
            chain_start(meta, zm_s, zm_r, k + 1)
            chain_start(xg, zx_s, zx_r, k + 1)
        both(dispatch_x, k)
        if k == 0:
            grads(z)
        else:
            both(grads, k - 1)
        chain_wait(gg, zg_s, zg_r, k)
        if k < planes - 2:
            chain_start(gg, zg_s, zg_r, k + 1)
        both(dispatch_g, k)
        both(acts, k)
        if k > 0:
            forward_both(k - 1)
    both(grads, planes - 2)

    is_end = jnp.where((z == 0) | (z == last), 1, 0)

    @pl.loop(0, 2)
    def _(phase):
        @pl.when(phase == is_end)
        def _():
            for p in range(planes):
                for i, (src, dst) in enumerate(((rows, rows_h), (scaled, scaled_h))):
                    for cp in halves(src, dst, i, p):
                        cp.wait()
                for i, ref in enumerate((gate_gr, up_gr, hid)):
                    rep_copy(ref, 2 + i, p).wait()
            weight_in(rows_h, gate_gr, gwo_v)
            out_copy(0).start()
            weight_in(rows_h, up_gr, uwo_v)
            out_copy(1).start()
            weight_down()
            out_copy(2).start()

        @pl.when(phase == 0)
        def _():
            forward_both(planes - 2)

    plane_wait(sg, ret, pr_s, pr_r, z)
    own_part[...] = jnp.dot(sel_t[z], ret[z], preferred_element_type=F32)

    @pl.when(z < last)
    def _():
        for q in range(PIECES):
            ret_wait(1, z, q)
        own_part[...] += rcv[1, z].astype(F32)

    @pl.when(z > 0)
    def _():
        for q in range(PIECES):
            ret_wait(0, z, q)
        own_part[...] += rcv[0, z].astype(F32)

    out_ref[...] = own_part[...].astype(BF16)
    for i in range(3):
        out_copy(i).wait()

    chain_drain(meta, zm_s, zm_r)
    chain_drain(xg, zx_s, zx_r)
    chain_drain(gg, zg_s, zg_r)
    plane_drain(st_x, rows, px_s, px_r)
    plane_drain(st_g, scaled, pg_s, pg_r)
    plane_drain(sg, ret, pr_s, pr_r)
    for p in range(planes):
        @pl.when(p < z)
        def _(p=p):
            for q in range(PIECES):
                ret_copy(1, p, q).wait_send()

        @pl.when(p > z)
        def _(p=p):
            for q in range(PIECES):
                ret_copy(0, p, q).wait_send()


def hand_over(*refs):
    count = len(refs) // 2
    srcs, dsts, sem = refs[:count], refs[count : 2 * count], refs[2 * count]
    copies = []
    for i in range(count):
        axis = len(srcs[i].shape) - 2
        piece = srcs[i].shape[axis] // PIECES
        for q in range(PIECES):
            at = (0,) * axis + (pl.ds(q * piece, piece),)
            copies.append(pltpu.make_async_copy(srcs[i].at[at], dsts[i].at[at], sem.at[i, q]))
    for cp in copies:
        cp.start()
    for cp in copies:
        cp.wait()


def chained(inputs, out_grad, expert_ids, gates, gate_w, up_w, down_w):
    tok, feat = inputs.shape
    half, hidden_n = gate_w.shape[1], gate_w.shape[2]
    experts = lax.axis_size("expert")
    planes = experts // COLS
    cap = 2 * tok * expert_ids.shape[1] // experts
    slots = COLS * cap
    total = planes * slots
    dma = pltpu.SemaphoreType.DMA
    vmem = pl.BlockSpec(memory_space=pltpu.VMEM)
    hbm = pl.BlockSpec(memory_space=pl.ANY)
    block = (planes, slots, feat)
    act = (planes, slots, hidden_n)
    scratch = [
        pltpu.VMEM((planes, tok, feat), BF16), pltpu.VMEM((planes, tok, feat), BF16),
        pltpu.VMEM((planes, 8, tok), F32),
        pltpu.VMEM(block, BF16), pltpu.VMEM(block, BF16), pltpu.VMEM(block, BF16), pltpu.VMEM(block, BF16),
        pltpu.VMEM((planes, tok, slots), BF16),
        pltpu.VMEM((feat, hidden_n), BF16), pltpu.VMEM((feat, hidden_n), BF16), pltpu.VMEM((hidden_n, feat), BF16),
        pltpu.VMEM(act, F32), pltpu.VMEM(act, F32),
        pltpu.VMEM((2,) + act, BF16), pltpu.VMEM((2,) + act, BF16), pltpu.VMEM((2,) + act, BF16),
        pltpu.VMEM((2, planes, slots, half), BF16), pltpu.VMEM((2, planes, slots, half), BF16),
        pltpu.VMEM(block, BF16), pltpu.VMEM(block, BF16),
        pltpu.VMEM((2, planes, tok, feat), BF16), pltpu.VMEM((planes, tok, feat), BF16),
        pltpu.VMEM((tok, feat), F32),
        pltpu.VMEM(gate_w.shape, BF16), pltpu.VMEM(up_w.shape, BF16), pltpu.VMEM(down_w.shape, BF16),
        dma((5,)), dma((3,)), dma((3,)),
        dma((2, planes - 1)), dma((2, planes - 1)), dma((2, planes - 1)), dma((2, planes - 1)),
        dma((2, planes - 1)), dma((2, planes - 1)),
        dma((planes, COLS - 1)), dma((planes, COLS - 1)), dma((planes, COLS - 1)), dma((planes, COLS - 1)),
        dma((planes, COLS - 1)), dma((planes, COLS - 1)),
        dma((planes, PIECES)), dma((2, planes, PIECES)), dma((5, planes)), dma((5, planes)), dma((2, planes)), dma((3,)),
    ]
    results = pl.pallas_call(
        functools.partial(layer_kernel, planes, experts, cap),
        out_shape=(
            jax.ShapeDtypeStruct((tok, feat), BF16),
            jax.ShapeDtypeStruct(gate_w.shape, BF16),
            jax.ShapeDtypeStruct(up_w.shape, BF16),
            jax.ShapeDtypeStruct(down_w.shape, BF16),
        ),
        in_specs=[vmem, vmem] + [hbm] * 5,
        out_specs=(vmem, hbm, hbm, hbm),
        scratch_shapes=scratch,
        compiler_params=pltpu.CompilerParams(
            collective_id=0, has_side_effects=True, vmem_limit_bytes=60 * 1024 * 1024
        ),
        cost_estimate=pl.CostEstimate(
            flops=18 * total * feat * hidden_n, bytes_accessed=8 * feat * hidden_n, transcendentals=total * hidden_n
        ),
    )(expert_ids.T, gates.T, inputs, out_grad, gate_w, up_w, down_w)
    return pl.pallas_call(
        hand_over,
        out_shape=tuple(jax.ShapeDtypeStruct(a.shape, a.dtype) for a in results),
        in_specs=[hbm] * 4,
        out_specs=(hbm,) * 4,
        scratch_shapes=[dma((4, PIECES))],
    )(*results)


def arrange(received, owners, local_exp, capacity):
    feature_n = received.shape[1]
    shaped = received.reshape(owners, local_exp, capacity, feature_n)
    return shaped.transpose(1, 0, 2, 3).reshape(local_exp, owners * capacity, feature_n)


def restore(slot_rows, owners, capacity):
    local_exp = slot_rows.shape[0]
    feature_n = slot_rows.shape[2]
    shaped = slot_rows.reshape(local_exp, owners, capacity, feature_n)
    return shaped.transpose(1, 0, 2, 3).reshape(owners * local_exp * capacity, feature_n)


def local(inputs, out_grad, expert_ids, gates, gate_w, up_w, down_w):
    if lax.axis_size("expert") <= 16:
        return chained(inputs, out_grad, expert_ids, gates, gate_w, up_w, down_w)
    tok_dev = inputs.shape[0]
    feature_n = inputs.shape[1]
    topk_n = expert_ids.shape[1]
    local_exp = gate_w.shape[0]
    owners = lax.axis_size("expert")
    expert_total = local_exp * owners
    capacity = 2 * tok_dev * topk_n // expert_total
    pair_count = tok_dev * topk_n
    slot_total = expert_total * capacity
    flat_ids = expert_ids.reshape(pair_count)
    one_hot = (flat_ids[:, None] == jnp.arange(expert_total, dtype=jnp.int32)[None, :]).astype(
        jnp.int32
    )
    rank_index = (
        jnp.sum(jnp.cumsum(one_hot, axis=0, dtype=jnp.int32) * one_hot, axis=1, dtype=jnp.int32) - 1
    )
    slot_index = flat_ids * capacity + rank_index
    input_pairs = jnp.repeat(inputs, topk_n, axis=0)
    scaled_pairs = (
        gates.reshape(pair_count, 1) * jnp.repeat(out_grad, topk_n, axis=0).astype(jnp.float32)
    ).astype(jnp.bfloat16)
    send_inputs = jnp.zeros((slot_total, feature_n), jnp.bfloat16).at[slot_index].set(input_pairs)
    send_grads = jnp.zeros((slot_total, feature_n), jnp.bfloat16).at[slot_index].set(scaled_pairs)
    full_gate, full_up, full_down = (
        lax.all_gather(gate_w, "rep", axis=1, tiled=True),
        lax.all_gather(up_w, "rep", axis=1, tiled=True),
        lax.all_gather(down_w, "rep", axis=2, tiled=True),
    )
    recv_inputs, recv_grads = (
        lax.all_to_all(send_inputs, "expert", split_axis=0, concat_axis=0, tiled=True),
        lax.all_to_all(send_grads, "expert", split_axis=0, concat_axis=0, tiled=True),
    )
    rows_in = arrange(recv_inputs, owners, local_exp, capacity)
    scaled_rows = arrange(recv_grads, owners, local_exp, capacity)
    gate_act = jnp.einsum("erd,edh->erh", rows_in, full_gate, preferred_element_type=jnp.float32)
    up_act = jnp.einsum("erd,edh->erh", rows_in, full_up, preferred_element_type=jnp.float32)
    gate_act, up_act = (gate_act, up_act)
    sigma = jax.nn.sigmoid(gate_act)
    silu_val = gate_act * sigma
    hidden = (silu_val * up_act).astype(jnp.bfloat16)
    hidden_grad = jnp.einsum(
        "erd,ehd->erh", scaled_rows, full_down, preferred_element_type=jnp.float32
    )
    gate_grad = (hidden_grad * up_act * sigma * (1.0 + gate_act * (1.0 - sigma))).astype(
        jnp.bfloat16
    )
    up_grad = (hidden_grad * silu_val).astype(jnp.bfloat16)
    first = jnp.einsum("erh,edh->erd", gate_grad, full_gate, preferred_element_type=jnp.float32)
    slot_grad = (
        first + jnp.einsum("erh,edh->erd", up_grad, full_up, preferred_element_type=jnp.float32)
    ).astype(jnp.bfloat16)
    returned = lax.all_to_all(
        restore(slot_grad, owners, capacity), "expert", split_axis=0, concat_axis=0, tiled=True
    )
    gate_part = jnp.einsum("erd,erh->edh", rows_in, gate_grad, preferred_element_type=jnp.float32)
    up_part = jnp.einsum("erd,erh->edh", rows_in, up_grad, preferred_element_type=jnp.float32)
    down_part = jnp.einsum("erh,erd->ehd", hidden, scaled_rows, preferred_element_type=jnp.float32)
    gate_sum, up_sum, down_sum = (
        lax.psum_scatter(
            gate_part.astype(jnp.bfloat16), "rep", scatter_dimension=1, tiled=True
        ).astype(jnp.float32),
        lax.psum_scatter(
            up_part.astype(jnp.bfloat16), "rep", scatter_dimension=1, tiled=True
        ).astype(jnp.float32),
        lax.psum_scatter(
            down_part.astype(jnp.bfloat16), "rep", scatter_dimension=2, tiled=True
        ).astype(jnp.float32),
    )
    picked = returned[slot_index]
    input_grad = jnp.sum(
        picked.reshape(tok_dev, topk_n, feature_n).astype(jnp.float32), axis=1
    ).astype(jnp.bfloat16)
    return (
        input_grad,
        gate_sum.astype(jnp.bfloat16),
        up_sum.astype(jnp.bfloat16),
        down_sum.astype(jnp.bfloat16),
    )


def solution(mesh):
    return jax.shard_map(
        local,
        mesh=mesh,
        in_specs=(
            P(("expert", "rep"), None),
            P(("expert", "rep"), None),
            P(("expert", "rep"), None),
            P(("expert", "rep"), None),
            P("expert", "rep", None),
            P("expert", "rep", None),
            P("expert", None, "rep"),
        ),
        out_specs=(
            P(("expert", "rep"), None),
            P("expert", "rep", None),
            P("expert", "rep", None),
            P("expert", None, "rep"),
        ),
        check_vma=False,
    )
```

```python
import functools

import jax
import jax.numpy as jnp
from jax import lax
from jax.experimental import pallas as pl
from jax.experimental.pallas import tpu as pltpu
from jax.sharding import PartitionSpec as P

MESH = pl.DeviceIdType.MESH
COLS = 4
PIECES = 4
GPARTS = 2
F32 = jnp.float32
BF16 = jnp.bfloat16
NT = (((1,), (1,)), ((), ()))
TN = (((0,), (0,)), ((), ()))


def layer_kernel(
    planes, experts, cap,
    ids_ref, gates_ref, x_hbm, g_hbm, gw_hbm, uw_hbm, dw_hbm,
    out_ref, gwo_ref, uwo_ref, dwo_ref,
    xg, gg, meta, st_x, st_g, rows, scaled, sel_t, wg, wu, wd, ga, ua,
    hid, gate_gr, up_gr, rows_h, scaled_h, sg, ret, rcv, snd,
    own_part, hg_part, gwo_v, uwo_v, dwo_v,
    load_sem, w_send, w_recv, zm_s, zm_r, zx_s, zx_r, zg_s, zg_r,
    px_s, px_r, pg_s, pg_r, pr_s, pr_r, zr_s, zr_r, rep_s, rep_r, loc_sem, out_sem,
):
    e, r = lax.axis_index("expert"), lax.axis_index("rep")
    z, c = e // COLS, e % COLS
    other = 1 - r
    tok = x_hbm.shape[0]
    last = planes - 1
    slots = COLS * cap
    half = gw_hbm.shape[1]
    feat = x_hbm.shape[1]
    hidden_n = gw_hbm.shape[2]
    total = planes * slots

    def al(v, m):
        return pl.multiple_of(v, m)

    w_at = [
        (gw_hbm.at[0], wg.at[pl.ds(al(r * half, half), half)]),
        (uw_hbm.at[0], wu.at[pl.ds(al(r * half, half), half)]),
        (dw_hbm.at[0], wd.at[:, pl.ds(al(r * half, half), half)]),
    ]
    load_x = pltpu.make_async_copy(x_hbm, xg.at[z], load_sem.at[0])
    load_g = pltpu.make_async_copy(g_hbm, gg.at[z], load_sem.at[1])
    load_x.start()
    load_g.start()
    load_w = [pltpu.make_async_copy(s, d, load_sem.at[2 + i]) for i, (s, d) in enumerate(w_at)]
    for cp in load_w:
        cp.start()

    barrier = pltpu.get_barrier_semaphore()
    for j in range(1, COLS):
        pl.semaphore_signal(barrier, inc=1, device_id=(z * COLS + (c + j) % COLS, r), device_id_type=MESH)
    pl.semaphore_signal(barrier, inc=1, device_id=(e, other), device_id_type=MESH)

    @pl.when(z < last)
    def _():
        pl.semaphore_signal(barrier, inc=1, device_id=(e + COLS, r), device_id_type=MESH)

    @pl.when(z > 0)
    def _():
        pl.semaphore_signal(barrier, inc=1, device_id=(e - COLS, r), device_id_type=MESH)

    id0, id1 = ids_ref[0:1, :], ids_ref[1:2, :]
    exp_iota = lax.broadcasted_iota(jnp.int32, (experts, tok), 0)
    one0 = jnp.where(exp_iota == id0, 1.0, 0.0)
    one1 = jnp.where(exp_iota == id1, 1.0, 0.0)
    before = jnp.where(
        lax.broadcasted_iota(jnp.int32, (tok, tok), 0) < lax.broadcasted_iota(jnp.int32, (tok, tok), 1), 1.0, 0.0
    ).astype(BF16)
    rank = jnp.dot((one0 + one1).astype(BF16), before, preferred_element_type=F32)
    slot0 = jnp.sum(rank * one0, axis=0, keepdims=True) + id0.astype(F32) * cap
    slot1 = jnp.sum(rank * one1, axis=0, keepdims=True) + id1.astype(F32) * cap
    meta[z] = jnp.concatenate(
        [slot0, slot1, gates_ref[0:1, :], gates_ref[1:2, :], jnp.zeros((4, tok), F32)], axis=0
    )
    neighbours = COLS + jnp.where(z < last, 1, 0) + jnp.where(z > 0, 1, 0)
    pl.semaphore_wait(barrier, neighbours)

    def span(part):
        wide = feat // GPARTS
        return (slice(None), pl.ds(part * wide, wide))

    def at_part(ref, i, part):
        return ref.at[i] if part is None else ref.at[(i,) + span(part)]

    def at_sem(sem, way, k, part):
        return sem.at[way, k] if part is None else sem.at[way, k, part]

    def chain_copy(buf, ss, rs, way, k, part, i, target):
        return pltpu.make_async_remote_copy(
            src_ref=at_part(buf, i, part), dst_ref=at_part(buf, i, part),
            send_sem=at_sem(ss, way, k, part), recv_sem=at_sem(rs, way, k, part),
            device_id=target, device_id_type=MESH)

    def up(buf, ss, rs, k, part):
        return chain_copy(buf, ss, rs, 0, k, part, jnp.maximum(z - k, 0), (e + COLS, r))

    def down(buf, ss, rs, k, part):
        return chain_copy(buf, ss, rs, 1, k, part, jnp.minimum(z + k, last), (e - COLS, r))

    def can_up(k):
        return (z < last) & (z - k >= 0)

    def can_down(k):
        return (z > 0) & (z + k <= last)

    def chain_start(buf, ss, rs, k, part=None):
        @pl.when(can_up(k))
        def _():
            up(buf, ss, rs, k, part).start()

        @pl.when(can_down(k))
        def _():
            down(buf, ss, rs, k, part).start()

    def chain_wait(buf, ss, rs, k, part=None):
        @pl.when(z - 1 - k >= 0)
        def _():
            chain_copy(buf, ss, rs, 0, k, part, jnp.maximum(z - 1 - k, 0), (e, other)).wait_recv()

        @pl.when(z + 1 + k <= last)
        def _():
            chain_copy(buf, ss, rs, 1, k, part, jnp.minimum(z + 1 + k, last), (e, other)).wait_recv()

    def chain_drain(buf, ss, rs, parts=(None,)):
        for k in range(planes - 1):
            for part in parts:
                @pl.when(can_up(k))
                def _(k=k, part=part):
                    up(buf, ss, rs, k, part).wait_send()

                @pl.when(can_down(k))
                def _(k=k, part=part):
                    down(buf, ss, rs, k, part).wait_send()

    def plane_copy(st, dst, ss, rs, p, j, q, parts):
        d = (c + j) % COLS
        cols = pl.ds(al(q * (feat // parts), feat // parts), feat // parts)
        return pltpu.make_async_remote_copy(
            src_ref=st.at[p, pl.ds(al(d * cap, cap), cap), cols],
            dst_ref=dst.at[p, pl.ds(al(c * cap, cap), cap), cols],
            send_sem=ss.at[p, j - 1, q], recv_sem=rs.at[p, j - 1, q],
            device_id=(z * COLS + d, r), device_id_type=MESH)

    def plane_send(st, dst, ss, rs, p, q=0, parts=1):
        for j in range(1, COLS):
            plane_copy(st, dst, ss, rs, p, j, q, parts).start()
        cols = pl.ds(al(q * (feat // parts), feat // parts), feat // parts)
        dst[p, pl.ds(al(c * cap, cap), cap), cols] = st[p, pl.ds(al(c * cap, cap), cap), cols]

    def plane_wait(st, dst, ss, rs, p, q=0, parts=1):
        for j in range(1, COLS):
            plane_copy(st, dst, ss, rs, p, j, q, parts).wait_recv()

    def plane_drain(st, dst, ss, rs, parts=1):
        for p in range(planes):
            for j in range(1, COLS):
                for q in range(parts):
                    plane_copy(st, dst, ss, rs, p, j, q, parts).wait_send()

    def selection(p):
        m = meta[p]
        place = (lax.broadcasted_iota(jnp.int32, (slots, tok), 0) + z * slots).astype(F32)
        return jnp.where(place == m[0:1, :], 1.0, 0.0), jnp.where(place == m[1:2, :], 1.0, 0.0), m

    def dispatch_x(p):
        s0, s1, _ = selection(p)
        pick = s0 + s1
        sel_t[p] = pick.T.astype(BF16)
        st_x[p] = jnp.dot(pick.astype(BF16), xg[p], preferred_element_type=F32).astype(BF16)
        plane_send(st_x, rows, px_s, px_r, p)

    def dispatch_g(p, part):
        s0, s1, m = selection(p)
        gate = jnp.sum(s0 * m[2:3, :] + s1 * m[3:4, :], axis=1, keepdims=True)
        at = (p,) + span(part)
        picked = jnp.dot((s0 + s1).astype(BF16), gg[at], preferred_element_type=F32)
        st_g[at] = (picked * gate).astype(BF16)
        plane_send(st_g, scaled, pg_s, pg_r, p, part, GPARTS)

    def both(fn, k):
        @pl.when(z - 1 - k >= 0)
        def _():
            fn(jnp.maximum(z - 1 - k, 0))

        @pl.when(z + 1 + k <= last)
        def _():
            fn(jnp.minimum(z + 1 + k, last))

    def w_copy(i):
        s, d = w_at[i]
        return pltpu.make_async_remote_copy(
            src_ref=s, dst_ref=d, send_sem=w_send.at[i], recv_sem=w_recv.at[i],
            device_id=(e, other), device_id_type=MESH)

    def halves(src, dst, i, p):
        lo = pl.ds(al(r * half, half), half)
        hi = pl.ds(al(other * half, half), half)
        return (
            pltpu.make_async_copy(src.at[p, :, lo], dst.at[r, p], loc_sem.at[i, p]),
            pltpu.make_async_remote_copy(
                src_ref=src.at[p, :, hi], dst_ref=dst.at[r, p], send_sem=rep_s.at[i, p], recv_sem=rep_r.at[i, p],
                device_id=(e, other), device_id_type=MESH),
        )

    def rep_copy(ref, i, p):
        return pltpu.make_async_remote_copy(
            src_ref=ref.at[r, p], dst_ref=ref.at[r, p], send_sem=rep_s.at[i, p], recv_sem=rep_r.at[i, p],
            device_id=(e, other), device_id_type=MESH)

    step_h = 256 if hidden_n % 256 == 0 else hidden_n
    step_d = feat // PIECES

    def acts(p):
        plane_wait(st_x, rows, px_s, px_r, p)
        for cp in halves(rows, rows_h, 0, p):
            cp.start()

        @pl.loop(0, hidden_n // step_h)
        def _(i):
            cols = pl.ds(al(i * step_h, step_h), step_h)
            ga[p, :, cols] = jnp.dot(rows[p], wg[:, cols], preferred_element_type=F32)
            ua[p, :, cols] = jnp.dot(rows[p], wu[:, cols], preferred_element_type=F32)

    def grads(p):
        for part in range(GPARTS):
            plane_wait(st_g, scaled, pg_s, pg_r, p, part, GPARTS)
            at = span(part)

            @pl.loop(0, hidden_n // step_h)
            def _(i):
                cols = pl.ds(al(i * step_h, step_h), step_h)
                hg = lax.dot_general(scaled[(p,) + at], wd[cols, at[1]], NT, preferred_element_type=F32)
                if part < GPARTS - 1:
                    hg_part[:, cols] = hg if part == 0 else hg_part[:, cols] + hg
                else:
                    if part > 0:
                        hg = hg + hg_part[:, cols]
                    gate_act, up_act = ga[p, :, cols], ua[p, :, cols]
                    sigma = jax.nn.sigmoid(gate_act)
                    silu = gate_act * sigma
                    hid[r, p, :, cols] = (silu * up_act).astype(BF16)
                    gate_gr[r, p, :, cols] = (hg * up_act * sigma * (1.0 + gate_act * (1.0 - sigma))).astype(BF16)
                    up_gr[r, p, :, cols] = (hg * silu).astype(BF16)

        @pl.loop(0, PIECES)
        def _(i):
            cols = pl.ds(al(i * step_d, step_d), step_d)
            v = lax.dot_general(gate_gr[r, p], wg[cols, :], NT, preferred_element_type=F32)
            v = v + lax.dot_general(up_gr[r, p], wu[cols, :], NT, preferred_element_type=F32)
            sg[p, :, cols] = v.astype(BF16)
            plane_send(sg, ret, pr_s, pr_r, p, i, PIECES)

        for i, ref in enumerate((gate_gr, up_gr, hid)):
            rep_copy(ref, 2 + i, p).start()
        for cp in halves(scaled, scaled_h, 1, p):
            cp.start()

    def piece(q):
        return pl.ds(al(q * step_d, step_d), step_d)

    def ret_copy(way, p, q):
        return pltpu.make_async_remote_copy(
            src_ref=snd.at[p, :, piece(q)], dst_ref=rcv.at[way, p, :, piece(q)],
            send_sem=zr_s.at[p, q], recv_sem=zr_r.at[way, p, q],
            device_id=(jnp.where(way == 0, e + COLS, e - COLS), r), device_id_type=MESH)

    def ret_wait(way, p, q):
        pltpu.make_async_remote_copy(
            src_ref=snd.at[p, :, piece(q)], dst_ref=rcv.at[way, p, :, piece(q)],
            send_sem=zr_s.at[p, q], recv_sem=zr_r.at[way, p, q],
            device_id=(e, other), device_id_type=MESH).wait_recv()

    def own_sum(p, q):
        plane_wait(sg, ret, pr_s, pr_r, p, q, PIECES)
        return jnp.dot(sel_t[p], ret[p, :, piece(q)], preferred_element_type=F32)

    def forward(way, p, first):
        @pl.loop(0, PIECES)
        def _(q):
            own = own_sum(p, q)

            @pl.when(first)
            def _():
                snd[p, :, piece(q)] = own.astype(BF16)

            @pl.when(jnp.logical_not(first))
            def _():
                ret_wait(way, p, q)
                snd[p, :, piece(q)] = (own + rcv[way, p, :, piece(q)].astype(F32)).astype(BF16)

            ret_copy(way, p, q).start()

    def forward_both(k):
        @pl.loop(0, 2)
        def _(side):
            way = jnp.where(z >= planes // 2, 1 - side, side)
            p = jnp.where(way == 1, last - 1 - k, k + 1)

            @pl.when(((way == 1) & (p < z)) | ((way == 0) & (p > z)))
            def _():
                forward(way, p, ((way == 1) & (z == last)) | ((way == 0) & (z == 0)))

    def weight_in(a_half, grad, out):
        step = 256

        @pl.loop(0, half // step)
        def _(i):
            cols = pl.ds(al(i * step, step), step)
            v = 0.0
            for rep in range(2):
                v = v + lax.dot_general(
                    a_half[rep, :, :, cols].reshape(total, step), grad[rep].reshape(total, hidden_n), TN,
                    preferred_element_type=F32)
            out[0, cols, :] = v.astype(BF16)

    def weight_down():
        @pl.loop(0, hidden_n // step_h)
        def _(i):
            cols = pl.ds(al(i * step_h, step_h), step_h)
            v = 0.0
            for rep in range(2):
                v = v + lax.dot_general(
                    hid[rep, :, :, cols].reshape(total, step_h), scaled_h[rep].reshape(total, half), TN,
                    preferred_element_type=F32)
            dwo_v[0, cols, :] = v.astype(BF16)

    def out_copy(i):
        src, dst = ((gwo_v, gwo_ref), (uwo_v, uwo_ref), (dwo_v, dwo_ref))[i]
        return pltpu.make_async_copy(src, dst, out_sem.at[i])

    chain_start(meta, zm_s, zm_r, 0)
    load_x.wait()
    chain_start(xg, zx_s, zx_r, 0)
    load_g.wait()
    for part in range(GPARTS):
        chain_start(gg, zg_s, zg_r, 0, part)
    for i in range(3):
        w_copy(i).start()
    dispatch_x(z)
    for part in range(GPARTS):
        dispatch_g(z, part)
    for cp in load_w:
        cp.wait()
    for i in range(3):
        w_copy(i).wait()
    acts(z)
    for k in range(planes - 1):
        chain_wait(meta, zm_s, zm_r, k)
        chain_wait(xg, zx_s, zx_r, k)
        if k < planes - 2:
            chain_start(meta, zm_s, zm_r, k + 1)
            chain_start(xg, zx_s, zx_r, k + 1)
        both(dispatch_x, k)
        if k == 0:
            grads(z)
        else:
            both(grads, k - 1)
        for part in range(GPARTS):
            chain_wait(gg, zg_s, zg_r, k, part)
            if k < planes - 2:
                chain_start(gg, zg_s, zg_r, k + 1, part)
            both(functools.partial(dispatch_g, part=part), k)
        both(acts, k)
        if k > 0:
            forward_both(k - 1)
    both(grads, planes - 2)

    is_end = jnp.where((z == 0) | (z == last), 1, 0)

    @pl.loop(0, 2)
    def _(phase):
        @pl.when(phase == is_end)
        def _():
            for p in range(planes):
                for i, (src, dst) in enumerate(((rows, rows_h), (scaled, scaled_h))):
                    for cp in halves(src, dst, i, p):
                        cp.wait()
                for i, ref in enumerate((gate_gr, up_gr, hid)):
                    rep_copy(ref, 2 + i, p).wait()
            weight_in(rows_h, gate_gr, gwo_v)
            out_copy(0).start()
            weight_in(rows_h, up_gr, uwo_v)
            out_copy(1).start()
            weight_down()
            out_copy(2).start()

        @pl.when(phase == 0)
        def _():
            forward_both(planes - 2)

    @pl.loop(0, PIECES)
    def _(q):
        own_part[...] = own_sum(z, q)

        @pl.when(z < last)
        def _():
            ret_wait(1, z, q)
            own_part[...] += rcv[1, z, :, piece(q)].astype(F32)

        @pl.when(z > 0)
        def _():
            ret_wait(0, z, q)
            own_part[...] += rcv[0, z, :, piece(q)].astype(F32)

        out_ref[:, piece(q)] = own_part[...].astype(BF16)

    for i in range(3):
        out_copy(i).wait()

    chain_drain(meta, zm_s, zm_r)
    chain_drain(xg, zx_s, zx_r)
    chain_drain(gg, zg_s, zg_r, range(GPARTS))
    plane_drain(st_x, rows, px_s, px_r)
    plane_drain(st_g, scaled, pg_s, pg_r, GPARTS)
    plane_drain(sg, ret, pr_s, pr_r, PIECES)
    for p in range(planes):
        @pl.when(p < z)
        def _(p=p):
            for q in range(PIECES):
                ret_copy(1, p, q).wait_send()

        @pl.when(p > z)
        def _(p=p):
            for q in range(PIECES):
                ret_copy(0, p, q).wait_send()


def hand_over(*refs):
    srcs, dsts, held, sems = refs[:4], refs[4:8], refs[8:12], refs[12]
    loads, stores = [], []
    for i in range(4):
        axis = len(srcs[i].shape) - 2
        piece = srcs[i].shape[axis] // PIECES
        for q in range(PIECES):
            at = (0,) * axis + (pl.ds(q * piece, piece),)
            loads.append(pltpu.make_async_copy(srcs[i].at[at], held[i].at[at], sems.at[0, i, q]))
            stores.append(pltpu.make_async_copy(held[i].at[at], dsts[i].at[at], sems.at[1, i, q]))
    for cp in loads:
        cp.start()
    for load, store in zip(loads, stores):
        load.wait()
        store.start()
    for cp in stores:
        cp.wait()


def chained(inputs, out_grad, expert_ids, gates, gate_w, up_w, down_w):
    tok, feat = inputs.shape
    half, hidden_n = gate_w.shape[1], gate_w.shape[2]
    experts = lax.axis_size("expert")
    planes = experts // COLS
    cap = 2 * tok * expert_ids.shape[1] // experts
    slots = COLS * cap
    total = planes * slots
    dma = pltpu.SemaphoreType.DMA
    vmem = pl.BlockSpec(memory_space=pltpu.VMEM)
    hbm = pl.BlockSpec(memory_space=pl.ANY)
    block = (planes, slots, feat)
    act = (planes, slots, hidden_n)
    scratch = [
        pltpu.VMEM((planes, tok, feat), BF16), pltpu.VMEM((planes, tok, feat), BF16),
        pltpu.VMEM((planes, 8, tok), F32),
        pltpu.VMEM(block, BF16), pltpu.VMEM(block, BF16), pltpu.VMEM(block, BF16), pltpu.VMEM(block, BF16),
        pltpu.VMEM((planes, tok, slots), BF16),
        pltpu.VMEM((feat, hidden_n), BF16), pltpu.VMEM((feat, hidden_n), BF16), pltpu.VMEM((hidden_n, feat), BF16),
        pltpu.VMEM(act, F32), pltpu.VMEM(act, F32),
        pltpu.VMEM((2,) + act, BF16), pltpu.VMEM((2,) + act, BF16), pltpu.VMEM((2,) + act, BF16),
        pltpu.VMEM((2, planes, slots, half), BF16), pltpu.VMEM((2, planes, slots, half), BF16),
        pltpu.VMEM(block, BF16), pltpu.VMEM(block, BF16),
        pltpu.VMEM((2, planes, tok, feat), BF16), pltpu.VMEM((planes, tok, feat), BF16),
        pltpu.VMEM((tok, feat // PIECES), F32), pltpu.VMEM((slots, hidden_n), F32),
        pltpu.VMEM(gate_w.shape, BF16), pltpu.VMEM(up_w.shape, BF16), pltpu.VMEM(down_w.shape, BF16),
        dma((5,)), dma((3,)), dma((3,)),
        dma((2, planes - 1)), dma((2, planes - 1)), dma((2, planes - 1)), dma((2, planes - 1)),
        dma((2, planes - 1, GPARTS)), dma((2, planes - 1, GPARTS)),
        dma((planes, COLS - 1, 1)), dma((planes, COLS - 1, 1)),
        dma((planes, COLS - 1, GPARTS)), dma((planes, COLS - 1, GPARTS)),
        dma((planes, COLS - 1, PIECES)), dma((planes, COLS - 1, PIECES)),
        dma((planes, PIECES)), dma((2, planes, PIECES)), dma((5, planes)), dma((5, planes)), dma((2, planes)), dma((3,)),
    ]
    results = pl.pallas_call(
        functools.partial(layer_kernel, planes, experts, cap),
        out_shape=(
            jax.ShapeDtypeStruct((tok, feat), BF16),
            jax.ShapeDtypeStruct(gate_w.shape, BF16),
            jax.ShapeDtypeStruct(up_w.shape, BF16),
            jax.ShapeDtypeStruct(down_w.shape, BF16),
        ),
        in_specs=[vmem, vmem] + [hbm] * 5,
        out_specs=(vmem, hbm, hbm, hbm),
        scratch_shapes=scratch,
        compiler_params=pltpu.CompilerParams(
            collective_id=0, has_side_effects=True, vmem_limit_bytes=60 * 1024 * 1024
        ),
        cost_estimate=pl.CostEstimate(
            flops=18 * total * feat * hidden_n, bytes_accessed=8 * feat * hidden_n, transcendentals=total * hidden_n
        ),
    )(expert_ids.T, gates.T, inputs, out_grad, gate_w, up_w, down_w)
    return pl.pallas_call(
        hand_over,
        out_shape=tuple(jax.ShapeDtypeStruct(a.shape, a.dtype) for a in results),
        in_specs=[hbm] * 4,
        out_specs=(hbm,) * 4,
        scratch_shapes=[pltpu.VMEM(a.shape, a.dtype) for a in results] + [dma((2, 4, PIECES))],
        compiler_params=pltpu.CompilerParams(vmem_limit_bytes=16 * 1024 * 1024),
    )(*results)


def arrange(received, owners, local_exp, capacity):
    feature_n = received.shape[1]
    shaped = received.reshape(owners, local_exp, capacity, feature_n)
    return shaped.transpose(1, 0, 2, 3).reshape(local_exp, owners * capacity, feature_n)


def restore(slot_rows, owners, capacity):
    local_exp = slot_rows.shape[0]
    feature_n = slot_rows.shape[2]
    shaped = slot_rows.reshape(local_exp, owners, capacity, feature_n)
    return shaped.transpose(1, 0, 2, 3).reshape(owners * local_exp * capacity, feature_n)


def local(inputs, out_grad, expert_ids, gates, gate_w, up_w, down_w):
    if lax.axis_size("expert") <= 16:
        return chained(inputs, out_grad, expert_ids, gates, gate_w, up_w, down_w)
    tok_dev = inputs.shape[0]
    feature_n = inputs.shape[1]
    topk_n = expert_ids.shape[1]
    local_exp = gate_w.shape[0]
    owners = lax.axis_size("expert")
    expert_total = local_exp * owners
    capacity = 2 * tok_dev * topk_n // expert_total
    pair_count = tok_dev * topk_n
    slot_total = expert_total * capacity
    flat_ids = expert_ids.reshape(pair_count)
    one_hot = (flat_ids[:, None] == jnp.arange(expert_total, dtype=jnp.int32)[None, :]).astype(
        jnp.int32
    )
    rank_index = (
        jnp.sum(jnp.cumsum(one_hot, axis=0, dtype=jnp.int32) * one_hot, axis=1, dtype=jnp.int32) - 1
    )
    slot_index = flat_ids * capacity + rank_index
    input_pairs = jnp.repeat(inputs, topk_n, axis=0)
    scaled_pairs = (
        gates.reshape(pair_count, 1) * jnp.repeat(out_grad, topk_n, axis=0).astype(jnp.float32)
    ).astype(jnp.bfloat16)
    send_inputs = jnp.zeros((slot_total, feature_n), jnp.bfloat16).at[slot_index].set(input_pairs)
    send_grads = jnp.zeros((slot_total, feature_n), jnp.bfloat16).at[slot_index].set(scaled_pairs)
    full_gate, full_up, full_down = (
        lax.all_gather(gate_w, "rep", axis=1, tiled=True),
        lax.all_gather(up_w, "rep", axis=1, tiled=True),
        lax.all_gather(down_w, "rep", axis=2, tiled=True),
    )
    recv_inputs, recv_grads = (
        lax.all_to_all(send_inputs, "expert", split_axis=0, concat_axis=0, tiled=True),
        lax.all_to_all(send_grads, "expert", split_axis=0, concat_axis=0, tiled=True),
    )
    rows_in = arrange(recv_inputs, owners, local_exp, capacity)
    scaled_rows = arrange(recv_grads, owners, local_exp, capacity)
    gate_act = jnp.einsum("erd,edh->erh", rows_in, full_gate, preferred_element_type=jnp.float32)
    up_act = jnp.einsum("erd,edh->erh", rows_in, full_up, preferred_element_type=jnp.float32)
    gate_act, up_act = (gate_act, up_act)
    sigma = jax.nn.sigmoid(gate_act)
    silu_val = gate_act * sigma
    hidden = (silu_val * up_act).astype(jnp.bfloat16)
    hidden_grad = jnp.einsum(
        "erd,ehd->erh", scaled_rows, full_down, preferred_element_type=jnp.float32
    )
    gate_grad = (hidden_grad * up_act * sigma * (1.0 + gate_act * (1.0 - sigma))).astype(
        jnp.bfloat16
    )
    up_grad = (hidden_grad * silu_val).astype(jnp.bfloat16)
    first = jnp.einsum("erh,edh->erd", gate_grad, full_gate, preferred_element_type=jnp.float32)
    slot_grad = (
        first + jnp.einsum("erh,edh->erd", up_grad, full_up, preferred_element_type=jnp.float32)
    ).astype(jnp.bfloat16)
    returned = lax.all_to_all(
        restore(slot_grad, owners, capacity), "expert", split_axis=0, concat_axis=0, tiled=True
    )
    gate_part = jnp.einsum("erd,erh->edh", rows_in, gate_grad, preferred_element_type=jnp.float32)
    up_part = jnp.einsum("erd,erh->edh", rows_in, up_grad, preferred_element_type=jnp.float32)
    down_part = jnp.einsum("erh,erd->ehd", hidden, scaled_rows, preferred_element_type=jnp.float32)
    gate_sum, up_sum, down_sum = (
        lax.psum_scatter(
            gate_part.astype(jnp.bfloat16), "rep", scatter_dimension=1, tiled=True
        ).astype(jnp.float32),
        lax.psum_scatter(
            up_part.astype(jnp.bfloat16), "rep", scatter_dimension=1, tiled=True
        ).astype(jnp.float32),
        lax.psum_scatter(
            down_part.astype(jnp.bfloat16), "rep", scatter_dimension=2, tiled=True
        ).astype(jnp.float32),
    )
    picked = returned[slot_index]
    input_grad = jnp.sum(
        picked.reshape(tok_dev, topk_n, feature_n).astype(jnp.float32), axis=1
    ).astype(jnp.bfloat16)
    return (
        input_grad,
        gate_sum.astype(jnp.bfloat16),
        up_sum.astype(jnp.bfloat16),
        down_sum.astype(jnp.bfloat16),
    )


def solution(mesh):
    return jax.shard_map(
        local,
        mesh=mesh,
        in_specs=(
            P(("expert", "rep"), None),
            P(("expert", "rep"), None),
            P(("expert", "rep"), None),
            P(("expert", "rep"), None),
            P("expert", "rep", None),
            P("expert", "rep", None),
            P("expert", None, "rep"),
        ),
        out_specs=(
            P(("expert", "rep"), None),
            P("expert", "rep", None),
            P("expert", "rep", None),
            P("expert", None, "rep"),
        ),
        check_vma=False,
    )
```

```python
import functools

import jax
import jax.numpy as jnp
from jax import lax
from jax.experimental import pallas as pl
from jax.experimental.pallas import tpu as pltpu
from jax.sharding import PartitionSpec as P

MESH = pl.DeviceIdType.MESH
COLS = 4
PIECES = 4
GPARTS = 2
F32 = jnp.float32
BF16 = jnp.bfloat16
NT = (((1,), (1,)), ((), ()))
TN = (((0,), (0,)), ((), ()))


def layer_kernel(
    planes, experts, cap,
    ids_ref, gates_ref, x_hbm, g_hbm, gw_hbm, uw_hbm, dw_hbm,
    out_ref, gwo_ref, uwo_ref, dwo_ref,
    xg, gg, meta, st_x, st_g, rows, scaled, sel_t, wg, wu, wd, ga, ua,
    hid, gate_gr, up_gr, rows_h, scaled_h, sg, ret, rcv, snd,
    own_part, hg_part, gwo_v, uwo_v, dwo_v,
    load_sem, w_send, w_recv, zm_s, zm_r, zx_s, zx_r, zg_s, zg_r,
    px_s, px_r, pg_s, pg_r, pr_s, pr_r, zr_s, zr_r, rep_s, rep_r, loc_sem, out_sem,
):
    e, r = lax.axis_index("expert"), lax.axis_index("rep")
    z, c = e // COLS, e % COLS
    other = 1 - r
    tok = x_hbm.shape[0]
    last = planes - 1
    slots = COLS * cap
    half = gw_hbm.shape[1]
    feat = x_hbm.shape[1]
    hidden_n = gw_hbm.shape[2]
    total = planes * slots

    def al(v, m):
        return pl.multiple_of(v, m)

    w_at = [
        (gw_hbm.at[0], wg.at[pl.ds(al(r * half, half), half)]),
        (uw_hbm.at[0], wu.at[pl.ds(al(r * half, half), half)]),
        (dw_hbm.at[0], wd.at[:, pl.ds(al(r * half, half), half)]),
    ]
    load_x = pltpu.make_async_copy(x_hbm, xg.at[z], load_sem.at[0])
    load_g = pltpu.make_async_copy(g_hbm, gg.at[z], load_sem.at[1])
    load_x.start()
    load_g.start()
    load_w = [pltpu.make_async_copy(s, d, load_sem.at[2 + i]) for i, (s, d) in enumerate(w_at)]
    for cp in load_w:
        cp.start()

    barrier = pltpu.get_barrier_semaphore()
    for j in range(1, COLS):
        pl.semaphore_signal(barrier, inc=1, device_id=(z * COLS + (c + j) % COLS, r), device_id_type=MESH)
    pl.semaphore_signal(barrier, inc=1, device_id=(e, other), device_id_type=MESH)

    @pl.when(z < last)
    def _():
        pl.semaphore_signal(barrier, inc=1, device_id=(e + COLS, r), device_id_type=MESH)

    @pl.when(z > 0)
    def _():
        pl.semaphore_signal(barrier, inc=1, device_id=(e - COLS, r), device_id_type=MESH)

    id0, id1 = ids_ref[0:1, :], ids_ref[1:2, :]
    exp_iota = lax.broadcasted_iota(jnp.int32, (experts, tok), 0)
    one0 = jnp.where(exp_iota == id0, 1.0, 0.0)
    one1 = jnp.where(exp_iota == id1, 1.0, 0.0)
    before = jnp.where(
        lax.broadcasted_iota(jnp.int32, (tok, tok), 0) < lax.broadcasted_iota(jnp.int32, (tok, tok), 1), 1.0, 0.0
    ).astype(BF16)
    rank = jnp.dot((one0 + one1).astype(BF16), before, preferred_element_type=F32)
    slot0 = jnp.sum(rank * one0, axis=0, keepdims=True) + id0.astype(F32) * cap
    slot1 = jnp.sum(rank * one1, axis=0, keepdims=True) + id1.astype(F32) * cap
    meta[z] = jnp.concatenate(
        [slot0, slot1, gates_ref[0:1, :], gates_ref[1:2, :], jnp.zeros((4, tok), F32)], axis=0
    )
    neighbours = COLS + jnp.where(z < last, 1, 0) + jnp.where(z > 0, 1, 0)
    pl.semaphore_wait(barrier, neighbours)

    def span(part):
        wide = feat // GPARTS
        return (slice(None), pl.ds(part * wide, wide))

    def at_part(ref, i, part):
        return ref.at[i] if part is None else ref.at[(i,) + span(part)]

    def at_sem(sem, way, k, part):
        return sem.at[way, k] if part is None else sem.at[way, k, part]

    def chain_copy(buf, ss, rs, way, k, part, i, target):
        return pltpu.make_async_remote_copy(
            src_ref=at_part(buf, i, part), dst_ref=at_part(buf, i, part),
            send_sem=at_sem(ss, way, k, part), recv_sem=at_sem(rs, way, k, part),
            device_id=target, device_id_type=MESH)

    def up(buf, ss, rs, k, part):
        return chain_copy(buf, ss, rs, 0, k, part, jnp.maximum(z - k, 0), (e + COLS, r))

    def down(buf, ss, rs, k, part):
        return chain_copy(buf, ss, rs, 1, k, part, jnp.minimum(z + k, last), (e - COLS, r))

    def can_up(k):
        return (z < last) & (z - k >= 0)

    def can_down(k):
        return (z > 0) & (z + k <= last)

    def chain_start(buf, ss, rs, k, part=None):
        @pl.when(can_up(k))
        def _():
            up(buf, ss, rs, k, part).start()

        @pl.when(can_down(k))
        def _():
            down(buf, ss, rs, k, part).start()

    def chain_wait(buf, ss, rs, k, part=None):
        @pl.when(z - 1 - k >= 0)
        def _():
            chain_copy(buf, ss, rs, 0, k, part, jnp.maximum(z - 1 - k, 0), (e, other)).wait_recv()

        @pl.when(z + 1 + k <= last)
        def _():
            chain_copy(buf, ss, rs, 1, k, part, jnp.minimum(z + 1 + k, last), (e, other)).wait_recv()

    def chain_drain(buf, ss, rs, parts=(None,)):
        for k in range(planes - 1):
            for part in parts:
                @pl.when(can_up(k))
                def _(k=k, part=part):
                    up(buf, ss, rs, k, part).wait_send()

                @pl.when(can_down(k))
                def _(k=k, part=part):
                    down(buf, ss, rs, k, part).wait_send()

    def plane_copy(st, dst, ss, rs, p, j, q, parts):
        d = (c + j) % COLS
        cols = pl.ds(al(q * (feat // parts), feat // parts), feat // parts)
        return pltpu.make_async_remote_copy(
            src_ref=st.at[p, pl.ds(al(d * cap, cap), cap), cols],
            dst_ref=dst.at[p, pl.ds(al(c * cap, cap), cap), cols],
            send_sem=ss.at[p, j - 1, q], recv_sem=rs.at[p, j - 1, q],
            device_id=(z * COLS + d, r), device_id_type=MESH)

    def plane_send(st, dst, ss, rs, p, q=0, parts=1):
        for j in range(1, COLS):
            plane_copy(st, dst, ss, rs, p, j, q, parts).start()
        cols = pl.ds(al(q * (feat // parts), feat // parts), feat // parts)
        dst[p, pl.ds(al(c * cap, cap), cap), cols] = st[p, pl.ds(al(c * cap, cap), cap), cols]

    def plane_wait(st, dst, ss, rs, p, q=0, parts=1):
        for j in range(1, COLS):
            plane_copy(st, dst, ss, rs, p, j, q, parts).wait_recv()

    def plane_drain(st, dst, ss, rs, parts=1):
        for p in range(planes):
            for j in range(1, COLS):
                for q in range(parts):
                    plane_copy(st, dst, ss, rs, p, j, q, parts).wait_send()

    def selection(p):
        m = meta[p]
        place = (lax.broadcasted_iota(jnp.int32, (slots, tok), 0) + z * slots).astype(F32)
        return jnp.where(place == m[0:1, :], 1.0, 0.0), jnp.where(place == m[1:2, :], 1.0, 0.0), m

    def dispatch_x(p):
        s0, s1, _ = selection(p)
        pick = s0 + s1
        sel_t[p] = pick.T.astype(BF16)
        st_x[p] = jnp.dot(pick.astype(BF16), xg[p], preferred_element_type=F32).astype(BF16)
        plane_send(st_x, rows, px_s, px_r, p)

    def dispatch_g(p, part):
        s0, s1, m = selection(p)
        gate = jnp.sum(s0 * m[2:3, :] + s1 * m[3:4, :], axis=1, keepdims=True)
        at = (p,) + span(part)
        picked = jnp.dot((s0 + s1).astype(BF16), gg[at], preferred_element_type=F32)
        st_g[at] = (picked * gate).astype(BF16)
        plane_send(st_g, scaled, pg_s, pg_r, p, part, GPARTS)

    def both(fn, k):
        @pl.when(z - 1 - k >= 0)
        def _():
            fn(jnp.maximum(z - 1 - k, 0))

        @pl.when(z + 1 + k <= last)
        def _():
            fn(jnp.minimum(z + 1 + k, last))

    def w_copy(i):
        s, d = w_at[i]
        return pltpu.make_async_remote_copy(
            src_ref=s, dst_ref=d, send_sem=w_send.at[i], recv_sem=w_recv.at[i],
            device_id=(e, other), device_id_type=MESH)

    def halves(src, dst, i, p):
        lo = pl.ds(al(r * half, half), half)
        hi = pl.ds(al(other * half, half), half)
        return (
            pltpu.make_async_copy(src.at[p, :, lo], dst.at[r, p], loc_sem.at[i, p]),
            pltpu.make_async_remote_copy(
                src_ref=src.at[p, :, hi], dst_ref=dst.at[r, p], send_sem=rep_s.at[i, p], recv_sem=rep_r.at[i, p],
                device_id=(e, other), device_id_type=MESH),
        )

    def rep_copy(ref, i, p):
        return pltpu.make_async_remote_copy(
            src_ref=ref.at[r, p], dst_ref=ref.at[r, p], send_sem=rep_s.at[i, p], recv_sem=rep_r.at[i, p],
            device_id=(e, other), device_id_type=MESH)

    step_h = 256 if hidden_n % 256 == 0 else hidden_n
    step_d = feat // PIECES

    def acts(p):
        plane_wait(st_x, rows, px_s, px_r, p)
        for cp in halves(rows, rows_h, 0, p):
            cp.start()

        @pl.loop(0, hidden_n // step_h)
        def _(i):
            cols = pl.ds(al(i * step_h, step_h), step_h)
            ga[p, :, cols] = jnp.dot(rows[p], wg[:, cols], preferred_element_type=F32)
            ua[p, :, cols] = jnp.dot(rows[p], wu[:, cols], preferred_element_type=F32)

    def grads(p):
        for part in range(GPARTS):
            plane_wait(st_g, scaled, pg_s, pg_r, p, part, GPARTS)
            at = span(part)

            @pl.loop(0, hidden_n // step_h)
            def _(i):
                cols = pl.ds(al(i * step_h, step_h), step_h)
                hg = lax.dot_general(scaled[(p,) + at], wd[cols, at[1]], NT, preferred_element_type=F32)
                if part < GPARTS - 1:
                    hg_part[:, cols] = hg if part == 0 else hg_part[:, cols] + hg
                else:
                    if part > 0:
                        hg = hg + hg_part[:, cols]
                    gate_act, up_act = ga[p, :, cols], ua[p, :, cols]
                    sigma = jax.nn.sigmoid(gate_act)
                    silu = gate_act * sigma
                    hid[r, p, :, cols] = (silu * up_act).astype(BF16)
                    gate_gr[r, p, :, cols] = (hg * up_act * sigma * (1.0 + gate_act * (1.0 - sigma))).astype(BF16)
                    up_gr[r, p, :, cols] = (hg * silu).astype(BF16)

        @pl.loop(0, PIECES)
        def _(i):
            cols = pl.ds(al(i * step_d, step_d), step_d)
            v = lax.dot_general(gate_gr[r, p], wg[cols, :], NT, preferred_element_type=F32)
            v = v + lax.dot_general(up_gr[r, p], wu[cols, :], NT, preferred_element_type=F32)
            sg[p, :, cols] = v.astype(BF16)
            plane_send(sg, ret, pr_s, pr_r, p, i, PIECES)

        for i, ref in enumerate((gate_gr, up_gr, hid)):
            rep_copy(ref, 2 + i, p).start()
        for cp in halves(scaled, scaled_h, 1, p):
            cp.start()

    def piece(q):
        return pl.ds(al(q * step_d, step_d), step_d)

    def ret_copy(way, p, q):
        return pltpu.make_async_remote_copy(
            src_ref=snd.at[p, :, piece(q)], dst_ref=rcv.at[way, p, :, piece(q)],
            send_sem=zr_s.at[p, q], recv_sem=zr_r.at[way, p, q],
            device_id=(jnp.where(way == 0, e + COLS, e - COLS), r), device_id_type=MESH)

    def ret_wait(way, p, q):
        pltpu.make_async_remote_copy(
            src_ref=snd.at[p, :, piece(q)], dst_ref=rcv.at[way, p, :, piece(q)],
            send_sem=zr_s.at[p, q], recv_sem=zr_r.at[way, p, q],
            device_id=(e, other), device_id_type=MESH).wait_recv()

    def own_sum(p, q):
        plane_wait(sg, ret, pr_s, pr_r, p, q, PIECES)
        return jnp.dot(sel_t[p], ret[p, :, piece(q)], preferred_element_type=F32)

    def forward(way, p, first):
        @pl.loop(0, PIECES)
        def _(q):
            own = own_sum(p, q)

            @pl.when(first)
            def _():
                snd[p, :, piece(q)] = own.astype(BF16)

            @pl.when(jnp.logical_not(first))
            def _():
                ret_wait(way, p, q)
                snd[p, :, piece(q)] = (own + rcv[way, p, :, piece(q)].astype(F32)).astype(BF16)

            ret_copy(way, p, q).start()

    def forward_both(k):
        @pl.loop(0, 2)
        def _(side):
            way = jnp.where(z >= planes // 2, 1 - side, side)
            p = jnp.where(way == 1, last - 1 - k, k + 1)

            @pl.when(((way == 1) & (p < z)) | ((way == 0) & (p > z)))
            def _():
                forward(way, p, ((way == 1) & (z == last)) | ((way == 0) & (z == 0)))

    def weight_in(a_half, grad, out):
        step = 256

        @pl.loop(0, half // step)
        def _(i):
            cols = pl.ds(al(i * step, step), step)
            v = 0.0
            for rep in range(2):
                v = v + lax.dot_general(
                    a_half[rep, :, :, cols].reshape(total, step), grad[rep].reshape(total, hidden_n), TN,
                    preferred_element_type=F32)
            out[0, cols, :] = v.astype(BF16)

    def weight_down():
        @pl.loop(0, hidden_n // step_h)
        def _(i):
            cols = pl.ds(al(i * step_h, step_h), step_h)
            v = 0.0
            for rep in range(2):
                v = v + lax.dot_general(
                    hid[rep, :, :, cols].reshape(total, step_h), scaled_h[rep].reshape(total, half), TN,
                    preferred_element_type=F32)
            dwo_v[0, cols, :] = v.astype(BF16)

    def out_copy(i):
        src, dst = ((gwo_v, gwo_ref), (uwo_v, uwo_ref), (dwo_v, dwo_ref))[i]
        return pltpu.make_async_copy(src, dst, out_sem.at[i])

    def weight_grads():
        @pl.loop(0, planes)
        def _(p):
            for i, (src, dst) in enumerate(((rows, rows_h), (scaled, scaled_h))):
                for cp in halves(src, dst, i, p):
                    cp.wait()
            for i, ref in enumerate((gate_gr, up_gr, hid)):
                rep_copy(ref, 2 + i, p).wait()

        weight_in(rows_h, gate_gr, gwo_v)
        out_copy(0).start()
        weight_in(rows_h, up_gr, uwo_v)
        out_copy(1).start()
        weight_down()
        out_copy(2).start()

    chain_start(meta, zm_s, zm_r, 0)
    load_x.wait()
    chain_start(xg, zx_s, zx_r, 0)
    load_g.wait()
    for i in range(3):
        w_copy(i).start()
    dispatch_x(z)
    for part in range(GPARTS):
        chain_start(gg, zg_s, zg_r, 0, part)
        dispatch_g(z, part)
    for cp in load_w:
        cp.wait()
    for i in range(3):
        w_copy(i).wait()
    acts(z)
    for k in range(planes - 1):
        chain_wait(meta, zm_s, zm_r, k)
        chain_wait(xg, zx_s, zx_r, k)
        if k < planes - 2:
            chain_start(meta, zm_s, zm_r, k + 1)
            chain_start(xg, zx_s, zx_r, k + 1)
        both(dispatch_x, k)
        if k == 0:
            grads(z)
        else:
            both(grads, k - 1)
        if k == planes - 2:
            @pl.when((z > 0) & (z < last))
            def _():
                weight_grads()

            both(acts, k)
            forward_both(k - 1)
        for part in range(GPARTS):
            chain_wait(gg, zg_s, zg_r, k, part)
            if k < planes - 2:
                chain_start(gg, zg_s, zg_r, k + 1, part)
            both(functools.partial(dispatch_g, part=part), k)
        if k < planes - 2:
            both(acts, k)
            if k > 0:
                forward_both(k - 1)
    both(grads, planes - 2)
    forward_both(planes - 2)

    @pl.when((z == 0) | (z == last))
    def _():
        weight_grads()

    @pl.loop(0, PIECES)
    def _(q):
        own_part[...] = own_sum(z, q)

        @pl.when(z < last)
        def _():
            ret_wait(1, z, q)
            own_part[...] += rcv[1, z, :, piece(q)].astype(F32)

        @pl.when(z > 0)
        def _():
            ret_wait(0, z, q)
            own_part[...] += rcv[0, z, :, piece(q)].astype(F32)

        out_ref[:, piece(q)] = own_part[...].astype(BF16)

    for i in range(3):
        out_copy(i).wait()

    chain_drain(meta, zm_s, zm_r)
    chain_drain(xg, zx_s, zx_r)
    chain_drain(gg, zg_s, zg_r, range(GPARTS))
    plane_drain(st_x, rows, px_s, px_r)
    plane_drain(st_g, scaled, pg_s, pg_r, GPARTS)
    plane_drain(sg, ret, pr_s, pr_r, PIECES)
    for p in range(planes):
        @pl.when(p < z)
        def _(p=p):
            for q in range(PIECES):
                ret_copy(1, p, q).wait_send()

        @pl.when(p > z)
        def _(p=p):
            for q in range(PIECES):
                ret_copy(0, p, q).wait_send()


def chained(inputs, out_grad, expert_ids, gates, gate_w, up_w, down_w):
    tok, feat = inputs.shape
    half, hidden_n = gate_w.shape[1], gate_w.shape[2]
    experts = lax.axis_size("expert")
    planes = experts // COLS
    cap = 2 * tok * expert_ids.shape[1] // experts
    slots = COLS * cap
    total = planes * slots
    dma = pltpu.SemaphoreType.DMA
    vmem = pl.BlockSpec(memory_space=pltpu.VMEM)
    hbm = pl.BlockSpec(memory_space=pl.ANY)
    block = (planes, slots, feat)
    act = (planes, slots, hidden_n)
    scratch = [
        pltpu.VMEM((planes, tok, feat), BF16), pltpu.VMEM((planes, tok, feat), BF16),
        pltpu.VMEM((planes, 8, tok), F32),
        pltpu.VMEM(block, BF16), pltpu.VMEM(block, BF16), pltpu.VMEM(block, BF16), pltpu.VMEM(block, BF16),
        pltpu.VMEM((planes, tok, slots), BF16),
        pltpu.VMEM((feat, hidden_n), BF16), pltpu.VMEM((feat, hidden_n), BF16), pltpu.VMEM((hidden_n, feat), BF16),
        pltpu.VMEM(act, F32), pltpu.VMEM(act, F32),
        pltpu.VMEM((2,) + act, BF16), pltpu.VMEM((2,) + act, BF16), pltpu.VMEM((2,) + act, BF16),
        pltpu.VMEM((2, planes, slots, half), BF16), pltpu.VMEM((2, planes, slots, half), BF16),
        pltpu.VMEM(block, BF16), pltpu.VMEM(block, BF16),
        pltpu.VMEM((2, planes, tok, feat), BF16), pltpu.VMEM((planes, tok, feat), BF16),
        pltpu.VMEM((tok, feat // PIECES), F32), pltpu.VMEM((slots, hidden_n), F32),
        pltpu.VMEM(gate_w.shape, BF16), pltpu.VMEM(up_w.shape, BF16), pltpu.VMEM(down_w.shape, BF16),
        dma((5,)), dma((3,)), dma((3,)),
        dma((2, planes - 1)), dma((2, planes - 1)), dma((2, planes - 1)), dma((2, planes - 1)),
        dma((2, planes - 1, GPARTS)), dma((2, planes - 1, GPARTS)),
        dma((planes, COLS - 1, 1)), dma((planes, COLS - 1, 1)),
        dma((planes, COLS - 1, GPARTS)), dma((planes, COLS - 1, GPARTS)),
        dma((planes, COLS - 1, PIECES)), dma((planes, COLS - 1, PIECES)),
        dma((planes, PIECES)), dma((2, planes, PIECES)), dma((5, planes)), dma((5, planes)), dma((2, planes)), dma((3,)),
    ]
    return pl.pallas_call(
        functools.partial(layer_kernel, planes, experts, cap),
        out_shape=(
            jax.ShapeDtypeStruct((tok, feat), BF16),
            jax.ShapeDtypeStruct(gate_w.shape, BF16),
            jax.ShapeDtypeStruct(up_w.shape, BF16),
            jax.ShapeDtypeStruct(down_w.shape, BF16),
        ),
        in_specs=[vmem, vmem] + [hbm] * 5,
        out_specs=(vmem, hbm, hbm, hbm),
        scratch_shapes=scratch,
        compiler_params=pltpu.CompilerParams(
            collective_id=0, has_side_effects=True, vmem_limit_bytes=50 * 1024 * 1024
        ),
        cost_estimate=pl.CostEstimate(
            flops=18 * total * feat * hidden_n, bytes_accessed=8 * feat * hidden_n, transcendentals=total * hidden_n
        ),
    )(expert_ids.T, gates.T, inputs, out_grad, gate_w, up_w, down_w)


def arrange(received, owners, local_exp, capacity):
    feature_n = received.shape[1]
    shaped = received.reshape(owners, local_exp, capacity, feature_n)
    return shaped.transpose(1, 0, 2, 3).reshape(local_exp, owners * capacity, feature_n)


def restore(slot_rows, owners, capacity):
    local_exp = slot_rows.shape[0]
    feature_n = slot_rows.shape[2]
    shaped = slot_rows.reshape(local_exp, owners, capacity, feature_n)
    return shaped.transpose(1, 0, 2, 3).reshape(owners * local_exp * capacity, feature_n)


def local(inputs, out_grad, expert_ids, gates, gate_w, up_w, down_w):
    if lax.axis_size("expert") <= 16:
        return chained(inputs, out_grad, expert_ids, gates, gate_w, up_w, down_w)
    tok_dev = inputs.shape[0]
    feature_n = inputs.shape[1]
    topk_n = expert_ids.shape[1]
    local_exp = gate_w.shape[0]
    owners = lax.axis_size("expert")
    expert_total = local_exp * owners
    capacity = 2 * tok_dev * topk_n // expert_total
    pair_count = tok_dev * topk_n
    slot_total = expert_total * capacity
    flat_ids = expert_ids.reshape(pair_count)
    one_hot = (flat_ids[:, None] == jnp.arange(expert_total, dtype=jnp.int32)[None, :]).astype(
        jnp.int32
    )
    rank_index = (
        jnp.sum(jnp.cumsum(one_hot, axis=0, dtype=jnp.int32) * one_hot, axis=1, dtype=jnp.int32) - 1
    )
    slot_index = flat_ids * capacity + rank_index
    input_pairs = jnp.repeat(inputs, topk_n, axis=0)
    scaled_pairs = (
        gates.reshape(pair_count, 1) * jnp.repeat(out_grad, topk_n, axis=0).astype(jnp.float32)
    ).astype(jnp.bfloat16)
    send_inputs = jnp.zeros((slot_total, feature_n), jnp.bfloat16).at[slot_index].set(input_pairs)
    send_grads = jnp.zeros((slot_total, feature_n), jnp.bfloat16).at[slot_index].set(scaled_pairs)
    full_gate, full_up, full_down = (
        lax.all_gather(gate_w, "rep", axis=1, tiled=True),
        lax.all_gather(up_w, "rep", axis=1, tiled=True),
        lax.all_gather(down_w, "rep", axis=2, tiled=True),
    )
    recv_inputs, recv_grads = (
        lax.all_to_all(send_inputs, "expert", split_axis=0, concat_axis=0, tiled=True),
        lax.all_to_all(send_grads, "expert", split_axis=0, concat_axis=0, tiled=True),
    )
    rows_in = arrange(recv_inputs, owners, local_exp, capacity)
    scaled_rows = arrange(recv_grads, owners, local_exp, capacity)
    gate_act = jnp.einsum("erd,edh->erh", rows_in, full_gate, preferred_element_type=jnp.float32)
    up_act = jnp.einsum("erd,edh->erh", rows_in, full_up, preferred_element_type=jnp.float32)
    gate_act, up_act = (gate_act, up_act)
    sigma = jax.nn.sigmoid(gate_act)
    silu_val = gate_act * sigma
    hidden = (silu_val * up_act).astype(jnp.bfloat16)
    hidden_grad = jnp.einsum(
        "erd,ehd->erh", scaled_rows, full_down, preferred_element_type=jnp.float32
    )
    gate_grad = (hidden_grad * up_act * sigma * (1.0 + gate_act * (1.0 - sigma))).astype(
        jnp.bfloat16
    )
    up_grad = (hidden_grad * silu_val).astype(jnp.bfloat16)
    first = jnp.einsum("erh,edh->erd", gate_grad, full_gate, preferred_element_type=jnp.float32)
    slot_grad = (
        first + jnp.einsum("erh,edh->erd", up_grad, full_up, preferred_element_type=jnp.float32)
    ).astype(jnp.bfloat16)
    returned = lax.all_to_all(
        restore(slot_grad, owners, capacity), "expert", split_axis=0, concat_axis=0, tiled=True
    )
    gate_part = jnp.einsum("erd,erh->edh", rows_in, gate_grad, preferred_element_type=jnp.float32)
    up_part = jnp.einsum("erd,erh->edh", rows_in, up_grad, preferred_element_type=jnp.float32)
    down_part = jnp.einsum("erh,erd->ehd", hidden, scaled_rows, preferred_element_type=jnp.float32)
    gate_sum, up_sum, down_sum = (
        lax.psum_scatter(
            gate_part.astype(jnp.bfloat16), "rep", scatter_dimension=1, tiled=True
        ).astype(jnp.float32),
        lax.psum_scatter(
            up_part.astype(jnp.bfloat16), "rep", scatter_dimension=1, tiled=True
        ).astype(jnp.float32),
        lax.psum_scatter(
            down_part.astype(jnp.bfloat16), "rep", scatter_dimension=2, tiled=True
        ).astype(jnp.float32),
    )
    picked = returned[slot_index]
    input_grad = jnp.sum(
        picked.reshape(tok_dev, topk_n, feature_n).astype(jnp.float32), axis=1
    ).astype(jnp.bfloat16)
    return (
        input_grad,
        gate_sum.astype(jnp.bfloat16),
        up_sum.astype(jnp.bfloat16),
        down_sum.astype(jnp.bfloat16),
    )


def solution(mesh):
    return jax.shard_map(
        local,
        mesh=mesh,
        in_specs=(
            P(("expert", "rep"), None),
            P(("expert", "rep"), None),
            P(("expert", "rep"), None),
            P(("expert", "rep"), None),
            P("expert", "rep", None),
            P("expert", "rep", None),
            P("expert", None, "rep"),
        ),
        out_specs=(
            P(("expert", "rep"), None),
            P("expert", "rep", None),
            P("expert", "rep", None),
            P("expert", None, "rep"),
        ),
        check_vma=False,
    )
```

```python
import functools

import jax
import jax.numpy as jnp
from jax import lax
from jax.experimental import pallas as pl
from jax.experimental.pallas import tpu as pltpu
from jax.sharding import PartitionSpec as P

MESH = pl.DeviceIdType.MESH
COLS = 4
PIECES = 4
GPARTS = 2
F32 = jnp.float32
BF16 = jnp.bfloat16
NT = (((1,), (1,)), ((), ()))
TN = (((0,), (0,)), ((), ()))


def layer_kernel(
    planes, experts, cap,
    ids_ref, gates_ref, x_hbm, g_hbm, gw_hbm, uw_hbm, dw_hbm,
    out_ref, gwo_ref, uwo_ref, dwo_ref,
    xg, gg, meta, st_x, st_g, rows, scaled, sel_t, wg, wu, wd, ga, ua,
    hid, gate_gr, up_gr, rows_h, scaled_h, sg, ret, rcv, snd,
    own_part, hg_part, gwo_v, uwo_v, dwo_v,
    load_sem, w_send, w_recv, zm_s, zm_r, zx_s, zx_r, zg_s, zg_r,
    px_s, px_r, pg_s, pg_r, pr_s, pr_r, zr_s, zr_r, rep_s, rep_r, loc_sem, out_sem,
):
    e, r = lax.axis_index("expert"), lax.axis_index("rep")
    z, c = e // COLS, e % COLS
    other = 1 - r
    tok = x_hbm.shape[0]
    last = planes - 1
    slots = COLS * cap
    half = gw_hbm.shape[1]
    feat = x_hbm.shape[1]
    hidden_n = gw_hbm.shape[2]
    total = planes * slots

    def al(v, m):
        return pl.multiple_of(v, m)

    w_at = [
        (gw_hbm.at[0], wg.at[pl.ds(al(r * half, half), half)]),
        (uw_hbm.at[0], wu.at[pl.ds(al(r * half, half), half)]),
        (dw_hbm.at[0], wd.at[:, pl.ds(al(r * half, half), half)]),
    ]
    load_x = pltpu.make_async_copy(x_hbm, xg.at[z], load_sem.at[0])
    load_g = pltpu.make_async_copy(g_hbm, gg.at[z], load_sem.at[1])
    load_x.start()
    load_g.start()
    load_w = [pltpu.make_async_copy(s, d, load_sem.at[2 + i]) for i, (s, d) in enumerate(w_at)]
    for cp in load_w:
        cp.start()

    barrier = pltpu.get_barrier_semaphore()
    for j in range(1, COLS):
        pl.semaphore_signal(barrier, inc=1, device_id=(z * COLS + (c + j) % COLS, r), device_id_type=MESH)
    pl.semaphore_signal(barrier, inc=1, device_id=(e, other), device_id_type=MESH)

    @pl.when(z < last)
    def _():
        pl.semaphore_signal(barrier, inc=1, device_id=(e + COLS, r), device_id_type=MESH)

    @pl.when(z > 0)
    def _():
        pl.semaphore_signal(barrier, inc=1, device_id=(e - COLS, r), device_id_type=MESH)

    id0, id1 = ids_ref[0:1, :], ids_ref[1:2, :]
    exp_iota = lax.broadcasted_iota(jnp.int32, (experts, tok), 0)
    one0 = jnp.where(exp_iota == id0, 1.0, 0.0)
    one1 = jnp.where(exp_iota == id1, 1.0, 0.0)
    before = jnp.where(
        lax.broadcasted_iota(jnp.int32, (tok, tok), 0) < lax.broadcasted_iota(jnp.int32, (tok, tok), 1), 1.0, 0.0
    ).astype(BF16)
    rank = jnp.dot((one0 + one1).astype(BF16), before, preferred_element_type=F32)
    slot0 = jnp.sum(rank * one0, axis=0, keepdims=True) + id0.astype(F32) * cap
    slot1 = jnp.sum(rank * one1, axis=0, keepdims=True) + id1.astype(F32) * cap
    meta[z] = jnp.concatenate(
        [slot0, slot1, gates_ref[0:1, :], gates_ref[1:2, :], jnp.zeros((4, tok), F32)], axis=0
    )
    neighbours = COLS + jnp.where(z < last, 1, 0) + jnp.where(z > 0, 1, 0)
    pl.semaphore_wait(barrier, neighbours)

    def span(part):
        wide = feat // GPARTS
        return (slice(None), pl.ds(part * wide, wide))

    def at_part(ref, i, part):
        return ref.at[i] if part is None else ref.at[(i,) + span(part)]

    def at_sem(sem, way, k, part):
        return sem.at[way, k] if part is None else sem.at[way, k, part]

    def chain_copy(buf, ss, rs, way, k, part, i, target):
        return pltpu.make_async_remote_copy(
            src_ref=at_part(buf, i, part), dst_ref=at_part(buf, i, part),
            send_sem=at_sem(ss, way, k, part), recv_sem=at_sem(rs, way, k, part),
            device_id=target, device_id_type=MESH)

    def up(buf, ss, rs, k, part):
        return chain_copy(buf, ss, rs, 0, k, part, jnp.maximum(z - k, 0), (e + COLS, r))

    def down(buf, ss, rs, k, part):
        return chain_copy(buf, ss, rs, 1, k, part, jnp.minimum(z + k, last), (e - COLS, r))

    def can_up(k):
        return (z < last) & (z - k >= 0)

    def can_down(k):
        return (z > 0) & (z + k <= last)

    def chain_start(buf, ss, rs, k, part=None):
        @pl.when(can_up(k))
        def _():
            up(buf, ss, rs, k, part).start()

        @pl.when(can_down(k))
        def _():
            down(buf, ss, rs, k, part).start()

    def chain_wait(buf, ss, rs, k, part=None):
        @pl.when(z - 1 - k >= 0)
        def _():
            chain_copy(buf, ss, rs, 0, k, part, jnp.maximum(z - 1 - k, 0), (e, other)).wait_recv()

        @pl.when(z + 1 + k <= last)
        def _():
            chain_copy(buf, ss, rs, 1, k, part, jnp.minimum(z + 1 + k, last), (e, other)).wait_recv()

    def chain_drain(buf, ss, rs, parts=(None,)):
        for k in range(planes - 1):
            for part in parts:
                @pl.when(can_up(k))
                def _(k=k, part=part):
                    up(buf, ss, rs, k, part).wait_send()

                @pl.when(can_down(k))
                def _(k=k, part=part):
                    down(buf, ss, rs, k, part).wait_send()

    def plane_copy(st, dst, ss, rs, p, j, q, parts):
        d = (c + j) % COLS
        cols = pl.ds(al(q * (feat // parts), feat // parts), feat // parts)
        return pltpu.make_async_remote_copy(
            src_ref=st.at[p, pl.ds(al(d * cap, cap), cap), cols],
            dst_ref=dst.at[p, pl.ds(al(c * cap, cap), cap), cols],
            send_sem=ss.at[p, j - 1, q], recv_sem=rs.at[p, j - 1, q],
            device_id=(z * COLS + d, r), device_id_type=MESH)

    def plane_send(st, dst, ss, rs, p, q=0, parts=1):
        for j in range(1, COLS):
            plane_copy(st, dst, ss, rs, p, j, q, parts).start()
        cols = pl.ds(al(q * (feat // parts), feat // parts), feat // parts)
        dst[p, pl.ds(al(c * cap, cap), cap), cols] = st[p, pl.ds(al(c * cap, cap), cap), cols]

    def plane_wait(st, dst, ss, rs, p, q=0, parts=1):
        for j in range(1, COLS):
            plane_copy(st, dst, ss, rs, p, j, q, parts).wait_recv()

    def plane_drain(st, dst, ss, rs, parts=1):
        for p in range(planes):
            for j in range(1, COLS):
                for q in range(parts):
                    plane_copy(st, dst, ss, rs, p, j, q, parts).wait_send()

    def selection(p):
        m = meta[p]
        place = (lax.broadcasted_iota(jnp.int32, (slots, tok), 0) + z * slots).astype(F32)
        return jnp.where(place == m[0:1, :], 1.0, 0.0), jnp.where(place == m[1:2, :], 1.0, 0.0), m

    def dispatch_x(p):
        s0, s1, _ = selection(p)
        pick = s0 + s1
        sel_t[p] = pick.T.astype(BF16)
        st_x[p] = jnp.dot(pick.astype(BF16), xg[p], preferred_element_type=F32).astype(BF16)
        plane_send(st_x, rows, px_s, px_r, p)

    def dispatch_g(p, part):
        s0, s1, m = selection(p)
        gate = jnp.sum(s0 * m[2:3, :] + s1 * m[3:4, :], axis=1, keepdims=True)
        at = (p,) + span(part)
        picked = jnp.dot((s0 + s1).astype(BF16), gg[at], preferred_element_type=F32)
        st_g[at] = (picked * gate).astype(BF16)
        plane_send(st_g, scaled, pg_s, pg_r, p, part, GPARTS)

    inner = (z > 0) & (z < last)
    at_end = (z == 0) | (z == last)

    def both(fn, k):
        @pl.when(z - 1 - k >= 0)
        def _():
            fn(jnp.maximum(z - 1 - k, 0))

        @pl.when(z + 1 + k <= last)
        def _():
            fn(jnp.minimum(z + 1 + k, last))

    def work(fn, k):
        if k < planes - 2:
            both(fn, k)
        else:
            below, above = z - 1 - k, z + 1 + k
            fn(jnp.where(below >= 0, below, jnp.where(above <= last, above, z)))

    def w_copy(i):
        s, d = w_at[i]
        return pltpu.make_async_remote_copy(
            src_ref=s, dst_ref=d, send_sem=w_send.at[i], recv_sem=w_recv.at[i],
            device_id=(e, other), device_id_type=MESH)

    def halves(src, dst, i, p):
        lo = pl.ds(al(r * half, half), half)
        hi = pl.ds(al(other * half, half), half)
        return (
            pltpu.make_async_copy(src.at[p, :, lo], dst.at[r, p], loc_sem.at[i, p]),
            pltpu.make_async_remote_copy(
                src_ref=src.at[p, :, hi], dst_ref=dst.at[r, p], send_sem=rep_s.at[i, p], recv_sem=rep_r.at[i, p],
                device_id=(e, other), device_id_type=MESH),
        )

    def rep_copy(ref, i, p):
        return pltpu.make_async_remote_copy(
            src_ref=ref.at[r, p], dst_ref=ref.at[r, p], send_sem=rep_s.at[i, p], recv_sem=rep_r.at[i, p],
            device_id=(e, other), device_id_type=MESH)

    step_h = 256 if hidden_n % 256 == 0 else hidden_n
    step_d = feat // PIECES

    def acts(p):
        plane_wait(st_x, rows, px_s, px_r, p)
        for cp in halves(rows, rows_h, 0, p):
            cp.start()

        @pl.loop(0, hidden_n // step_h)
        def _(i):
            cols = pl.ds(al(i * step_h, step_h), step_h)
            ga[p, :, cols] = jnp.dot(rows[p], wg[:, cols], preferred_element_type=F32)
            ua[p, :, cols] = jnp.dot(rows[p], wu[:, cols], preferred_element_type=F32)

    def grads(p):
        for part in range(GPARTS):
            plane_wait(st_g, scaled, pg_s, pg_r, p, part, GPARTS)
            at = span(part)

            @pl.loop(0, hidden_n // step_h)
            def _(i):
                cols = pl.ds(al(i * step_h, step_h), step_h)
                hg = lax.dot_general(scaled[(p,) + at], wd[cols, at[1]], NT, preferred_element_type=F32)
                if part < GPARTS - 1:
                    hg_part[:, cols] = hg if part == 0 else hg_part[:, cols] + hg
                else:
                    if part > 0:
                        hg = hg + hg_part[:, cols]
                    gate_act, up_act = ga[p, :, cols], ua[p, :, cols]
                    sigma = jax.nn.sigmoid(gate_act)
                    silu = gate_act * sigma
                    hid[r, p, :, cols] = (silu * up_act).astype(BF16)
                    gate_gr[r, p, :, cols] = (hg * up_act * sigma * (1.0 + gate_act * (1.0 - sigma))).astype(BF16)
                    up_gr[r, p, :, cols] = (hg * silu).astype(BF16)

        @pl.loop(0, PIECES)
        def _(i):
            cols = pl.ds(al(i * step_d, step_d), step_d)
            v = lax.dot_general(gate_gr[r, p], wg[cols, :], NT, preferred_element_type=F32)
            v = v + lax.dot_general(up_gr[r, p], wu[cols, :], NT, preferred_element_type=F32)
            sg[p, :, cols] = v.astype(BF16)
            plane_send(sg, ret, pr_s, pr_r, p, i, PIECES)

        for i, ref in enumerate((gate_gr, up_gr, hid)):
            rep_copy(ref, 2 + i, p).start()
        for cp in halves(scaled, scaled_h, 1, p):
            cp.start()

    def piece(q):
        return pl.ds(al(q * step_d, step_d), step_d)

    def ret_copy(way, p, q):
        return pltpu.make_async_remote_copy(
            src_ref=snd.at[p, :, piece(q)], dst_ref=rcv.at[way, p, :, piece(q)],
            send_sem=zr_s.at[p, q], recv_sem=zr_r.at[way, p, q],
            device_id=(jnp.where(way == 0, e + COLS, e - COLS), r), device_id_type=MESH)

    def ret_wait(way, p, q):
        pltpu.make_async_remote_copy(
            src_ref=snd.at[p, :, piece(q)], dst_ref=rcv.at[way, p, :, piece(q)],
            send_sem=zr_s.at[p, q], recv_sem=zr_r.at[way, p, q],
            device_id=(e, other), device_id_type=MESH).wait_recv()

    def own_sum(p, q):
        plane_wait(sg, ret, pr_s, pr_r, p, q, PIECES)
        return jnp.dot(sel_t[p], ret[p, :, piece(q)], preferred_element_type=F32)

    def forward(way, p, first):
        @pl.loop(0, PIECES)
        def _(q):
            own = own_sum(p, q)

            @pl.when(first)
            def _():
                snd[p, :, piece(q)] = own.astype(BF16)

            @pl.when(jnp.logical_not(first))
            def _():
                ret_wait(way, p, q)
                snd[p, :, piece(q)] = (own + rcv[way, p, :, piece(q)].astype(F32)).astype(BF16)

            ret_copy(way, p, q).start()

    def forward_both(k):
        @pl.loop(0, 2)
        def _(side):
            way = jnp.where(z >= planes // 2, 1 - side, side)
            p = jnp.where(way == 1, last - 1 - k, k + 1)

            @pl.when(((way == 1) & (p < z)) | ((way == 0) & (p > z)))
            def _():
                forward(way, p, ((way == 1) & (z == last)) | ((way == 0) & (z == 0)))

    def weight_in(a_half, grad, out):
        step = 256

        @pl.loop(0, half // step)
        def _(i):
            cols = pl.ds(al(i * step, step), step)
            v = 0.0
            for rep in range(2):
                v = v + lax.dot_general(
                    a_half[rep, :, :, cols].reshape(total, step), grad[rep].reshape(total, hidden_n), TN,
                    preferred_element_type=F32)
            out[0, cols, :] = v.astype(BF16)

    def weight_down():
        @pl.loop(0, hidden_n // step_h)
        def _(i):
            cols = pl.ds(al(i * step_h, step_h), step_h)
            v = 0.0
            for rep in range(2):
                v = v + lax.dot_general(
                    hid[rep, :, :, cols].reshape(total, step_h), scaled_h[rep].reshape(total, half), TN,
                    preferred_element_type=F32)
            dwo_v[0, cols, :] = v.astype(BF16)

    def out_copy(i):
        src, dst = ((gwo_v, gwo_ref), (uwo_v, uwo_ref), (dwo_v, dwo_ref))[i]
        return pltpu.make_async_copy(src, dst, out_sem.at[i])

    def weight_grads():
        @pl.loop(0, planes)
        def _(p):
            for i, (src, dst) in enumerate(((rows, rows_h), (scaled, scaled_h))):
                for cp in halves(src, dst, i, p):
                    cp.wait()
            for i, ref in enumerate((gate_gr, up_gr, hid)):
                rep_copy(ref, 2 + i, p).wait()

        weight_in(rows_h, gate_gr, gwo_v)
        out_copy(0).start()
        weight_in(rows_h, up_gr, uwo_v)
        out_copy(1).start()
        weight_down()
        out_copy(2).start()

    chain_start(meta, zm_s, zm_r, 0)
    load_x.wait()
    chain_start(xg, zx_s, zx_r, 0)
    load_g.wait()
    for i in range(3):
        w_copy(i).start()
    dispatch_x(z)
    for part in range(GPARTS):
        chain_start(gg, zg_s, zg_r, 0, part)
        dispatch_g(z, part)
    for cp in load_w:
        cp.wait()
    for i in range(3):
        w_copy(i).wait()

    @pl.when(at_end)
    def _():
        acts(z)

    for k in range(planes - 1):
        chain_wait(meta, zm_s, zm_r, k)
        chain_wait(xg, zx_s, zx_r, k)
        if k < planes - 2:
            chain_start(meta, zm_s, zm_r, k + 1)
            chain_start(xg, zx_s, zx_r, k + 1)
        both(dispatch_x, k)
        if k == 0:
            @pl.when(at_end)
            def _():
                grads(z)
        else:
            both(grads, k - 1)
        if k == planes - 2:
            work(acts, k)

            @pl.when(at_end)
            def _():
                forward_both(k - 1)

        for part in range(GPARTS):
            chain_wait(gg, zg_s, zg_r, k, part)
            if k < planes - 2:
                chain_start(gg, zg_s, zg_r, k + 1, part)
            both(functools.partial(dispatch_g, part=part), k)
        if k < planes - 2:
            both(acts, k)
            if k > 0:
                forward_both(k - 1)
    work(grads, planes - 2)

    @pl.when(inner)
    def _():
        weight_grads()
        forward_both(planes - 3)

    forward_both(planes - 2)

    @pl.when(at_end)
    def _():
        weight_grads()

    @pl.loop(0, PIECES)
    def _(q):
        own_part[...] = own_sum(z, q)

        @pl.when(z < last)
        def _():
            ret_wait(1, z, q)
            own_part[...] += rcv[1, z, :, piece(q)].astype(F32)

        @pl.when(z > 0)
        def _():
            ret_wait(0, z, q)
            own_part[...] += rcv[0, z, :, piece(q)].astype(F32)

        out_ref[:, piece(q)] = own_part[...].astype(BF16)

    for i in range(3):
        out_copy(i).wait()

    chain_drain(meta, zm_s, zm_r)
    chain_drain(xg, zx_s, zx_r)
    chain_drain(gg, zg_s, zg_r, range(GPARTS))
    plane_drain(st_x, rows, px_s, px_r)
    plane_drain(st_g, scaled, pg_s, pg_r, GPARTS)
    plane_drain(sg, ret, pr_s, pr_r, PIECES)
    for p in range(planes):
        @pl.when(p < z)
        def _(p=p):
            for q in range(PIECES):
                ret_copy(1, p, q).wait_send()

        @pl.when(p > z)
        def _(p=p):
            for q in range(PIECES):
                ret_copy(0, p, q).wait_send()


def chained(inputs, out_grad, expert_ids, gates, gate_w, up_w, down_w):
    tok, feat = inputs.shape
    half, hidden_n = gate_w.shape[1], gate_w.shape[2]
    experts = lax.axis_size("expert")
    planes = experts // COLS
    cap = 2 * tok * expert_ids.shape[1] // experts
    slots = COLS * cap
    total = planes * slots
    dma = pltpu.SemaphoreType.DMA
    vmem = pl.BlockSpec(memory_space=pltpu.VMEM)
    hbm = pl.BlockSpec(memory_space=pl.ANY)
    block = (planes, slots, feat)
    act = (planes, slots, hidden_n)
    scratch = [
        pltpu.VMEM((planes, tok, feat), BF16), pltpu.VMEM((planes, tok, feat), BF16),
        pltpu.VMEM((planes, 8, tok), F32),
        pltpu.VMEM(block, BF16), pltpu.VMEM(block, BF16), pltpu.VMEM(block, BF16), pltpu.VMEM(block, BF16),
        pltpu.VMEM((planes, tok, slots), BF16),
        pltpu.VMEM((feat, hidden_n), BF16), pltpu.VMEM((feat, hidden_n), BF16), pltpu.VMEM((hidden_n, feat), BF16),
        pltpu.VMEM(act, F32), pltpu.VMEM(act, F32),
        pltpu.VMEM((2,) + act, BF16), pltpu.VMEM((2,) + act, BF16), pltpu.VMEM((2,) + act, BF16),
        pltpu.VMEM((2, planes, slots, half), BF16), pltpu.VMEM((2, planes, slots, half), BF16),
        pltpu.VMEM(block, BF16), pltpu.VMEM(block, BF16),
        pltpu.VMEM((2, planes, tok, feat), BF16), pltpu.VMEM((planes, tok, feat), BF16),
        pltpu.VMEM((tok, feat // PIECES), F32), pltpu.VMEM((slots, hidden_n), F32),
        pltpu.VMEM(gate_w.shape, BF16), pltpu.VMEM(up_w.shape, BF16), pltpu.VMEM(down_w.shape, BF16),
        dma((5,)), dma((3,)), dma((3,)),
        dma((2, planes - 1)), dma((2, planes - 1)), dma((2, planes - 1)), dma((2, planes - 1)),
        dma((2, planes - 1, GPARTS)), dma((2, planes - 1, GPARTS)),
        dma((planes, COLS - 1, 1)), dma((planes, COLS - 1, 1)),
        dma((planes, COLS - 1, GPARTS)), dma((planes, COLS - 1, GPARTS)),
        dma((planes, COLS - 1, PIECES)), dma((planes, COLS - 1, PIECES)),
        dma((planes, PIECES)), dma((2, planes, PIECES)), dma((5, planes)), dma((5, planes)), dma((2, planes)), dma((3,)),
    ]
    return pl.pallas_call(
        functools.partial(layer_kernel, planes, experts, cap),
        out_shape=(
            jax.ShapeDtypeStruct((tok, feat), BF16),
            jax.ShapeDtypeStruct(gate_w.shape, BF16),
            jax.ShapeDtypeStruct(up_w.shape, BF16),
            jax.ShapeDtypeStruct(down_w.shape, BF16),
        ),
        in_specs=[vmem, vmem] + [hbm] * 5,
        out_specs=(vmem, hbm, hbm, hbm),
        scratch_shapes=scratch,
        compiler_params=pltpu.CompilerParams(
            collective_id=0, has_side_effects=True, vmem_limit_bytes=56 * 1024 * 1024
        ),
        cost_estimate=pl.CostEstimate(
            flops=18 * total * feat * hidden_n, bytes_accessed=8 * feat * hidden_n, transcendentals=total * hidden_n
        ),
    )(expert_ids.T, gates.T, inputs, out_grad, gate_w, up_w, down_w)


def arrange(received, owners, local_exp, capacity):
    feature_n = received.shape[1]
    shaped = received.reshape(owners, local_exp, capacity, feature_n)
    return shaped.transpose(1, 0, 2, 3).reshape(local_exp, owners * capacity, feature_n)


def restore(slot_rows, owners, capacity):
    local_exp = slot_rows.shape[0]
    feature_n = slot_rows.shape[2]
    shaped = slot_rows.reshape(local_exp, owners, capacity, feature_n)
    return shaped.transpose(1, 0, 2, 3).reshape(owners * local_exp * capacity, feature_n)


def local(inputs, out_grad, expert_ids, gates, gate_w, up_w, down_w):
    if lax.axis_size("expert") <= 16:
        return chained(inputs, out_grad, expert_ids, gates, gate_w, up_w, down_w)
    tok_dev = inputs.shape[0]
    feature_n = inputs.shape[1]
    topk_n = expert_ids.shape[1]
    local_exp = gate_w.shape[0]
    owners = lax.axis_size("expert")
    expert_total = local_exp * owners
    capacity = 2 * tok_dev * topk_n // expert_total
    pair_count = tok_dev * topk_n
    slot_total = expert_total * capacity
    flat_ids = expert_ids.reshape(pair_count)
    one_hot = (flat_ids[:, None] == jnp.arange(expert_total, dtype=jnp.int32)[None, :]).astype(
        jnp.int32
    )
    rank_index = (
        jnp.sum(jnp.cumsum(one_hot, axis=0, dtype=jnp.int32) * one_hot, axis=1, dtype=jnp.int32) - 1
    )
    slot_index = flat_ids * capacity + rank_index
    input_pairs = jnp.repeat(inputs, topk_n, axis=0)
    scaled_pairs = (
        gates.reshape(pair_count, 1) * jnp.repeat(out_grad, topk_n, axis=0).astype(jnp.float32)
    ).astype(jnp.bfloat16)
    send_inputs = jnp.zeros((slot_total, feature_n), jnp.bfloat16).at[slot_index].set(input_pairs)
    send_grads = jnp.zeros((slot_total, feature_n), jnp.bfloat16).at[slot_index].set(scaled_pairs)
    full_gate, full_up, full_down = (
        lax.all_gather(gate_w, "rep", axis=1, tiled=True),
        lax.all_gather(up_w, "rep", axis=1, tiled=True),
        lax.all_gather(down_w, "rep", axis=2, tiled=True),
    )
    recv_inputs, recv_grads = (
        lax.all_to_all(send_inputs, "expert", split_axis=0, concat_axis=0, tiled=True),
        lax.all_to_all(send_grads, "expert", split_axis=0, concat_axis=0, tiled=True),
    )
    rows_in = arrange(recv_inputs, owners, local_exp, capacity)
    scaled_rows = arrange(recv_grads, owners, local_exp, capacity)
    gate_act = jnp.einsum("erd,edh->erh", rows_in, full_gate, preferred_element_type=jnp.float32)
    up_act = jnp.einsum("erd,edh->erh", rows_in, full_up, preferred_element_type=jnp.float32)
    gate_act, up_act = (gate_act, up_act)
    sigma = jax.nn.sigmoid(gate_act)
    silu_val = gate_act * sigma
    hidden = (silu_val * up_act).astype(jnp.bfloat16)
    hidden_grad = jnp.einsum(
        "erd,ehd->erh", scaled_rows, full_down, preferred_element_type=jnp.float32
    )
    gate_grad = (hidden_grad * up_act * sigma * (1.0 + gate_act * (1.0 - sigma))).astype(
        jnp.bfloat16
    )
    up_grad = (hidden_grad * silu_val).astype(jnp.bfloat16)
    first = jnp.einsum("erh,edh->erd", gate_grad, full_gate, preferred_element_type=jnp.float32)
    slot_grad = (
        first + jnp.einsum("erh,edh->erd", up_grad, full_up, preferred_element_type=jnp.float32)
    ).astype(jnp.bfloat16)
    returned = lax.all_to_all(
        restore(slot_grad, owners, capacity), "expert", split_axis=0, concat_axis=0, tiled=True
    )
    gate_part = jnp.einsum("erd,erh->edh", rows_in, gate_grad, preferred_element_type=jnp.float32)
    up_part = jnp.einsum("erd,erh->edh", rows_in, up_grad, preferred_element_type=jnp.float32)
    down_part = jnp.einsum("erh,erd->ehd", hidden, scaled_rows, preferred_element_type=jnp.float32)
    gate_sum, up_sum, down_sum = (
        lax.psum_scatter(
            gate_part.astype(jnp.bfloat16), "rep", scatter_dimension=1, tiled=True
        ).astype(jnp.float32),
        lax.psum_scatter(
            up_part.astype(jnp.bfloat16), "rep", scatter_dimension=1, tiled=True
        ).astype(jnp.float32),
        lax.psum_scatter(
            down_part.astype(jnp.bfloat16), "rep", scatter_dimension=2, tiled=True
        ).astype(jnp.float32),
    )
    picked = returned[slot_index]
    input_grad = jnp.sum(
        picked.reshape(tok_dev, topk_n, feature_n).astype(jnp.float32), axis=1
    ).astype(jnp.bfloat16)
    return (
        input_grad,
        gate_sum.astype(jnp.bfloat16),
        up_sum.astype(jnp.bfloat16),
        down_sum.astype(jnp.bfloat16),
    )


def solution(mesh):
    return jax.shard_map(
        local,
        mesh=mesh,
        in_specs=(
            P(("expert", "rep"), None),
            P(("expert", "rep"), None),
            P(("expert", "rep"), None),
            P(("expert", "rep"), None),
            P("expert", "rep", None),
            P("expert", "rep", None),
            P("expert", None, "rep"),
        ),
        out_specs=(
            P(("expert", "rep"), None),
            P("expert", "rep", None),
            P("expert", "rep", None),
            P("expert", None, "rep"),
        ),
        check_vma=False,
    )
```

```python
import functools

import jax
import jax.numpy as jnp
from jax import lax
from jax.experimental import pallas as pl
from jax.experimental.pallas import tpu as pltpu
from jax.sharding import PartitionSpec as P

MESH = pl.DeviceIdType.MESH
COLS = 4
PIECES = 4
GPARTS = 2
F32 = jnp.float32
BF16 = jnp.bfloat16
NT = (((1,), (1,)), ((), ()))
TN = (((0,), (0,)), ((), ()))


def layer_kernel(
    planes, experts, cap,
    ids_ref, gates_ref, x_hbm, g_hbm, gw_hbm, uw_hbm, dw_hbm,
    out_ref, gwo_ref, uwo_ref, dwo_ref,
    xg, gg, meta, st_x, st_g, rows, scaled, sel_t, wg, wu, wd, ga, ua,
    hid, gate_gr, up_gr, rows_h, scaled_h, sg, ret, rcv, snd,
    own_part, hg_part, gwo_v, uwo_v, dwo_v,
    load_sem, w_send, w_recv, zm_s, zm_r, zx_s, zx_r, zg_s, zg_r,
    px_s, px_r, pg_s, pg_r, pr_s, pr_r, zr_s, zr_r, rep_s, rep_r, loc_sem, out_sem,
):
    e, r = lax.axis_index("expert"), lax.axis_index("rep")
    z, c = e // COLS, e % COLS
    other = 1 - r
    tok = x_hbm.shape[0]
    last = planes - 1
    slots = COLS * cap
    half = gw_hbm.shape[1]
    feat = x_hbm.shape[1]
    hidden_n = gw_hbm.shape[2]
    total = planes * slots

    def al(v, m):
        return pl.multiple_of(v, m)

    w_at = [
        (gw_hbm.at[0], wg.at[pl.ds(al(r * half, half), half)]),
        (uw_hbm.at[0], wu.at[pl.ds(al(r * half, half), half)]),
        (dw_hbm.at[0], wd.at[:, pl.ds(al(r * half, half), half)]),
    ]
    load_x = pltpu.make_async_copy(x_hbm, xg.at[z], load_sem.at[0])
    load_g = pltpu.make_async_copy(g_hbm, gg.at[z], load_sem.at[1])
    load_x.start()
    load_g.start()
    load_w = [pltpu.make_async_copy(s, d, load_sem.at[2 + i]) for i, (s, d) in enumerate(w_at)]
    for cp in load_w:
        cp.start()

    barrier = pltpu.get_barrier_semaphore()
    for j in range(1, COLS):
        pl.semaphore_signal(barrier, inc=1, device_id=(z * COLS + (c + j) % COLS, r), device_id_type=MESH)
    pl.semaphore_signal(barrier, inc=1, device_id=(e, other), device_id_type=MESH)

    @pl.when(z < last)
    def _():
        pl.semaphore_signal(barrier, inc=1, device_id=(e + COLS, r), device_id_type=MESH)

    @pl.when(z > 0)
    def _():
        pl.semaphore_signal(barrier, inc=1, device_id=(e - COLS, r), device_id_type=MESH)

    id0, id1 = ids_ref[0:1, :], ids_ref[1:2, :]
    exp_iota = lax.broadcasted_iota(jnp.int32, (experts, tok), 0)
    one0 = jnp.where(exp_iota == id0, 1.0, 0.0)
    one1 = jnp.where(exp_iota == id1, 1.0, 0.0)
    before = jnp.where(
        lax.broadcasted_iota(jnp.int32, (tok, tok), 0) < lax.broadcasted_iota(jnp.int32, (tok, tok), 1), 1.0, 0.0
    ).astype(BF16)
    rank = jnp.dot((one0 + one1).astype(BF16), before, preferred_element_type=F32)
    slot0 = jnp.sum(rank * one0, axis=0, keepdims=True) + id0.astype(F32) * cap
    slot1 = jnp.sum(rank * one1, axis=0, keepdims=True) + id1.astype(F32) * cap
    meta[z] = jnp.concatenate(
        [slot0, slot1, gates_ref[0:1, :], gates_ref[1:2, :], jnp.zeros((4, tok), F32)], axis=0
    )
    neighbours = COLS + jnp.where(z < last, 1, 0) + jnp.where(z > 0, 1, 0)
    pl.semaphore_wait(barrier, neighbours)

    def span(part):
        wide = feat // GPARTS
        return (slice(None), pl.ds(part * wide, wide))

    def at_part(ref, i, part):
        return ref.at[i] if part is None else ref.at[(i,) + span(part)]

    def at_sem(sem, way, k, part):
        return sem.at[way, k] if part is None else sem.at[way, k, part]

    def chain_copy(buf, ss, rs, way, k, part, i, target):
        return pltpu.make_async_remote_copy(
            src_ref=at_part(buf, i, part), dst_ref=at_part(buf, i, part),
            send_sem=at_sem(ss, way, k, part), recv_sem=at_sem(rs, way, k, part),
            device_id=target, device_id_type=MESH)

    def up(buf, ss, rs, k, part):
        return chain_copy(buf, ss, rs, 0, k, part, jnp.maximum(z - k, 0), (e + COLS, r))

    def down(buf, ss, rs, k, part):
        return chain_copy(buf, ss, rs, 1, k, part, jnp.minimum(z + k, last), (e - COLS, r))

    def can_up(k):
        return (z < last) & (z - k >= 0)

    def can_down(k):
        return (z > 0) & (z + k <= last)

    def chain_start(buf, ss, rs, k, part=None):
        @pl.when(can_up(k))
        def _():
            up(buf, ss, rs, k, part).start()

        @pl.when(can_down(k))
        def _():
            down(buf, ss, rs, k, part).start()

    def chain_wait(buf, ss, rs, k, part=None):
        @pl.when(z - 1 - k >= 0)
        def _():
            chain_copy(buf, ss, rs, 0, k, part, jnp.maximum(z - 1 - k, 0), (e, other)).wait_recv()

        @pl.when(z + 1 + k <= last)
        def _():
            chain_copy(buf, ss, rs, 1, k, part, jnp.minimum(z + 1 + k, last), (e, other)).wait_recv()

    def chain_drain(buf, ss, rs, parts=(None,)):
        for k in range(planes - 1):
            for part in parts:
                @pl.when(can_up(k))
                def _(k=k, part=part):
                    up(buf, ss, rs, k, part).wait_send()

                @pl.when(can_down(k))
                def _(k=k, part=part):
                    down(buf, ss, rs, k, part).wait_send()

    def plane_copy(st, dst, ss, rs, p, j, q, parts):
        d = (c + j) % COLS
        cols = pl.ds(al(q * (feat // parts), feat // parts), feat // parts)
        return pltpu.make_async_remote_copy(
            src_ref=st.at[p, pl.ds(al(d * cap, cap), cap), cols],
            dst_ref=dst.at[p, pl.ds(al(c * cap, cap), cap), cols],
            send_sem=ss.at[p, j - 1, q], recv_sem=rs.at[p, j - 1, q],
            device_id=(z * COLS + d, r), device_id_type=MESH)

    def plane_send(st, dst, ss, rs, p, q=0, parts=1):
        for j in range(1, COLS):
            plane_copy(st, dst, ss, rs, p, j, q, parts).start()
        cols = pl.ds(al(q * (feat // parts), feat // parts), feat // parts)
        dst[p, pl.ds(al(c * cap, cap), cap), cols] = st[p, pl.ds(al(c * cap, cap), cap), cols]

    def plane_wait(st, dst, ss, rs, p, q=0, parts=1):
        for j in range(1, COLS):
            plane_copy(st, dst, ss, rs, p, j, q, parts).wait_recv()

    def plane_drain(st, dst, ss, rs, parts=1):
        for p in range(planes):
            for j in range(1, COLS):
                for q in range(parts):
                    plane_copy(st, dst, ss, rs, p, j, q, parts).wait_send()

    def selection(p):
        m = meta[p]
        place = (lax.broadcasted_iota(jnp.int32, (slots, tok), 0) + z * slots).astype(F32)
        return jnp.where(place == m[0:1, :], 1.0, 0.0), jnp.where(place == m[1:2, :], 1.0, 0.0), m

    def dispatch_x(p):
        s0, s1, _ = selection(p)
        pick = s0 + s1
        sel_t[p] = pick.T.astype(BF16)
        st_x[p] = jnp.dot(pick.astype(BF16), xg[p], preferred_element_type=F32).astype(BF16)
        plane_send(st_x, rows, px_s, px_r, p)

    def dispatch_g(p, part):
        s0, s1, m = selection(p)
        gate = jnp.sum(s0 * m[2:3, :] + s1 * m[3:4, :], axis=1, keepdims=True)
        at = (p,) + span(part)
        picked = jnp.dot((s0 + s1).astype(BF16), gg[at], preferred_element_type=F32)
        st_g[at] = (picked * gate).astype(BF16)
        plane_send(st_g, scaled, pg_s, pg_r, p, part, GPARTS)

    inner = (z > 0) & (z < last)
    at_end = (z == 0) | (z == last)

    def both(fn, k):
        @pl.when(z - 1 - k >= 0)
        def _():
            fn(jnp.maximum(z - 1 - k, 0))

        @pl.when(z + 1 + k <= last)
        def _():
            fn(jnp.minimum(z + 1 + k, last))

    def work(fn, k):
        if k < planes - 2:
            both(fn, k)
        else:
            below, above = z - 1 - k, z + 1 + k
            fn(jnp.where(below >= 0, below, jnp.where(above <= last, above, z)))

    def w_copy(i):
        s, d = w_at[i]
        return pltpu.make_async_remote_copy(
            src_ref=s, dst_ref=d, send_sem=w_send.at[i], recv_sem=w_recv.at[i],
            device_id=(e, other), device_id_type=MESH)

    def halves(src, dst, i, p):
        lo = pl.ds(al(r * half, half), half)
        hi = pl.ds(al(other * half, half), half)
        return (
            pltpu.make_async_copy(src.at[p, :, lo], dst.at[r, p], loc_sem.at[i, p]),
            pltpu.make_async_remote_copy(
                src_ref=src.at[p, :, hi], dst_ref=dst.at[r, p], send_sem=rep_s.at[i, p], recv_sem=rep_r.at[i, p],
                device_id=(e, other), device_id_type=MESH),
        )

    def rep_copy(ref, i, p):
        return pltpu.make_async_remote_copy(
            src_ref=ref.at[r, p], dst_ref=ref.at[r, p], send_sem=rep_s.at[i, p], recv_sem=rep_r.at[i, p],
            device_id=(e, other), device_id_type=MESH)

    step_h = 256 if hidden_n % 256 == 0 else hidden_n
    step_d = feat // PIECES

    def acts(p):
        plane_wait(st_x, rows, px_s, px_r, p)
        for cp in halves(rows, rows_h, 0, p):
            cp.start()

        @pl.loop(0, hidden_n // step_h)
        def _(i):
            cols = pl.ds(al(i * step_h, step_h), step_h)
            ga[p, :, cols] = jnp.dot(rows[p], wg[:, cols], preferred_element_type=F32)
            ua[p, :, cols] = jnp.dot(rows[p], wu[:, cols], preferred_element_type=F32)

    def grads(p):
        for part in range(GPARTS):
            plane_wait(st_g, scaled, pg_s, pg_r, p, part, GPARTS)
            at = span(part)

            @pl.loop(0, hidden_n // step_h)
            def _(i):
                cols = pl.ds(al(i * step_h, step_h), step_h)
                hg = lax.dot_general(scaled[(p,) + at], wd[cols, at[1]], NT, preferred_element_type=F32)
                if part < GPARTS - 1:
                    hg_part[:, cols] = hg if part == 0 else hg_part[:, cols] + hg
                else:
                    if part > 0:
                        hg = hg + hg_part[:, cols]
                    gate_act, up_act = ga[p, :, cols], ua[p, :, cols]
                    sigma = jax.nn.sigmoid(gate_act)
                    silu = gate_act * sigma
                    hid[r, p, :, cols] = (silu * up_act).astype(BF16)
                    gate_gr[r, p, :, cols] = (hg * up_act * sigma * (1.0 + gate_act * (1.0 - sigma))).astype(BF16)
                    up_gr[r, p, :, cols] = (hg * silu).astype(BF16)

        @pl.loop(0, PIECES)
        def _(i):
            cols = pl.ds(al(i * step_d, step_d), step_d)
            v = lax.dot_general(gate_gr[r, p], wg[cols, :], NT, preferred_element_type=F32)
            v = v + lax.dot_general(up_gr[r, p], wu[cols, :], NT, preferred_element_type=F32)
            sg[p, :, cols] = v.astype(BF16)
            plane_send(sg, ret, pr_s, pr_r, p, i, PIECES)

        for i, ref in enumerate((gate_gr, up_gr, hid)):
            rep_copy(ref, 2 + i, p).start()
        for cp in halves(scaled, scaled_h, 1, p):
            cp.start()

    def piece(q):
        return pl.ds(al(q * step_d, step_d), step_d)

    def ret_copy(way, p, q):
        return pltpu.make_async_remote_copy(
            src_ref=snd.at[p, :, piece(q)], dst_ref=rcv.at[way, p, :, piece(q)],
            send_sem=zr_s.at[p, q], recv_sem=zr_r.at[way, p, q],
            device_id=(jnp.where(way == 0, e + COLS, e - COLS), r), device_id_type=MESH)

    def ret_wait(way, p, q):
        pltpu.make_async_remote_copy(
            src_ref=snd.at[p, :, piece(q)], dst_ref=rcv.at[way, p, :, piece(q)],
            send_sem=zr_s.at[p, q], recv_sem=zr_r.at[way, p, q],
            device_id=(e, other), device_id_type=MESH).wait_recv()

    def own_sum(p, q):
        plane_wait(sg, ret, pr_s, pr_r, p, q, PIECES)
        return jnp.dot(sel_t[p], ret[p, :, piece(q)], preferred_element_type=F32)

    def forward(way, p, first):
        @pl.loop(0, PIECES)
        def _(q):
            own = own_sum(p, q)

            @pl.when(first)
            def _():
                snd[p, :, piece(q)] = own.astype(BF16)

            @pl.when(jnp.logical_not(first))
            def _():
                ret_wait(way, p, q)
                snd[p, :, piece(q)] = (own + rcv[way, p, :, piece(q)].astype(F32)).astype(BF16)

            ret_copy(way, p, q).start()

    def forward_both(k):
        @pl.loop(0, 2)
        def _(side):
            way = jnp.where(z >= planes // 2, 1 - side, side)
            p = jnp.where(way == 1, last - 1 - k, k + 1)

            @pl.when(((way == 1) & (p < z)) | ((way == 0) & (p > z)))
            def _():
                forward(way, p, ((way == 1) & (z == last)) | ((way == 0) & (z == 0)))

    def weight_in(a_half, grad, out):
        step = 256

        @pl.loop(0, half // step)
        def _(i):
            cols = pl.ds(al(i * step, step), step)
            v = 0.0
            for rep in range(2):
                v = v + lax.dot_general(
                    a_half[rep, :, :, cols].reshape(total, step), grad[rep].reshape(total, hidden_n), TN,
                    preferred_element_type=F32)
            out[0, cols, :] = v.astype(BF16)

    def weight_down():
        @pl.loop(0, hidden_n // step_h)
        def _(i):
            cols = pl.ds(al(i * step_h, step_h), step_h)
            v = 0.0
            for rep in range(2):
                v = v + lax.dot_general(
                    hid[rep, :, :, cols].reshape(total, step_h), scaled_h[rep].reshape(total, half), TN,
                    preferred_element_type=F32)
            dwo_v[0, cols, :] = v.astype(BF16)

    def out_copy(i):
        src, dst = ((gwo_v, gwo_ref), (uwo_v, uwo_ref), (dwo_v, dwo_ref))[i]
        return pltpu.make_async_copy(src, dst, out_sem.at[i])

    def weight_grads():
        @pl.loop(0, planes)
        def _(p):
            for i, (src, dst) in enumerate(((rows, rows_h), (scaled, scaled_h))):
                for cp in halves(src, dst, i, p):
                    cp.wait()
            for i, ref in enumerate((gate_gr, up_gr, hid)):
                rep_copy(ref, 2 + i, p).wait()

        weight_in(rows_h, gate_gr, gwo_v)
        out_copy(0).start()
        weight_in(rows_h, up_gr, uwo_v)
        out_copy(1).start()
        weight_down()
        out_copy(2).start()

    chain_start(meta, zm_s, zm_r, 0)
    load_x.wait()
    chain_start(xg, zx_s, zx_r, 0)
    load_g.wait()
    for i in range(3):
        w_copy(i).start()
    dispatch_x(z)
    for part in range(GPARTS):
        chain_start(gg, zg_s, zg_r, 0, part)
        dispatch_g(z, part)
    for cp in load_w:
        cp.wait()
    for i in range(3):
        w_copy(i).wait()

    @pl.when(at_end)
    def _():
        acts(z)

    for k in range(planes - 1):
        chain_wait(meta, zm_s, zm_r, k)
        chain_wait(xg, zx_s, zx_r, k)
        if k < planes - 2:
            chain_start(meta, zm_s, zm_r, k + 1)
            chain_start(xg, zx_s, zx_r, k + 1)
        both(dispatch_x, k)
        if k == 0:
            @pl.when(at_end)
            def _():
                grads(z)
        else:
            both(grads, k - 1)
        if k == planes - 2:
            work(acts, k)

            @pl.when(at_end)
            def _():
                forward_both(k - 1)

        for part in range(GPARTS):
            chain_wait(gg, zg_s, zg_r, k, part)
            if k < planes - 2:
                chain_start(gg, zg_s, zg_r, k + 1, part)
            both(functools.partial(dispatch_g, part=part), k)
        if k < planes - 2:
            both(acts, k)
            if k > 0:
                forward_both(k - 1)
    work(grads, planes - 2)

    @pl.when(inner)
    def _():
        weight_grads()
        forward_both(planes - 3)

    forward_both(planes - 2)

    @pl.when(at_end)
    def _():
        weight_grads()

    @pl.loop(0, PIECES)
    def _(q):
        own_part[...] = own_sum(z, q)

        @pl.when(z < last)
        def _():
            ret_wait(1, z, q)
            own_part[...] += rcv[1, z, :, piece(q)].astype(F32)

        @pl.when(z > 0)
        def _():
            ret_wait(0, z, q)
            own_part[...] += rcv[0, z, :, piece(q)].astype(F32)

        out_ref[:, piece(q)] = own_part[...].astype(BF16)

    for i in range(3):
        out_copy(i).wait()

    chain_drain(meta, zm_s, zm_r)
    chain_drain(xg, zx_s, zx_r)
    chain_drain(gg, zg_s, zg_r, range(GPARTS))
    plane_drain(st_x, rows, px_s, px_r)
    plane_drain(st_g, scaled, pg_s, pg_r, GPARTS)
    plane_drain(sg, ret, pr_s, pr_r, PIECES)
    for p in range(planes):
        @pl.when(p < z)
        def _(p=p):
            for q in range(PIECES):
                ret_copy(1, p, q).wait_send()

        @pl.when(p > z)
        def _(p=p):
            for q in range(PIECES):
                ret_copy(0, p, q).wait_send()


def chained(inputs, out_grad, expert_ids, gates, gate_w, up_w, down_w):
    tok, feat = inputs.shape
    half, hidden_n = gate_w.shape[1], gate_w.shape[2]
    experts = lax.axis_size("expert")
    planes = experts // COLS
    cap = 2 * tok * expert_ids.shape[1] // experts
    slots = COLS * cap
    total = planes * slots
    dma = pltpu.SemaphoreType.DMA
    vmem = pl.BlockSpec(memory_space=pltpu.VMEM)
    hbm = pl.BlockSpec(memory_space=pl.ANY)
    block = (planes, slots, feat)
    act = (planes, slots, hidden_n)
    scratch = [
        pltpu.VMEM((planes, tok, feat), BF16), pltpu.VMEM((planes, tok, feat), BF16),
        pltpu.VMEM((planes, 8, tok), F32),
        pltpu.VMEM(block, BF16), pltpu.VMEM(block, BF16), pltpu.VMEM(block, BF16), pltpu.VMEM(block, BF16),
        pltpu.VMEM((planes, tok, slots), BF16),
        pltpu.VMEM((feat, hidden_n), BF16), pltpu.VMEM((feat, hidden_n), BF16), pltpu.VMEM((hidden_n, feat), BF16),
        pltpu.VMEM(act, F32), pltpu.VMEM(act, F32),
        pltpu.VMEM((2,) + act, BF16), pltpu.VMEM((2,) + act, BF16), pltpu.VMEM((2,) + act, BF16),
        pltpu.VMEM((2, planes, slots, half), BF16), pltpu.VMEM((2, planes, slots, half), BF16),
        pltpu.VMEM(block, BF16), pltpu.VMEM(block, BF16),
        pltpu.VMEM((2, planes, tok, feat), BF16), pltpu.VMEM((planes, tok, feat), BF16),
        pltpu.VMEM((tok, feat // PIECES), F32), pltpu.VMEM((slots, hidden_n), F32),
        pltpu.VMEM(gate_w.shape, BF16), pltpu.VMEM(up_w.shape, BF16), pltpu.VMEM(down_w.shape, BF16),
        dma((5,)), dma((3,)), dma((3,)),
        dma((2, planes - 1)), dma((2, planes - 1)), dma((2, planes - 1)), dma((2, planes - 1)),
        dma((2, planes - 1, GPARTS)), dma((2, planes - 1, GPARTS)),
        dma((planes, COLS - 1, 1)), dma((planes, COLS - 1, 1)),
        dma((planes, COLS - 1, GPARTS)), dma((planes, COLS - 1, GPARTS)),
        dma((planes, COLS - 1, PIECES)), dma((planes, COLS - 1, PIECES)),
        dma((planes, PIECES)), dma((2, planes, PIECES)), dma((5, planes)), dma((5, planes)), dma((2, planes)), dma((3,)),
    ]
    return pl.pallas_call(
        functools.partial(layer_kernel, planes, experts, cap),
        out_shape=(
            jax.ShapeDtypeStruct((tok, feat), BF16),
            jax.ShapeDtypeStruct(gate_w.shape, BF16),
            jax.ShapeDtypeStruct(up_w.shape, BF16),
            jax.ShapeDtypeStruct(down_w.shape, BF16),
        ),
        in_specs=[vmem, vmem] + [hbm] * 5,
        out_specs=(vmem, hbm, hbm, hbm),
        scratch_shapes=scratch,
        compiler_params=pltpu.CompilerParams(
            collective_id=0, has_side_effects=True, vmem_limit_bytes=50 * 1024 * 1024
        ),
        cost_estimate=pl.CostEstimate(
            flops=18 * total * feat * hidden_n, bytes_accessed=8 * feat * hidden_n, transcendentals=total * hidden_n
        ),
    )(expert_ids.T, gates.T, inputs, out_grad, gate_w, up_w, down_w)


def arrange(received, owners, local_exp, capacity):
    feature_n = received.shape[1]
    shaped = received.reshape(owners, local_exp, capacity, feature_n)
    return shaped.transpose(1, 0, 2, 3).reshape(local_exp, owners * capacity, feature_n)


def restore(slot_rows, owners, capacity):
    local_exp = slot_rows.shape[0]
    feature_n = slot_rows.shape[2]
    shaped = slot_rows.reshape(local_exp, owners, capacity, feature_n)
    return shaped.transpose(1, 0, 2, 3).reshape(owners * local_exp * capacity, feature_n)


def local(inputs, out_grad, expert_ids, gates, gate_w, up_w, down_w):
    if lax.axis_size("expert") <= 16:
        return chained(inputs, out_grad, expert_ids, gates, gate_w, up_w, down_w)
    tok_dev = inputs.shape[0]
    feature_n = inputs.shape[1]
    topk_n = expert_ids.shape[1]
    local_exp = gate_w.shape[0]
    owners = lax.axis_size("expert")
    expert_total = local_exp * owners
    capacity = 2 * tok_dev * topk_n // expert_total
    pair_count = tok_dev * topk_n
    slot_total = expert_total * capacity
    flat_ids = expert_ids.reshape(pair_count)
    one_hot = (flat_ids[:, None] == jnp.arange(expert_total, dtype=jnp.int32)[None, :]).astype(
        jnp.int32
    )
    rank_index = (
        jnp.sum(jnp.cumsum(one_hot, axis=0, dtype=jnp.int32) * one_hot, axis=1, dtype=jnp.int32) - 1
    )
    slot_index = flat_ids * capacity + rank_index
    input_pairs = jnp.repeat(inputs, topk_n, axis=0)
    scaled_pairs = (
        gates.reshape(pair_count, 1) * jnp.repeat(out_grad, topk_n, axis=0).astype(jnp.float32)
    ).astype(jnp.bfloat16)
    send_inputs = jnp.zeros((slot_total, feature_n), jnp.bfloat16).at[slot_index].set(input_pairs)
    send_grads = jnp.zeros((slot_total, feature_n), jnp.bfloat16).at[slot_index].set(scaled_pairs)
    full_gate, full_up, full_down = (
        lax.all_gather(gate_w, "rep", axis=1, tiled=True),
        lax.all_gather(up_w, "rep", axis=1, tiled=True),
        lax.all_gather(down_w, "rep", axis=2, tiled=True),
    )
    recv_inputs, recv_grads = (
        lax.all_to_all(send_inputs, "expert", split_axis=0, concat_axis=0, tiled=True),
        lax.all_to_all(send_grads, "expert", split_axis=0, concat_axis=0, tiled=True),
    )
    rows_in = arrange(recv_inputs, owners, local_exp, capacity)
    scaled_rows = arrange(recv_grads, owners, local_exp, capacity)
    gate_act = jnp.einsum("erd,edh->erh", rows_in, full_gate, preferred_element_type=jnp.float32)
    up_act = jnp.einsum("erd,edh->erh", rows_in, full_up, preferred_element_type=jnp.float32)
    gate_act, up_act = (gate_act, up_act)
    sigma = jax.nn.sigmoid(gate_act)
    silu_val = gate_act * sigma
    hidden = (silu_val * up_act).astype(jnp.bfloat16)
    hidden_grad = jnp.einsum(
        "erd,ehd->erh", scaled_rows, full_down, preferred_element_type=jnp.float32
    )
    gate_grad = (hidden_grad * up_act * sigma * (1.0 + gate_act * (1.0 - sigma))).astype(
        jnp.bfloat16
    )
    up_grad = (hidden_grad * silu_val).astype(jnp.bfloat16)
    first = jnp.einsum("erh,edh->erd", gate_grad, full_gate, preferred_element_type=jnp.float32)
    slot_grad = (
        first + jnp.einsum("erh,edh->erd", up_grad, full_up, preferred_element_type=jnp.float32)
    ).astype(jnp.bfloat16)
    returned = lax.all_to_all(
        restore(slot_grad, owners, capacity), "expert", split_axis=0, concat_axis=0, tiled=True
    )
    gate_part = jnp.einsum("erd,erh->edh", rows_in, gate_grad, preferred_element_type=jnp.float32)
    up_part = jnp.einsum("erd,erh->edh", rows_in, up_grad, preferred_element_type=jnp.float32)
    down_part = jnp.einsum("erh,erd->ehd", hidden, scaled_rows, preferred_element_type=jnp.float32)
    gate_sum, up_sum, down_sum = (
        lax.psum_scatter(
            gate_part.astype(jnp.bfloat16), "rep", scatter_dimension=1, tiled=True
        ).astype(jnp.float32),
        lax.psum_scatter(
            up_part.astype(jnp.bfloat16), "rep", scatter_dimension=1, tiled=True
        ).astype(jnp.float32),
        lax.psum_scatter(
            down_part.astype(jnp.bfloat16), "rep", scatter_dimension=2, tiled=True
        ).astype(jnp.float32),
    )
    picked = returned[slot_index]
    input_grad = jnp.sum(
        picked.reshape(tok_dev, topk_n, feature_n).astype(jnp.float32), axis=1
    ).astype(jnp.bfloat16)
    return (
        input_grad,
        gate_sum.astype(jnp.bfloat16),
        up_sum.astype(jnp.bfloat16),
        down_sum.astype(jnp.bfloat16),
    )


def solution(mesh):
    return jax.shard_map(
        local,
        mesh=mesh,
        in_specs=(
            P(("expert", "rep"), None),
            P(("expert", "rep"), None),
            P(("expert", "rep"), None),
            P(("expert", "rep"), None),
            P("expert", "rep", None),
            P("expert", "rep", None),
            P("expert", None, "rep"),
        ),
        out_specs=(
            P(("expert", "rep"), None),
            P("expert", "rep", None),
            P("expert", "rep", None),
            P("expert", None, "rep"),
        ),
        check_vma=False,
    )
```
